128 devices in a mesh: child: 2 (over y_lo), row: 8 (over x, core), col: 8 (over z, y_hi).
Axes of the slice: x: 4, y: 4 (y_hi: 2, y_lo: 2; y = y_hi * 2 + y_lo), z: 4, core: 2. Of those that a mesh axis runs over, the one named last changes fastest.
Arguments:
- child_blocks: float32 [2, 8192, 8192], P('child', 'row', 'col'), as said below
- child_panels: bfloat16 [2, 8192, 1024], P('child', 'row'), may hold values from -0.1875 to 0.1875
- child_patterns: int32 [2, 32, 32], replicated, may hold values from 0 to 1, as said below
- child_maps: int32 [2, 32], replicated, may hold values from 0 to 47, as said below
- parent_place: int32 [48], replicated, may hold values from 0 to 47, as said below
- parent_front: float32 [12288, 12288], P(('child', 'row'), 'col'), as said below
Outputs:
- factored: float32 [12288, 12288], P(('child', 'row'), 'col')
The draws below stay inside these ranges and needn't reach their ends.
Inputs may be any that keep to these rules, and one draw needn't show every extreme that they name: `parent_place`: a permutation. The entries of one child are distinct; within each aligned block of 4 entries of one child, the values parent_place[child_maps[c, i]] // 6 are distinct. `child_patterns`: symmetric in its two tile dimensions, with ones on the diagonal. `child_blocks`: each child's block is symmetric. `parent_front`: symmetric; the diagonal entries inside stored tiles (parent_place[0], parent_place[0]) and (parent_place[1], parent_place[1]) lie between 200 and 400.
All inputs are finite; a program needn't handle non-finite values.
Results may differ from the reference program's by a relative error of at most 0.0003.
Values may be sent and summed in bfloat16 or wider, within the bound.
No kernel may reach another device: no remote copies, remote signals or barrier semaphores. Data moves between devices by JAX's collectives and lax.ppermute only.
A program may use at most 128 MiB of HBM per device.

```python
import math
import jax
import jax.numpy as jnp
from jax import lax

TILE = 256
DEPTH = 1024
CHILD_TILES_DEV = 4
PARENT_TILES_DEV = 3
PANEL = 512
CHILD_TILES = 32
PARENT_TILES = 48
CHILD_ORDER = 8192
PARENT_ORDER = 12288


def move_front(within, slot_value, group_width, index_pos):
    target_group = slot_value // group_width
    target_pos = slot_value % group_width
    group_row = within[target_group]
    positions = jnp.arange(group_width)
    current = group_row[index_pos]
    new_row = jnp.where(group_row == target_pos, current, jnp.where(positions == index_pos, target_pos, group_row))
    return within.at[target_group].set(new_row)


def layout_tables(key):
    folded = jax.random.fold_in(key, 11)
    place_key, child_key = jax.random.split(folded)
    ordering = jax.random.permutation(place_key, PARENT_TILES).astype(jnp.int32)
    inverse = jnp.argsort(ordering).astype(jnp.int32)
    blocks = CHILD_TILES // CHILD_TILES_DEV
    stride = blocks // CHILD_TILES_DEV
    group_width = 2 * PARENT_TILES_DEV
    mappings = []
    for member in range(2):
        subkeys = jax.random.split(jax.random.fold_in(child_key, member), 4)
        relabel = jax.random.permutation(subkeys[0], blocks)
        block_order = jax.random.permutation(subkeys[1], blocks)
        within = jax.vmap(lambda subkey: jax.random.permutation(subkey, group_width))(jax.random.split(subkeys[2], blocks))
        within = move_front(within, ordering[PARENT_TILES - 1], group_width, 0)
        within = move_front(within, ordering[0], group_width, 1)
        position = jax.vmap(lambda subkey: jax.random.permutation(subkey, CHILD_TILES_DEV))(jax.random.split(subkeys[3], blocks))
        block_ids = jnp.arange(blocks)[:, None]
        ranks_row = jnp.arange(CHILD_TILES_DEV)[None, :]
        groups = relabel[(block_ids + ranks_row * stride) % blocks]
        slot_ids = groups * group_width + within[groups, ranks_row]
        tile_ids = block_order[block_ids] * CHILD_TILES_DEV + position
        mapping = jnp.zeros((CHILD_TILES,), jnp.int32).at[tile_ids.reshape(-1)].set(inverse[slot_ids].reshape(-1))
        mappings.append(mapping)
    return (ordering, jnp.stack(mappings).astype(jnp.int32))


def draw_parent_place(key, part):
    return layout_tables(key)[0]


def draw_child_maps(key, part):
    return layout_tables(key)[1]


def draw_child_patterns(key, part):
    folded = jax.random.fold_in(key, 23)
    first, second = jax.random.split(folded)
    density = jax.random.randint(first, (2, 1, 1), 35, 96)
    rolls = jax.random.randint(second, (2, CHILD_TILES, CHILD_TILES), 0, 100)
    lower = jnp.tril(rolls < density)
    symmetric = jnp.logical_or(lower, jnp.swapaxes(lower, 1, 2))
    identity = jnp.eye(CHILD_TILES, dtype=bool)[None]
    return jnp.where(identity, 1, symmetric.astype(jnp.int32)).astype(jnp.int32)


def draw_child_blocks(key, part):
    folded = jax.random.fold_in(key, 31)
    dims_shape = (2, CHILD_ORDER, CHILD_ORDER)
    raw_values = jax.random.normal(folded, dims_shape, jnp.float32)
    return (raw_values + jnp.swapaxes(raw_values, 1, 2)) / math.sqrt(2.0)


def draw_parent_front(key, part):
    ordering = layout_tables(key)[0]
    folded = jax.random.fold_in(key, 37)
    first, second = jax.random.split(folded)
    dims_shape = (PARENT_ORDER, PARENT_ORDER)
    raw_values = jax.random.normal(first, dims_shape, jnp.float32)
    symmetric = (raw_values + raw_values.T) / math.sqrt(2.0)
    tile_ids = jnp.arange(PARENT_ORDER) // TILE
    pivot = jnp.logical_or(tile_ids == ordering[0], tile_ids == ordering[1])
    strip = pivot[:, None] != pivot[None, :]
    scaled = jnp.where(strip, 4.0 * symmetric, symmetric)
    diagonal = jax.random.uniform(second, (PARENT_ORDER,), jnp.float32, 200.0, 400.0)
    identity = jnp.logical_and(jnp.eye(PARENT_ORDER, dtype=bool), pivot[:, None])
    return jnp.where(identity, diagonal[None, :], scaled)


def shard_levels(own_key, shape, cuts, least, largest):
    def one(dim, parts):
        draws = jax.random.uniform(jax.random.fold_in(jax.random.fold_in(own_key, 6), dim), (parts,), jnp.float32, least / len(cuts), largest / len(cuts))
        return jnp.repeat(jnp.exp(draws), shape[dim] // parts).reshape((-1,) + (1,) * (len(shape) - dim - 1))

    factor_of = one(*cuts[0])
    for cut in cuts[1:]:
        factor_of = factor_of * one(*cut)
    return factor_of


def noise(rng, shape, spread, limit, cuts=(), kind=jnp.bfloat16):
    factor_of = shard_levels(rng, shape, cuts, -0.22, 0.18) if cuts else 1.0
    values = jax.random.normal(rng, shape, jnp.float32) * spread * factor_of
    return jnp.minimum(jnp.maximum(values, -limit), limit).astype(kind)


def setup_inputs(seed: int = 0) -> dict:
    key_list = jax.random.split(jax.random.key(seed), 7)
    return {
        "child_blocks": draw_child_blocks(jax.random.fold_in(key_list[6], 71), 0),
        "child_panels": noise(key_list[1], (2, CHILD_ORDER, DEPTH), DEPTH ** -0.5, 0.1875, ((0, 2), (1, 8))),
        "child_patterns": draw_child_patterns(jax.random.fold_in(key_list[6], 71), 0),
        "child_maps": draw_child_maps(jax.random.fold_in(key_list[6], 71), 0),
        "parent_place": draw_parent_place(jax.random.fold_in(key_list[6], 71), 0),
        "parent_front": draw_parent_front(jax.random.fold_in(key_list[6], 71), 0),
    }


def reference(child_blocks, child_panels, child_patterns, child_maps, parent_place, parent_front):
    frontal = parent_front.reshape(PARENT_TILES, TILE, PARENT_TILES, TILE)
    for member in range(2):
        panel_data = child_panels[member].astype(jnp.float32)
        product = jnp.dot(panel_data.astype(jnp.float32), panel_data.T.astype(jnp.float32), precision=lax.Precision.HIGHEST, preferred_element_type=jnp.float32)
        tile_mask = child_patterns[member].astype(jnp.float32)
        update = (child_blocks[member] - product).reshape(CHILD_TILES, TILE, CHILD_TILES, TILE) * tile_mask[:, None, :, None]
        slot_list = parent_place[child_maps[member]]
        frontal = frontal.at[slot_list[:, None], :, slot_list[None, :], :].add(update.transpose(0, 2, 1, 3))
    panel_slots = parent_place[0:2]
    diagonal_block = frontal[panel_slots[:, None], :, panel_slots[None, :], :]
    diagonal_block = diagonal_block.transpose(0, 2, 1, 3).reshape(PANEL, PANEL)
    factor = jnp.linalg.cholesky(diagonal_block)
    column = frontal[:, :, panel_slots, :].reshape(PARENT_ORDER, PANEL)
    panel_rows = lax.linalg.triangular_solve(factor, column, left_side=False, lower=True, transpose_a=True)
    flattened = frontal.reshape(PARENT_ORDER, PARENT_ORDER)
    result = flattened - jnp.dot(panel_rows.astype(jnp.float32), panel_rows.T.astype(jnp.float32), precision=lax.Precision.HIGHEST, preferred_element_type=jnp.float32)
    result_tiles = result.reshape(PARENT_TILES, TILE, PARENT_TILES, TILE)
    result_tiles = result_tiles.at[:, :, panel_slots, :].set(panel_rows.reshape(PARENT_TILES, TILE, 2, TILE))
    return result_tiles.reshape(PARENT_ORDER, PARENT_ORDER)
```

```python
import functools

import jax
import jax.numpy as jnp
from jax import lax
from jax.experimental import pallas as pl
from jax.experimental.pallas import tpu as pltpu
from jax.sharding import Mesh
from jax.sharding import PartitionSpec as P

TILE = 256
PANEL = 512
CODE = 16
CT = 4
RT = 3
QT = 6
STRIP = 32
SROWS = RT * STRIP + CODE
AXES = ("child", "x", "core", "z", "yh")
SIZES = (2, 4, 2, 4, 2)
MIB = 1 << 20
F32 = jnp.float32
I32 = jnp.int32
I16 = jnp.int16
BF16 = jnp.bfloat16
HIGHEST = lax.Precision.HIGHEST


def flat(c, x, k, z, y):
    return (((c * 4 + x) * 2 + k) * 4 + z) * 2 + y


def everyone():
    return [
        (c, x, k, z, y)
        for c in range(2)
        for x in range(4)
        for k in range(2)
        for z in range(4)
        for y in range(2)
    ]


def shift(v, dc=0, dx=0, dk=0, dz=0, dy=0):
    pairs = [
        (flat(c, x, k, z, y), flat(c ^ dc, (x + dx) % 4, k ^ dk, (z + dz) % 4, y ^ dy))
        for c, x, k, z, y in everyone()
    ]
    return lax.ppermute(v, AXES, pairs)


def encode(u):
    top = jnp.max(jnp.abs(u), axis=0, keepdims=True)
    code = jnp.ceil(jnp.log2(jnp.maximum(top, 1e-30)) * 128.0)
    q = jnp.clip(jnp.floor(u * jnp.exp2(15.0 - code * (1.0 / 128.0)) + 0.5), -32767.0, 32767.0)
    return q.astype(I32).astype(I16), code


def scale_rows(code):
    return jnp.broadcast_to(code, (CODE, code.shape[1])).astype(I32).astype(I16)


def as_float(q):
    return q.astype(I32).astype(F32)


def column_scale(codes):
    return jnp.exp2(as_float(codes)[0:1, :] * (1.0 / 128.0) - 15.0)


def update_kernel(ids, maps, place, pat, blk, pan, par, front, send, diag, tile, sem):
    i = pl.program_id(0)
    ch, r, c, g = ids[0], ids[1], ids[2], ids[3]

    @pl.when(i == 0)
    def _():
        diag[...] = jnp.zeros_like(diag)
        for a in range(2):
            for b in range(2):
                ea, eb = place[a], place[b]

                @pl.when((ea // RT == g) & (eb // QT == c))
                def _():
                    rows = pl.multiple_of((ea % RT) * TILE, TILE)
                    cols = pl.multiple_of((eb % QT) * TILE, TILE)
                    copy = pltpu.make_async_copy(
                        front.at[pl.ds(rows, TILE), pl.ds(cols, TILE)], tile, sem
                    )
                    copy.start()
                    copy.wait()
                    diag[a * TILE : (a + 1) * TILE, b * TILE : (b + 1) * TILE] = tile[...]

    si = place[maps[ch, r * CT + i]]
    for j in range(CT):
        cols = slice(j * TILE, (j + 1) * TILE)
        prod = lax.dot_general(
            pan[...], par[cols, :], (((1,), (1,)), ((), ())), preferred_element_type=F32
        )
        u = (blk[:, cols] - prod) * pat[ch, r * CT + i, c * CT + j].astype(F32)
        q, code = encode(u)
        send[0, 0:TILE, cols] = q
        send[0, TILE:, cols] = scale_rows(code)
        sj = place[maps[ch, c * CT + j]]
        for a in range(2):
            for b in range(2):

                @pl.when((si == place[a]) & (sj == place[b]))
                def _():
                    diag[a * TILE : (a + 1) * TILE, b * TILE : (b + 1) * TILE] += u


def update(ids, maps, place, pat, blk, pan, par, front):
    def slot(i, ids, maps, place, pat):
        return place[maps[ids[0], ids[1] * CT + i]] // QT, 0, 0

    return pl.pallas_call(
        update_kernel,
        grid_spec=pltpu.PrefetchScalarGridSpec(
            num_scalar_prefetch=4,
            grid=(CT,),
            in_specs=[
                pl.BlockSpec((TILE, 1024), lambda i, *s: (i, 0)),
                pl.BlockSpec((TILE, 1024), lambda i, *s: (i, 0)),
                pl.BlockSpec((1024, 1024), lambda i, *s: (0, 0)),
                pl.BlockSpec(memory_space=pl.ANY),
            ],
            out_specs=[
                pl.BlockSpec((1, TILE + CODE, 1024), slot),
                pl.BlockSpec((PANEL, PANEL), lambda i, *s: (0, 0)),
            ],
            scratch_shapes=[pltpu.VMEM((TILE, TILE), F32), pltpu.SemaphoreType.DMA],
        ),
        out_shape=[
            jax.ShapeDtypeStruct((8, TILE + CODE, 1024), I16),
            jax.ShapeDtypeStruct((PANEL, PANEL), F32),
        ],
        compiler_params=pltpu.CompilerParams(vmem_limit_bytes=40 * MIB),
        cost_estimate=pl.CostEstimate(flops=1 << 31, bytes_accessed=14 * MIB, transcendentals=0),
    )(ids, maps, place, pat, blk, pan, par, front)


def find(maps, place, ch, slot):
    def step(i, found):
        return jnp.where(place[maps[ch, i]] == slot, i, found)

    return lax.fori_loop(0, 32, step, jnp.int32(-1))


def route_kernel(ids, maps, place, own, other, send, sems):
    c, g, core = ids[2], ids[3], ids[4]

    def each(act):
        for ch in range(2):
            for p in range(RT):
                i = rows[ch * RT + p]
                src = ch * 4 + i // 8
                for j in range(CT):
                    q = place[maps[ch, c * CT + j]] // QT
                    sem = sems.at[(ch * RT + p) * CT + j]
                    for here, buf in ((True, own), (False, other)):

                        @pl.when((i >= 0) & (((i // 4) % 2 == core) == here))
                        def _():
                            copy = pltpu.make_async_copy(
                                buf.at[src, :, pl.ds(j * TILE, TILE)],
                                send.at[q, ch * RT + p],
                                sem,
                            )
                            act(copy)

    rows = [find(maps, place, ch, g * RT + p) for ch in range(2) for p in range(RT)]
    each(lambda copy: copy.start())
    each(lambda copy: copy.wait())


def route(ids, maps, place, own, other):
    return pl.pallas_call(
        route_kernel,
        grid_spec=pltpu.PrefetchScalarGridSpec(
            num_scalar_prefetch=3,
            grid=(1,),
            in_specs=[pl.BlockSpec(memory_space=pl.ANY)] * 2,
            out_specs=pl.BlockSpec(memory_space=pl.ANY),
            scratch_shapes=[pltpu.SemaphoreType.DMA((24,))],
        ),
        out_shape=jax.ShapeDtypeStruct((8, 2 * RT, TILE + CODE, TILE), I16),
        cost_estimate=pl.CostEstimate(flops=0, bytes_accessed=8 * MIB, transcendentals=0),
    )(ids, maps, place, own, other)


def strips_kernel(ids, maps, place, own, other, front, *rest):
    outs, (acc, tile, wide, sem) = rest[:8], rest[8:]
    c, g, core, z, yh = ids[2], ids[3], ids[4], ids[5], ids[6]
    acc[...] = jnp.zeros_like(acc)
    for a in range(2):
        cols = slice(a * TILE, (a + 1) * TILE)

        @pl.when(place[a] // QT == c)
        def _():
            at = pl.multiple_of((place[a] % QT) * TILE, TILE)
            copy = pltpu.make_async_copy(front.at[:, pl.ds(at, TILE)], wide, sem)
            copy.start()
            copy.wait()
            acc[:, cols] = wide[...]

        for ch in range(2):
            ja = find(maps, place, ch, place[a])

            @pl.when((ja >= 0) & (ja // CT == c))
            def _():
                at = pl.multiple_of((ja % CT) * TILE, TILE)
                for p in range(RT):
                    i = find(maps, place, ch, g * RT + p)
                    for here, buf in ((True, own), (False, other)):

                        @pl.when((i >= 0) & (((i // 4) % 2 == core) == here))
                        def _():
                            copy = pltpu.make_async_copy(
                                buf.at[ch * 4 + i // 8, :, pl.ds(at, TILE)], tile, sem
                            )
                            copy.start()
                            copy.wait()
                            acc[p * TILE : (p + 1) * TILE, cols] += as_float(
                                tile[0:TILE, :]
                            ) * column_scale(tile[TILE:, :])

    for m in range(8):
        s = ((z + m // 2) % 4) * 2 + (yh + m % 2) % 2
        parts = [
            acc[pl.ds(pl.multiple_of(p * TILE + s * STRIP, STRIP), STRIP), :] for p in range(RT)
        ]
        q, code = encode(jnp.concatenate(parts, 0))
        outs[m][0 : RT * STRIP, :] = q
        outs[m][RT * STRIP :, :] = scale_rows(code)


def strips(ids, maps, place, own, other, front):
    return pl.pallas_call(
        strips_kernel,
        grid_spec=pltpu.PrefetchScalarGridSpec(
            num_scalar_prefetch=3,
            grid=(1,),
            in_specs=[pl.BlockSpec(memory_space=pl.ANY)] * 3,
            out_specs=[pl.BlockSpec((SROWS, PANEL), lambda i, *s: (0, 0))] * 8,
            scratch_shapes=[
                pltpu.VMEM((RT * TILE, PANEL), F32),
                pltpu.VMEM((TILE + CODE, TILE), I16),
                pltpu.VMEM((RT * TILE, TILE), F32),
                pltpu.SemaphoreType.DMA,
            ],
        ),
        out_shape=[jax.ShapeDtypeStruct((SROWS, PANEL), I16)] * 8,
        compiler_params=pltpu.CompilerParams(vmem_limit_bytes=24 * MIB),
        cost_estimate=pl.CostEstimate(flops=0, bytes_accessed=4 * MIB, transcendentals=0),
    )(ids, maps, place, own, other, front)


def decode_strip(ref, lead=()):
    q = ref[lead + (slice(0, RT * STRIP), slice(None))]
    codes = ref[lead + (slice(RT * STRIP, SROWS), slice(None))]
    return as_float(q) * column_scale(codes)


def merge_kernel(*refs):
    total = decode_strip(refs[0])
    for ref in refs[1:8]:
        total = total + decode_strip(ref)
    q, code = encode(total)
    refs[8][0 : RT * STRIP, :] = q
    refs[8][RT * STRIP :, :] = scale_rows(code)


def merge(parts):
    return pl.pallas_call(
        merge_kernel,
        out_shape=jax.ShapeDtypeStruct((SROWS, PANEL), I16),
        cost_estimate=pl.CostEstimate(flops=0, bytes_accessed=MIB, transcendentals=0),
    )(*parts)


def nt(a, b):
    return lax.dot_general(
        a, b, (((1,), (1,)), ((), ())), precision=HIGHEST, preferred_element_type=F32
    )


def nn(a, b):
    return lax.dot_general(
        a, b, (((1,), (0,)), ((), ())), precision=HIGHEST, preferred_element_type=F32
    )


NB = 128


def inverse_kernel(a_ref, out, w, f):
    n = PANEL // NB
    out[...] = jnp.zeros_like(out)
    row = lax.broadcasted_iota(I32, (NB, NB), 0)
    col = lax.broadcasted_iota(I32, (NB, NB), 1)
    eye = row == col
    lanes = lax.broadcasted_iota(I32, (1, 2 * NB), 1)
    sub = lax.broadcasted_iota(I32, (NB, 1), 0)

    def blk(i):
        return slice(i * NB, (i + 1) * NB)

    f[...] = a_ref[...]
    for k in range(n):
        w[:, :NB] = f[blk(k), blk(k)]
        w[:, NB:] = jnp.where(eye, 1.0, 0.0).astype(F32)

        def step(j, _):
            line = w[pl.ds(j, 1), :]
            pivot = jnp.sum(jnp.where(lanes == j, line, 0.0), axis=1, keepdims=True)
            column = jnp.sum(jnp.where(col == j, w[:, :NB], 0.0), axis=1, keepdims=True)
            factor = jnp.where(sub > j, column / pivot, 0.0)
            w[...] = w[...] - factor * line
            return 0

        lax.fori_loop(0, NB, step, 0)
        d = jnp.sum(jnp.where(eye, w[:, :NB], 0.0), axis=1, keepdims=True)
        inv = w[:, NB:] * (1.0 / jnp.sqrt(d))
        out[blk(k), blk(k)] = inv
        rest = (k + 1) * NB
        if rest < PANEL:
            below = nt(f[rest:, blk(k)], inv)
            f[rest:, blk(k)] = below
            f[rest:, rest:] = f[rest:, rest:] - nt(below, below)
    for k in range(1, n):
        acc = nn(f[blk(k), : k * NB], out[: k * NB, : k * NB])
        out[blk(k), : k * NB] = -nn(out[blk(k), blk(k)], acc)


def inverse_factor(a):
    return pl.pallas_call(
        inverse_kernel,
        out_shape=jax.ShapeDtypeStruct((PANEL, PANEL), F32),
        scratch_shapes=[pltpu.VMEM((NB, 2 * NB), F32), pltpu.VMEM((PANEL, PANEL), F32)],
        compiler_params=pltpu.CompilerParams(vmem_limit_bytes=24 * MIB),
        cost_estimate=pl.CostEstimate(flops=1 << 34, bytes_accessed=2 * MIB, transcendentals=0),
    )(a)


def split(v):
    hi = v.astype(BF16)
    return hi, (v - hi.astype(F32)).astype(BF16)


def dot3(a, b):
    def one(x, y):
        return lax.dot_general(x, y, (((1,), (1,)), ((), ())), preferred_element_type=F32)

    return one(a[0], b[0]) + (one(a[0], b[1]) + one(a[1], b[0]))


def final_kernel(
    ids, maps, place, diag, inv, gr, gown, goth, recv, front, out,
    gbuf, ph, plo, rows_f, tiles, inv_h, inv_l, tsem,
):
    p = pl.program_id(0)
    c, g, core, k = ids[2], ids[3], ids[4], ids[7]
    e = (place[0], place[1])

    @pl.when(p == 0)
    def _():
        hi, lo = split(inv[...])
        inv_h[...] = hi
        inv_l[...] = lo

        def fill(base, ref, order, first):
            for s in range(8):
                v = decode_strip(ref, (order(s),))
                for t in range(RT):
                    gbuf[base + t * TILE + s * STRIP : base + t * TILE + (s + 1) * STRIP, :] = v[
                        t * STRIP : (t + 1) * STRIP, :
                    ]
            for t in range(RT):
                for a in range(2):

                    @pl.when(first + t == e[a])
                    def _():
                        gbuf[base + t * TILE : base + (t + 1) * TILE, :] = diag[
                            a * TILE : (a + 1) * TILE, :
                        ]

        fill(0, gr, lambda s: s, g * RT)
        for b in range(2):
            base = RT * TILE * (1 + b)

            @pl.when(core == b)
            def _():
                fill(base, gown, lambda s: k ^ s, c * QT + b * RT)

            @pl.when(core != b)
            def _():
                fill(base, goth, lambda s: k ^ s, c * QT + b * RT)

        for t in range(9):
            rows = slice(t * TILE, (t + 1) * TILE)
            v = dot3(split(gbuf[rows, :]), (inv_h[...], inv_l[...]))
            hi, lo = split(v)
            ph[rows, :] = hi
            plo[rows, :] = lo
            if t < RT:
                rows_f[rows, :] = v

    pr = pl.ds(pl.multiple_of(p * TILE, TILE), TILE)
    left = (ph[pr, :], plo[pr, :])
    srow = g * RT + p
    there = [find(maps, place, ch, srow) >= 0 for ch in range(2)]
    js = [[find(maps, place, ch, c * QT + t) for t in range(QT)] for ch in range(2)]

    def each(act):
        for ch in range(2):
            for t in range(QT):

                @pl.when(there[ch] & (js[ch][t] >= 0))
                def _():
                    act(
                        pltpu.make_async_copy(
                            recv.at[js[ch][t] // CT, ch * RT + p],
                            tiles.at[ch * QT + t],
                            tsem.at[ch * QT + t],
                        )
                    )

    each(lambda copy: copy.start())
    for t in range(QT):
        cols = slice(t * TILE, (t + 1) * TILE)
        right = slice((RT + t) * TILE, (RT + t + 1) * TILE)
        out[:, cols] = front[:, cols] - dot3(left, (ph[right, :], plo[right, :]))
    each(lambda copy: copy.wait())
    for t in range(QT):
        cols = slice(t * TILE, (t + 1) * TILE)
        for ch in range(2):

            @pl.when(there[ch] & (js[ch][t] >= 0))
            def _():
                out[:, cols] += as_float(tiles[ch * QT + t, 0:TILE, :]) * column_scale(
                    tiles[ch * QT + t, TILE:, :]
                )

        for a in range(2):

            @pl.when(c * QT + t == e[a])
            def _():
                out[:, cols] = rows_f[pr, a * TILE : (a + 1) * TILE]


def final(ids, maps, place, diag, inv, gr, gown, goth, recv, front):
    def whole(*shape):
        return pl.BlockSpec(shape, lambda i, *s: (0,) * len(shape))

    line = pl.BlockSpec((TILE, QT * TILE), lambda i, *s: (i, 0))
    return pl.pallas_call(
        final_kernel,
        grid_spec=pltpu.PrefetchScalarGridSpec(
            num_scalar_prefetch=3,
            grid=(RT,),
            in_specs=[
                whole(PANEL, PANEL),
                whole(PANEL, PANEL),
                whole(8, SROWS, PANEL),
                whole(8, SROWS, PANEL),
                whole(8, SROWS, PANEL),
                pl.BlockSpec(memory_space=pl.ANY),
                line,
            ],
            out_specs=line,
            scratch_shapes=[
                pltpu.VMEM((9 * TILE, PANEL), F32),
                pltpu.VMEM((9 * TILE, PANEL), BF16),
                pltpu.VMEM((9 * TILE, PANEL), BF16),
                pltpu.VMEM((RT * TILE, PANEL), F32),
                pltpu.VMEM((2 * QT, TILE + CODE, TILE), I16),
                pltpu.VMEM((PANEL, PANEL), BF16),
                pltpu.VMEM((PANEL, PANEL), BF16),
                pltpu.SemaphoreType.DMA((2 * QT,)),
            ],
        ),
        out_shape=jax.ShapeDtypeStruct((RT * TILE, QT * TILE), F32),
        compiler_params=pltpu.CompilerParams(vmem_limit_bytes=52 * MIB),
        cost_estimate=pl.CostEstimate(flops=1 << 33, bytes_accessed=20 * MIB, transcendentals=0),
    )(ids, maps, place, diag, inv, gr, gown, goth, recv, front)


def pick(v, at):
    return lax.dynamic_index_in_dim(v, at, 0, keepdims=False)


def fetch_partner(panel, x, core, z, yh):
    tiles = panel.reshape(4, TILE, 1024)
    piece = pick(tiles, (z - x) % 4)
    halves = []
    for h in range(2):
        came = []
        for dx in (1, 2, 3):
            pairs = [
                (flat(c, xs, y, (xs + 2 * h + b) % 4, y), flat(c, (xs + dx) % 4, b, xs, y))
                for c in range(2)
                for xs in range(4)
                for y in range(2)
                for b in range(2)
            ]
            came.append(lax.ppermute(piece, AXES, pairs))
        halves.append(came)
    two = jnp.stack([pick(tiles, 1 - core), pick(tiles, 3 - core)])
    pairs = [
        (flat(c, x, y, x, y), flat(c, x, 1 - y, x, y))
        for c in range(2)
        for x in range(4)
        for y in range(2)
    ]
    beside = lax.ppermute(two, AXES, pairs)
    owner = (x == z) & (core == yh)
    way = (x - z) % 4
    mine = []
    for h in range(2):
        a, b, d = halves[h]
        got = jnp.where(way == 1, a, jnp.where(way == 2, b, jnp.where(way == 3, d, beside[h])))
        mine.append(jnp.where(owner, pick(tiles, core + 2 * h), got))
    mine = jnp.stack(mine)
    other = shift(mine, dk=1)
    even = jnp.where(core == 0, mine, other)
    odd = jnp.where(core == 0, other, mine)
    return jnp.stack([even[0], odd[0], even[1], odd[1]]).reshape(1024, 1024)


def sum_everywhere(v, x, z):
    v = v.reshape(4, 128, PANEL)
    got = [shift(pick(v, (x + d) % 4), dx=d) for d in (1, 3, 2)]
    v = pick(v, x) + got[0] + got[1] + got[2]
    v = v.reshape(4, 32, PANEL)
    got = [shift(pick(v, (z + d) % 4), dz=d) for d in (1, 3, 2)]
    v = pick(v, z) + got[0] + got[1] + got[2]
    v = v + shift(v, dk=1)
    v = (v + shift(v, dc=1, dy=1)) + (shift(v, dc=1) + shift(v, dy=1))
    full = jnp.zeros((4, 32, PANEL), F32)
    full = lax.dynamic_update_index_in_dim(full, v, z, 0)
    for d in (1, 3, 2):
        full = lax.dynamic_update_index_in_dim(full, shift(v, dz=d), (z - d) % 4, 0)
    v = full.reshape(128, PANEL)
    full = jnp.zeros((4, 128, PANEL), F32)
    full = lax.dynamic_update_index_in_dim(full, v, x, 0)
    for d in (1, 3, 2):
        full = lax.dynamic_update_index_in_dim(full, shift(v, dx=d), (x - d) % 4, 0)
    return full.reshape(PANEL, PANEL)


def cross(v, m):
    pairs = []
    for c, x, k, z, y in everyone():
        kd, qd = (z * 2 + y) ^ m, c * 4 + x
        pairs.append((flat(c, x, k, z, y), flat(kd // 4, kd % 4, k, qd // 2, qd % 2)))
    return lax.ppermute(v, AXES, pairs)


def body(child_blocks, child_panels, child_patterns, child_maps, parent_place, parent_front):
    ch, x, core, z, yh = (lax.axis_index(n).astype(I32) for n in AXES)
    r, c = x * 2 + core, z * 2 + yh
    ids = jnp.stack([ch, r, c, ch * 8 + r, core, z, yh, ch * 4 + x])
    maps, place = child_maps, parent_place
    panel = child_panels[0]
    partner = fetch_partner(panel, x, core, z, yh)
    send, diag = update(
        ids, maps, place, child_patterns, child_blocks[0], panel, partner, parent_front
    )
    own = lax.all_to_all(send, ("child", "x"), split_axis=0, concat_axis=0, tiled=True)
    other = shift(own, dk=1)
    diag = sum_everywhere(diag, x, z)
    inv = inverse_factor(diag)
    send = route(ids, maps, place, own, other)
    recv = lax.all_to_all(send, ("z", "yh"), split_axis=0, concat_axis=0, tiled=True)
    parts = strips(ids, maps, place, own, other, parent_front)
    parts = [parts[0]] + [shift(parts[m], dz=m // 2, dy=m % 2) for m in range(1, 8)]
    strip = merge(parts)
    gr = lax.all_gather(strip, ("z", "yh"))
    gown = jnp.stack([cross(strip, m) for m in range(8)])
    goth = shift(gown, dk=1)
    return final(ids, maps, place, diag, inv, gr, gown, goth, recv, parent_front)


def solution(mesh):
    fine = Mesh(mesh.devices.reshape(SIZES), AXES)
    rows, cols = ("x", "core"), ("z", "yh")
    return jax.shard_map(
        body,
        mesh=fine,
        in_specs=(
            P("child", rows, cols),
            P("child", rows, None),
            P(),
            P(),
            P(),
            P(("child", "x", "core"), cols),
        ),
        out_specs=P(("child", "x", "core"), cols),
        check_vma=False,
    )
```

```python
import functools

import jax
import jax.numpy as jnp
from jax import lax
from jax.experimental import pallas as pl
from jax.experimental.pallas import tpu as pltpu
from jax.sharding import Mesh
from jax.sharding import PartitionSpec as P

TILE = 256
PANEL = 512
CODE = 16
CT = 4
RT = 3
QT = 6
STRIP = 32
SROWS = RT * STRIP + CODE
AXES = ("child", "x", "core", "z", "yh")
SIZES = (2, 4, 2, 4, 2)
MIB = 1 << 20
F32 = jnp.float32
I32 = jnp.int32
I16 = jnp.int16
BF16 = jnp.bfloat16
HIGHEST = lax.Precision.HIGHEST


def flat(c, x, k, z, y):
    return (((c * 4 + x) * 2 + k) * 4 + z) * 2 + y


def everyone():
    return [
        (c, x, k, z, y)
        for c in range(2)
        for x in range(4)
        for k in range(2)
        for z in range(4)
        for y in range(2)
    ]


def shift(v, dc=0, dx=0, dk=0, dz=0, dy=0):
    pairs = [
        (flat(c, x, k, z, y), flat(c ^ dc, (x + dx) % 4, k ^ dk, (z + dz) % 4, y ^ dy))
        for c, x, k, z, y in everyone()
    ]
    return lax.ppermute(v, AXES, pairs)


def encode(u):
    top = jnp.max(jnp.abs(u), axis=0, keepdims=True)
    code = jnp.ceil(jnp.log2(jnp.maximum(top, 1e-30)) * 128.0)
    q = jnp.clip(jnp.floor(u * jnp.exp2(15.0 - code * (1.0 / 128.0)) + 0.5), -32767.0, 32767.0)
    return q.astype(I32).astype(I16), code


def scale_rows(code):
    return jnp.broadcast_to(code, (CODE, code.shape[1])).astype(I32).astype(I16)


def as_float(q):
    return q.astype(I32).astype(F32)


def column_scale(codes):
    return jnp.exp2(as_float(codes)[0:1, :] * (1.0 / 128.0) - 15.0)


def update_kernel(ids, maps, place, pat, blk, pan, par, front, send, diag, tile, sem):
    i = pl.program_id(0)
    ch, r, c, g = ids[0], ids[1], ids[2], ids[3]

    @pl.when(i == 0)
    def _():
        diag[...] = jnp.zeros_like(diag)
        for a in range(2):
            for b in range(2):
                ea, eb = place[a], place[b]

                @pl.when((ea // RT == g) & (eb // QT == c))
                def _():
                    rows = pl.multiple_of((ea % RT) * TILE, TILE)
                    cols = pl.multiple_of((eb % QT) * TILE, TILE)
                    copy = pltpu.make_async_copy(
                        front.at[pl.ds(rows, TILE), pl.ds(cols, TILE)], tile, sem
                    )
                    copy.start()
                    copy.wait()
                    diag[a * TILE : (a + 1) * TILE, b * TILE : (b + 1) * TILE] = tile[...]

    si = place[maps[ch, r * CT + i]]
    for j in range(CT):
        cols = slice(j * TILE, (j + 1) * TILE)
        prod = lax.dot_general(
            pan[...], par[cols, :], (((1,), (1,)), ((), ())), preferred_element_type=F32
        )
        u = (blk[:, cols] - prod) * pat[ch, r * CT + i, c * CT + j].astype(F32)
        q, code = encode(u)
        send[0, 0:TILE, cols] = q
        send[0, TILE:, cols] = scale_rows(code)
        sj = place[maps[ch, c * CT + j]]
        for a in range(2):
            for b in range(2):

                @pl.when((si == place[a]) & (sj == place[b]))
                def _():
                    diag[a * TILE : (a + 1) * TILE, b * TILE : (b + 1) * TILE] += u


def update(ids, maps, place, pat, blk, pan, par, front):
    def slot(i, ids, maps, place, pat):
        return place[maps[ids[0], ids[1] * CT + i]] // QT, 0, 0

    return pl.pallas_call(
        update_kernel,
        grid_spec=pltpu.PrefetchScalarGridSpec(
            num_scalar_prefetch=4,
            grid=(CT,),
            in_specs=[
                pl.BlockSpec((TILE, 1024), lambda i, *s: (i, 0)),
                pl.BlockSpec((TILE, 1024), lambda i, *s: (i, 0)),
                pl.BlockSpec((1024, 1024), lambda i, *s: (0, 0)),
                pl.BlockSpec(memory_space=pl.ANY),
            ],
            out_specs=[
                pl.BlockSpec((1, TILE + CODE, 1024), slot),
                pl.BlockSpec((PANEL, PANEL), lambda i, *s: (0, 0)),
            ],
            scratch_shapes=[pltpu.VMEM((TILE, TILE), F32), pltpu.SemaphoreType.DMA],
        ),
        out_shape=[
            jax.ShapeDtypeStruct((8, TILE + CODE, 1024), I16),
            jax.ShapeDtypeStruct((PANEL, PANEL), F32),
        ],
        compiler_params=pltpu.CompilerParams(vmem_limit_bytes=40 * MIB),
        cost_estimate=pl.CostEstimate(flops=1 << 31, bytes_accessed=14 * MIB, transcendentals=0),
    )(ids, maps, place, pat, blk, pan, par, front)


def find(maps, place, ch, slot):
    def step(i, found):
        return jnp.where(place[maps[ch, i]] == slot, i, found)

    return lax.fori_loop(0, 32, step, jnp.int32(-1))


def route_kernel(ids, maps, place, own, other, send, sems):
    c, g, core = ids[2], ids[3], ids[4]

    def each(act):
        for ch in range(2):
            for p in range(RT):
                i = rows[ch * RT + p]
                src = ch * 4 + i // 8
                for j in range(CT):
                    q = place[maps[ch, c * CT + j]] // QT
                    sem = sems.at[(ch * RT + p) * CT + j]
                    for here, buf in ((True, own), (False, other)):

                        @pl.when((i >= 0) & (((i // 4) % 2 == core) == here))
                        def _():
                            copy = pltpu.make_async_copy(
                                buf.at[src, :, pl.ds(j * TILE, TILE)],
                                send.at[q, ch * RT + p],
                                sem,
                            )
                            act(copy)

    rows = [find(maps, place, ch, g * RT + p) for ch in range(2) for p in range(RT)]
    each(lambda copy: copy.start())
    each(lambda copy: copy.wait())


def route(ids, maps, place, own, other):
    return pl.pallas_call(
        route_kernel,
        grid_spec=pltpu.PrefetchScalarGridSpec(
            num_scalar_prefetch=3,
            grid=(1,),
            in_specs=[pl.BlockSpec(memory_space=pl.ANY)] * 2,
            out_specs=pl.BlockSpec((8, 2 * RT, TILE + CODE, TILE), lambda i, *s: (0, 0, 0, 0)),
            scratch_shapes=[pltpu.SemaphoreType.DMA((24,))],
        ),
        out_shape=jax.ShapeDtypeStruct((8, 2 * RT, TILE + CODE, TILE), I16),
        compiler_params=pltpu.CompilerParams(vmem_limit_bytes=32 * MIB),
        cost_estimate=pl.CostEstimate(flops=0, bytes_accessed=8 * MIB, transcendentals=0),
    )(ids, maps, place, own, other)


def strips_kernel(ids, maps, place, own, other, front, *rest):
    outs, (acc, tile, wide, sem) = rest[:8], rest[8:]
    c, g, core, z, yh = ids[2], ids[3], ids[4], ids[5], ids[6]
    acc[...] = jnp.zeros_like(acc)
    for a in range(2):
        cols = slice(a * TILE, (a + 1) * TILE)

        @pl.when(place[a] // QT == c)
        def _():
            at = pl.multiple_of((place[a] % QT) * TILE, TILE)
            copy = pltpu.make_async_copy(front.at[:, pl.ds(at, TILE)], wide, sem)
            copy.start()
            copy.wait()
            acc[:, cols] = wide[...]

        for ch in range(2):
            ja = find(maps, place, ch, place[a])

            @pl.when((ja >= 0) & (ja // CT == c))
            def _():
                at = pl.multiple_of((ja % CT) * TILE, TILE)
                for p in range(RT):
                    i = find(maps, place, ch, g * RT + p)
                    for here, buf in ((True, own), (False, other)):

                        @pl.when((i >= 0) & (((i // 4) % 2 == core) == here))
                        def _():
                            copy = pltpu.make_async_copy(
                                buf.at[ch * 4 + i // 8, :, pl.ds(at, TILE)], tile, sem
                            )
                            copy.start()
                            copy.wait()
                            acc[p * TILE : (p + 1) * TILE, cols] += as_float(
                                tile[0:TILE, :]
                            ) * column_scale(tile[TILE:, :])

    for m in range(8):
        s = ((z + m // 2) % 4) * 2 + (yh + m % 2) % 2
        parts = [
            acc[pl.ds(pl.multiple_of(p * TILE + s * STRIP, STRIP), STRIP), :] for p in range(RT)
        ]
        q, code = encode(jnp.concatenate(parts, 0))
        outs[m][0 : RT * STRIP, :] = q
        outs[m][RT * STRIP :, :] = scale_rows(code)


def strips(ids, maps, place, own, other, front):
    return pl.pallas_call(
        strips_kernel,
        grid_spec=pltpu.PrefetchScalarGridSpec(
            num_scalar_prefetch=3,
            grid=(1,),
            in_specs=[pl.BlockSpec(memory_space=pl.ANY)] * 3,
            out_specs=[pl.BlockSpec((SROWS, PANEL), lambda i, *s: (0, 0))] * 8,
            scratch_shapes=[
                pltpu.VMEM((RT * TILE, PANEL), F32),
                pltpu.VMEM((TILE + CODE, TILE), I16),
                pltpu.VMEM((RT * TILE, TILE), F32),
                pltpu.SemaphoreType.DMA,
            ],
        ),
        out_shape=[jax.ShapeDtypeStruct((SROWS, PANEL), I16)] * 8,
        compiler_params=pltpu.CompilerParams(vmem_limit_bytes=24 * MIB),
        cost_estimate=pl.CostEstimate(flops=0, bytes_accessed=4 * MIB, transcendentals=0),
    )(ids, maps, place, own, other, front)


def decode_strip(ref, lead=()):
    q = ref[lead + (slice(0, RT * STRIP), slice(None))]
    codes = ref[lead + (slice(RT * STRIP, SROWS), slice(None))]
    return as_float(q) * column_scale(codes)


def merge_kernel(*refs):
    total = decode_strip(refs[0])
    for ref in refs[1:8]:
        total = total + decode_strip(ref)
    q, code = encode(total)
    refs[8][0 : RT * STRIP, :] = q
    refs[8][RT * STRIP :, :] = scale_rows(code)


def merge(parts):
    return pl.pallas_call(
        merge_kernel,
        out_shape=jax.ShapeDtypeStruct((SROWS, PANEL), I16),
        cost_estimate=pl.CostEstimate(flops=0, bytes_accessed=MIB, transcendentals=0),
    )(*parts)


def nt(a, b):
    return lax.dot_general(
        a, b, (((1,), (1,)), ((), ())), precision=HIGHEST, preferred_element_type=F32
    )


def nn(a, b):
    return lax.dot_general(
        a, b, (((1,), (0,)), ((), ())), precision=HIGHEST, preferred_element_type=F32
    )


NB = 128
WAYS = 4


def inverse_kernel(a_ref, out, w, f):
    n = PANEL // NB
    out[...] = jnp.zeros_like(out)
    row = lax.broadcasted_iota(I32, (NB, NB), 0)
    col = lax.broadcasted_iota(I32, (NB, NB), 1)
    eye = row == col
    lanes = lax.broadcasted_iota(I32, (1, 2 * NB), 1)
    sub = lax.broadcasted_iota(I32, (NB, 1), 0)

    def blk(i):
        return slice(i * NB, (i + 1) * NB)

    f[...] = a_ref[...]
    for k in range(n):
        w[:, :NB] = f[blk(k), blk(k)]
        w[:, NB:] = jnp.where(eye, 1.0, 0.0).astype(F32)

        def step(n4, _):
            j = n4 * WAYS
            lines = [w[pl.ds(j + a, 1), :] for a in range(WAYS)]
            square = w[:, :NB]
            columns = [
                jnp.sum(jnp.where(col == j + a, square, 0.0), axis=1, keepdims=True)
                for a in range(WAYS)
            ]
            small = [
                [
                    jnp.sum(jnp.where(lanes == j + b, lines[a], 0.0), axis=1, keepdims=True)
                    if b >= a
                    else None
                    for b in range(WAYS)
                ]
                for a in range(WAYS)
            ]
            factors = []
            for a in range(WAYS):
                inverse = 1.0 / small[a][a]
                for b in range(a + 1, WAYS):
                    times = small[a][b] * inverse
                    for d in range(b, WAYS):
                        small[b][d] = small[b][d] - times * small[a][d]
                    lines[b] = lines[b] - times * lines[a]
                    columns[b] = columns[b] - times * columns[a]
                factors.append(jnp.where(sub >= j + WAYS, columns[a] * inverse, 0.0))
            total = w[...]
            for a in range(WAYS):
                total = total - factors[a] * lines[a]
            w[...] = total
            for a in range(1, WAYS):
                w[pl.ds(j + a, 1), :] = lines[a]
            return 0

        lax.fori_loop(0, NB // WAYS, step, 0)
        d = jnp.sum(jnp.where(eye, w[:, :NB], 0.0), axis=1, keepdims=True)
        inv = w[:, NB:] * (1.0 / jnp.sqrt(d))
        out[blk(k), blk(k)] = inv
        rest = (k + 1) * NB
        if rest < PANEL:
            below = nt(f[rest:, blk(k)], inv)
            f[rest:, blk(k)] = below
            f[rest:, rest:] = f[rest:, rest:] - nt(below, below)
    for k in range(1, n):
        acc = nn(f[blk(k), : k * NB], out[: k * NB, : k * NB])
        out[blk(k), : k * NB] = -nn(out[blk(k), blk(k)], acc)


def inverse_factor(a):
    return pl.pallas_call(
        inverse_kernel,
        out_shape=jax.ShapeDtypeStruct((PANEL, PANEL), F32),
        scratch_shapes=[pltpu.VMEM((NB, 2 * NB), F32), pltpu.VMEM((PANEL, PANEL), F32)],
        compiler_params=pltpu.CompilerParams(vmem_limit_bytes=24 * MIB),
        cost_estimate=pl.CostEstimate(flops=1 << 34, bytes_accessed=2 * MIB, transcendentals=0),
    )(a)


def split(v):
    hi = v.astype(BF16)
    return hi, (v - hi.astype(F32)).astype(BF16)


def dot3(a, b):
    def one(x, y):
        return lax.dot_general(x, y, (((1,), (1,)), ((), ())), preferred_element_type=F32)

    return one(a[0], b[0]) + (one(a[0], b[1]) + one(a[1], b[0]))


def panel_kernel(ids, maps, place, diag, inv, gr, gown, goth, ph, plo, rows_f, gbuf):
    c, g, core, k, z, yh = ids[2], ids[3], ids[4], ids[7], ids[5], ids[6]
    e = (place[0], place[1])
    inv2 = split(inv[...])

    def fill(base, ref, order, first):
        for s in range(8):
            v = decode_strip(ref, (order(s),))
            for t in range(RT):
                gbuf[base + t * TILE + s * STRIP : base + t * TILE + (s + 1) * STRIP, :] = v[
                    t * STRIP : (t + 1) * STRIP, :
                ]
        for t in range(RT):
            for a in range(2):

                @pl.when(first + t == e[a])
                def _():
                    gbuf[base + t * TILE : base + (t + 1) * TILE, :] = diag[
                        a * TILE : (a + 1) * TILE, :
                    ]

    fill(
        0, gr, lambda s: lax.rem((yh + s) % 2, 2) * 4 + lax.rem(z - s // 2 + 4, 4), g * RT
    )
    for b in range(2):
        base = RT * TILE * (1 + b)

        @pl.when(core == b)
        def _():
            fill(base, gown, lambda s: k ^ s, c * QT + b * RT)

        @pl.when(core != b)
        def _():
            fill(base, goth, lambda s: k ^ s, c * QT + b * RT)

    for t in range(9):
        rows = slice(t * TILE, (t + 1) * TILE)
        v = dot3(split(gbuf[rows, :]), inv2)
        hi, lo = split(v)
        ph[rows, :] = hi
        plo[rows, :] = lo
        if t < RT:
            rows_f[rows, :] = v


def panel_rows(ids, maps, place, diag, inv, gr, gown, goth):
    def whole(*shape):
        return pl.BlockSpec(shape, lambda i, *s: (0,) * len(shape))

    return pl.pallas_call(
        panel_kernel,
        grid_spec=pltpu.PrefetchScalarGridSpec(
            num_scalar_prefetch=3,
            grid=(1,),
            in_specs=[whole(PANEL, PANEL)] * 2 + [whole(8, SROWS, PANEL)] * 3,
            out_specs=[whole(9 * TILE, PANEL)] * 2 + [whole(RT * TILE, PANEL)],
            scratch_shapes=[pltpu.VMEM((9 * TILE, PANEL), F32)],
        ),
        out_shape=[jax.ShapeDtypeStruct((9 * TILE, PANEL), BF16)] * 2
        + [jax.ShapeDtypeStruct((RT * TILE, PANEL), F32)],
        compiler_params=pltpu.CompilerParams(vmem_limit_bytes=52 * MIB),
        cost_estimate=pl.CostEstimate(flops=1 << 33, bytes_accessed=16 * MIB, transcendentals=0),
    )(ids, maps, place, diag, inv, gr, gown, goth)


def final_kernel(ids, maps, place, ph, plo, rows_f, recv, front, out, tiles, tsem):
    p = pl.program_id(0)
    c, g = ids[2], ids[3]
    e = (place[0], place[1])
    pr = pl.ds(pl.multiple_of(p * TILE, TILE), TILE)
    srow = g * RT + p
    there = [find(maps, place, ch, srow) >= 0 for ch in range(2)]
    js = [[find(maps, place, ch, c * QT + t) for t in range(QT)] for ch in range(2)]

    def each(act):
        for ch in range(2):
            for t in range(QT):

                @pl.when(there[ch] & (js[ch][t] >= 0))
                def _():
                    act(
                        pltpu.make_async_copy(
                            recv.at[js[ch][t] // CT, ch * RT + p],
                            tiles.at[ch * QT + t],
                            tsem.at[ch * QT + t],
                        )
                    )

    each(lambda copy: copy.start())
    left = (ph[pr, :], plo[pr, :])
    for t in range(QT):
        cols = slice(t * TILE, (t + 1) * TILE)
        right = slice((RT + t) * TILE, (RT + t + 1) * TILE)
        out[:, cols] = front[:, cols] - dot3(left, (ph[right, :], plo[right, :]))
    each(lambda copy: copy.wait())
    for t in range(QT):
        cols = slice(t * TILE, (t + 1) * TILE)
        for ch in range(2):

            @pl.when(there[ch] & (js[ch][t] >= 0))
            def _():
                out[:, cols] += as_float(tiles[ch * QT + t, 0:TILE, :]) * column_scale(
                    tiles[ch * QT + t, TILE:, :]
                )

        for a in range(2):

            @pl.when(c * QT + t == e[a])
            def _():
                out[:, cols] = rows_f[:, a * TILE : (a + 1) * TILE]


def final(ids, maps, place, ph, plo, rows_f, recv, front):
    def whole(*shape):
        return pl.BlockSpec(shape, lambda i, *s: (0,) * len(shape))

    line = pl.BlockSpec((TILE, QT * TILE), lambda i, *s: (i, 0))
    return pl.pallas_call(
        final_kernel,
        grid_spec=pltpu.PrefetchScalarGridSpec(
            num_scalar_prefetch=3,
            grid=(RT,),
            in_specs=[
                whole(9 * TILE, PANEL),
                whole(9 * TILE, PANEL),
                pl.BlockSpec((TILE, PANEL), lambda i, *s: (i, 0)),
                pl.BlockSpec(memory_space=pl.ANY),
                line,
            ],
            out_specs=line,
            scratch_shapes=[
                pltpu.VMEM((2 * QT, TILE + CODE, TILE), I16),
                pltpu.SemaphoreType.DMA((2 * QT,)),
            ],
        ),
        out_shape=jax.ShapeDtypeStruct((RT * TILE, QT * TILE), F32),
        compiler_params=pltpu.CompilerParams(vmem_limit_bytes=52 * MIB),
        cost_estimate=pl.CostEstimate(flops=1 << 32, bytes_accessed=20 * MIB, transcendentals=0),
    )(ids, maps, place, ph, plo, rows_f, recv, front)


def pick(v, at):
    return lax.dynamic_index_in_dim(v, at, 0, keepdims=False)


def fetch_partner(panel, x, core, z, yh):
    tiles = panel.reshape(4, TILE, 1024)
    piece = pick(tiles, (z - x) % 4)
    halves = []
    for h in range(2):
        came = []
        for dx in (1, 2, 3):
            pairs = [
                (flat(c, xs, y, (xs + 2 * h + b) % 4, y), flat(c, (xs + dx) % 4, b, xs, y))
                for c in range(2)
                for xs in range(4)
                for y in range(2)
                for b in range(2)
            ]
            came.append(lax.ppermute(piece, AXES, pairs))
        halves.append(came)
    two = jnp.stack([pick(tiles, 1 - core), pick(tiles, 3 - core)])
    pairs = [
        (flat(c, x, y, x, y), flat(c, x, 1 - y, x, y))
        for c in range(2)
        for x in range(4)
        for y in range(2)
    ]
    beside = lax.ppermute(two, AXES, pairs)
    owner = (x == z) & (core == yh)
    way = (x - z) % 4
    mine = []
    for h in range(2):
        a, b, d = halves[h]
        got = jnp.where(way == 1, a, jnp.where(way == 2, b, jnp.where(way == 3, d, beside[h])))
        mine.append(jnp.where(owner, pick(tiles, core + 2 * h), got))
    mine = jnp.stack(mine)
    other = shift(mine, dk=1)
    even = jnp.where(core == 0, mine, other)
    odd = jnp.where(core == 0, other, mine)
    return jnp.stack([even[0], odd[0], even[1], odd[1]]).reshape(1024, 1024)


def sum_everywhere(v, x, z):
    v = v.reshape(4, 128, PANEL)
    got = [shift(pick(v, (x + d) % 4), dx=d) for d in (1, 3, 2)]
    v = pick(v, x) + got[0] + got[1] + got[2]
    v = v.reshape(4, 32, PANEL)
    got = [shift(pick(v, (z + d) % 4), dz=d) for d in (1, 3, 2)]
    v = pick(v, z) + got[0] + got[1] + got[2]
    v = v + shift(v, dk=1)
    v = (v + shift(v, dc=1, dy=1)) + (shift(v, dc=1) + shift(v, dy=1))
    full = jnp.zeros((4, 32, PANEL), F32)
    full = lax.dynamic_update_index_in_dim(full, v, z, 0)
    for d in (1, 3, 2):
        full = lax.dynamic_update_index_in_dim(full, shift(v, dz=d), (z - d) % 4, 0)
    v = full.reshape(128, PANEL)
    full = jnp.zeros((4, 128, PANEL), F32)
    full = lax.dynamic_update_index_in_dim(full, v, x, 0)
    for d in (1, 3, 2):
        full = lax.dynamic_update_index_in_dim(full, shift(v, dx=d), (x - d) % 4, 0)
    return full.reshape(PANEL, PANEL)


def cross(v, m):
    pairs = []
    for c, x, k, z, y in everyone():
        kd, qd = (z * 2 + y) ^ m, c * 4 + x
        pairs.append((flat(c, x, k, z, y), flat(kd // 4, kd % 4, k, qd // 2, qd % 2)))
    return lax.ppermute(v, AXES, pairs)


def body(child_blocks, child_panels, child_patterns, child_maps, parent_place, parent_front):
    ch, x, core, z, yh = (lax.axis_index(n).astype(I32) for n in AXES)
    r, c = x * 2 + core, z * 2 + yh
    ids = jnp.stack([ch, r, c, ch * 8 + r, core, z, yh, ch * 4 + x])
    maps, place = child_maps, parent_place
    panel = child_panels[0]
    partner = fetch_partner(panel, x, core, z, yh)
    send, diag = update(
        ids, maps, place, child_patterns, child_blocks[0], panel, partner, parent_front
    )
    own = lax.all_to_all(send, ("child", "x"), split_axis=0, concat_axis=0, tiled=True)
    diag = sum_everywhere(diag, x, z)
    own, diag = lax.optimization_barrier((own, diag))
    other = shift(own, dk=1)
    send = route(ids, maps, place, own, other)
    recv = lax.all_to_all(send, ("z", "yh"), split_axis=0, concat_axis=0, tiled=True)
    parts = strips(ids, maps, place, own, other, parent_front)
    parts = [parts[0]] + [shift(parts[m], dz=m // 2, dy=m % 2) for m in range(1, 8)]
    inv = inverse_factor(diag)
    strip = merge(parts)
    crossed = jnp.stack([cross(strip, m) for m in range(8)])
    line = jnp.stack([strip] + [shift(strip, dz=d) for d in range(1, 4)])
    gr = jnp.concatenate([line, shift(line, dy=1)])
    ph, plo, rows_f = panel_rows(ids, maps, place, diag, inv, gr, crossed, shift(crossed, dk=1))
    return final(ids, maps, place, ph, plo, rows_f, recv, parent_front)


def solution(mesh):
    fine = Mesh(mesh.devices.reshape(SIZES), AXES)
    rows, cols = ("x", "core"), ("z", "yh")
    return jax.shard_map(
        body,
        mesh=fine,
        in_specs=(
            P("child", rows, cols),
            P("child", rows, None),
            P(),
            P(),
            P(),
            P(("child", "x", "core"), cols),
        ),
        out_specs=P(("child", "x", "core"), cols),
        check_vma=False,
    )
```

```python
import jax
import jax.numpy as jnp
from jax import lax
from jax.experimental import pallas as pl
from jax.experimental.pallas import tpu as pltpu
from jax.sharding import Mesh
from jax.sharding import PartitionSpec as P

TILE = 256
PANEL = 512
CODE = 16
CT = 4
RT = 3
QT = 6
STRIP = 32
SROWS = RT * STRIP + CODE
AXES = ("child", "x", "core", "z", "yh")
SIZES = (2, 4, 2, 4, 2)
MIB = 1 << 20
F32 = jnp.float32
I32 = jnp.int32
I16 = jnp.int16
BF16 = jnp.bfloat16
HIGHEST = lax.Precision.HIGHEST


def flat(c, x, k, z, y):
    return (((c * 4 + x) * 2 + k) * 4 + z) * 2 + y


def everyone():
    return [
        (c, x, k, z, y)
        for c in range(2)
        for x in range(4)
        for k in range(2)
        for z in range(4)
        for y in range(2)
    ]


def shift(v, dc=0, dx=0, dk=0, dz=0, dy=0):
    pairs = [
        (flat(c, x, k, z, y), flat(c ^ dc, (x + dx) % 4, k ^ dk, (z + dz) % 4, y ^ dy))
        for c, x, k, z, y in everyone()
    ]
    return lax.ppermute(v, AXES, pairs)


def encode(u):
    top = jnp.max(jnp.abs(u), axis=0, keepdims=True)
    code = jnp.ceil(jnp.log2(jnp.maximum(top, 1e-30)) * 128.0)
    q = jnp.clip(jnp.floor(u * jnp.exp2(15.0 - code * (1.0 / 128.0)) + 0.5), -32767.0, 32767.0)
    return q.astype(I32).astype(I16), code


def scale_rows(code):
    return jnp.broadcast_to(code, (CODE, code.shape[1])).astype(I32).astype(I16)


def as_float(q):
    return q.astype(I32).astype(F32)


def column_scale(codes):
    return jnp.exp2(as_float(codes)[0:1, :] * (1.0 / 128.0) - 15.0)


def update_kernel(ids, slots, pat, blk, pan, par, front, send, diag, gcol, tile, sem):
    i = pl.program_id(0)
    ch, r, c, g = ids[0], ids[1], ids[2], ids[3]
    e = (ids[8], ids[9])

    @pl.when(i == 0)
    def _():
        diag[...] = jnp.zeros_like(diag)
        for a in range(2):
            for b in range(2):

                @pl.when((e[a] // RT == g) & (e[b] // QT == c))
                def _():
                    rows = pl.multiple_of((e[a] % RT) * TILE, TILE)
                    cols = pl.multiple_of((e[b] % QT) * TILE, TILE)
                    copy = pltpu.make_async_copy(
                        front.at[pl.ds(rows, TILE), pl.ds(cols, TILE)], tile, sem
                    )
                    copy.start()
                    copy.wait()
                    diag[a * TILE : (a + 1) * TILE, b * TILE : (b + 1) * TILE] = tile[...]

    si = slots[ch, r * CT + i]
    for j in range(CT):
        cols = slice(j * TILE, (j + 1) * TILE)
        prod = lax.dot_general(
            pan[...], par[cols, :], (((1,), (1,)), ((), ())), preferred_element_type=F32
        )
        u = (blk[:, cols] - prod) * pat[ch, r * CT + i, c * CT + j].astype(F32)
        q, code = encode(u)
        send[0, 0:TILE, cols] = q
        send[0, TILE:, cols] = scale_rows(code)
        sj = slots[ch, c * CT + j]
        for b in range(2):
            at = slice(b * TILE, (b + 1) * TILE)

            @pl.when(sj == e[b])
            def _():
                gcol[:, at] = u
                for a in range(2):

                    @pl.when(si == e[a])
                    def _():
                        diag[a * TILE : (a + 1) * TILE, at] += u


def update(ids, slots, pat, blk, pan, par, front):
    def slot(i, ids, slots, pat):
        return slots[ids[0], ids[1] * CT + i] // QT, 0, 0

    return pl.pallas_call(
        update_kernel,
        grid_spec=pltpu.PrefetchScalarGridSpec(
            num_scalar_prefetch=3,
            grid=(CT,),
            in_specs=[
                pl.BlockSpec((TILE, 1024), lambda i, *s: (i, 0)),
                pl.BlockSpec((TILE, 1024), lambda i, *s: (i, 0)),
                pl.BlockSpec((1024, 1024), lambda i, *s: (0, 0)),
                pl.BlockSpec(memory_space=pl.ANY),
            ],
            out_specs=[
                pl.BlockSpec((1, TILE + CODE, 1024), slot),
                pl.BlockSpec((PANEL, PANEL), lambda i, *s: (0, 0)),
                pl.BlockSpec((TILE, PANEL), lambda i, *s: (i, 0)),
            ],
            scratch_shapes=[pltpu.VMEM((TILE, TILE), F32), pltpu.SemaphoreType.DMA],
        ),
        out_shape=[
            jax.ShapeDtypeStruct((8, TILE + CODE, 1024), I16),
            jax.ShapeDtypeStruct((PANEL, PANEL), F32),
            jax.ShapeDtypeStruct((CT * TILE, PANEL), F32),
        ],
        compiler_params=pltpu.CompilerParams(vmem_limit_bytes=40 * MIB),
        cost_estimate=pl.CostEstimate(flops=1 << 31, bytes_accessed=14 * MIB, transcendentals=0),
    )(ids, slots, pat, blk, pan, par, front)


def strips_kernel(ids, gcol, front, *rest):
    outs, (wide, sem) = rest[:4], rest[4:]
    c, z = ids[2], ids[5]
    for a in range(2):
        e = ids[8 + a]

        @pl.when(e // QT == c)
        def _():
            at = pl.multiple_of((e % QT) * TILE, TILE)
            copy = pltpu.make_async_copy(
                front.at[:, pl.ds(at, TILE)], wide.at[:, pl.ds(a * TILE, TILE)], sem
            )
            copy.start()
            copy.wait()

    for d in range(4):
        for f in range(2):
            s = ((z + d) % 4) * 2 + f
            at = 0
            for ref, n in ((gcol, CT), (wide, RT)):
                parts = [
                    ref[pl.ds(pl.multiple_of(p * TILE + s * STRIP, STRIP), STRIP), :]
                    for p in range(n)
                ]
                q, code = encode(jnp.concatenate(parts, 0))
                outs[d][f, at : at + n * STRIP, :] = q
                outs[d][f, at + n * STRIP : at + n * STRIP + CODE, :] = scale_rows(code)
                at += n * STRIP + CODE


def strips(ids, gcol, front):
    return pl.pallas_call(
        strips_kernel,
        grid_spec=pltpu.PrefetchScalarGridSpec(
            num_scalar_prefetch=1,
            grid=(1,),
            in_specs=[
                pl.BlockSpec((CT * TILE, PANEL), lambda i, *s: (0, 0)),
                pl.BlockSpec(memory_space=pl.ANY),
            ],
            out_specs=[pl.BlockSpec((2, TILE, PANEL), lambda i, *s: (0, 0, 0))] * 4,
            scratch_shapes=[pltpu.VMEM((RT * TILE, PANEL), F32), pltpu.SemaphoreType.DMA],
        ),
        out_shape=[jax.ShapeDtypeStruct((2, TILE, PANEL), I16)] * 4,
        compiler_params=pltpu.CompilerParams(vmem_limit_bytes=24 * MIB),
        cost_estimate=pl.CostEstimate(flops=0, bytes_accessed=6 * MIB, transcendentals=0),
    )(ids, gcol, front)


CHILD_CODE = CT * STRIP
FRONT = CHILD_CODE + CODE
FRONT_CODE = FRONT + RT * STRIP


def compose_kernel(ids, where, own, other, out, acc, kept):
    q = pl.program_id(0)
    ch, core, k, x = ids[0], ids[4], ids[7], ids[10]
    half = lax.broadcasted_iota(I32, (STRIP, PANEL), 1) < TILE

    def group(q):
        first = q * QT + core * RT
        d, f = lax.rem(x - q % 4 + 4, 4), lax.rem(ch + q // 4, 2)
        acc[...] = as_float(own[d, f, FRONT:FRONT_CODE, :]) * column_scale(
            own[d, f, FRONT_CODE:, :]
        )
        for m in range(2):
            known = [(where[m, ids[8 + a]] >= 0).astype(I32) for a in range(2)]
            mask = jnp.where(half, known[0], known[1]) > 0
            for p in range(RT):
                i = where[m, first + p]
                for here, ref in ((True, own), (False, other)):

                    @pl.when((i >= 0) & (((i // CT) % 2 == core) == here))
                    def _():
                        dm, fm = lax.rem(x - i // 8 + 4, 4), lax.rem(ch + m, 2)
                        row = pl.multiple_of((i % CT) * STRIP, STRIP)
                        v = as_float(ref[dm, fm, pl.ds(row, STRIP), :]) * column_scale(
                            ref[dm, fm, CHILD_CODE:FRONT, :]
                        )
                        acc[p * STRIP : (p + 1) * STRIP, :] += jnp.where(mask, v, 0.0)

        return encode(acc[...])

    @pl.when(q == 0)
    def _():
        v, code = group(k)
        kept[0 : RT * STRIP, :] = v
        kept[RT * STRIP :, :] = scale_rows(code)

    v, code = group(q)
    out[0, 0] = kept[...]
    out[0, 1, 0 : RT * STRIP, :] = v
    out[0, 1, RT * STRIP :, :] = scale_rows(code)


def compose(ids, where, own, other):
    whole = pl.BlockSpec((4, 2, TILE, PANEL), lambda i, *s: (0, 0, 0, 0))
    return pl.pallas_call(
        compose_kernel,
        grid_spec=pltpu.PrefetchScalarGridSpec(
            num_scalar_prefetch=2,
            grid=(8,),
            in_specs=[whole] * 2,
            out_specs=pl.BlockSpec((1, 2, SROWS, PANEL), lambda i, *s: (i, 0, 0, 0)),
            scratch_shapes=[
                pltpu.VMEM((RT * STRIP, PANEL), F32),
                pltpu.VMEM((SROWS, PANEL), I16),
            ],
        ),
        out_shape=jax.ShapeDtypeStruct((8, 2, SROWS, PANEL), I16),
        compiler_params=pltpu.CompilerParams(vmem_limit_bytes=24 * MIB),
        cost_estimate=pl.CostEstimate(flops=0, bytes_accessed=6 * MIB, transcendentals=0),
    )(ids, where, own, other)


def route_kernel(ids, slots, where, own, other, send, sems):
    c, g, core = ids[2], ids[3], ids[4]

    def each(act):
        for ch in range(2):
            for p in range(RT):
                i = rows[ch * RT + p]
                src = ch * 4 + i // 8
                for j in range(CT):
                    q = slots[ch, c * CT + j] // QT
                    sem = sems.at[(ch * RT + p) * CT + j]
                    for here, buf in ((True, own), (False, other)):

                        @pl.when((i >= 0) & (((i // 4) % 2 == core) == here))
                        def _():
                            copy = pltpu.make_async_copy(
                                buf.at[src, :, pl.ds(j * TILE, TILE)],
                                send.at[q, ch * RT + p],
                                sem,
                            )
                            act(copy)

    rows = [where[ch, g * RT + p] for ch in range(2) for p in range(RT)]
    each(lambda copy: copy.start())
    each(lambda copy: copy.wait())


def route(ids, slots, where, own, other):
    return pl.pallas_call(
        route_kernel,
        grid_spec=pltpu.PrefetchScalarGridSpec(
            num_scalar_prefetch=3,
            grid=(1,),
            in_specs=[pl.BlockSpec(memory_space=pl.ANY)] * 2,
            out_specs=pl.BlockSpec((8, 2 * RT, TILE + CODE, TILE), lambda i, *s: (0, 0, 0, 0)),
            scratch_shapes=[pltpu.SemaphoreType.DMA((24,))],
        ),
        out_shape=jax.ShapeDtypeStruct((8, 2 * RT, TILE + CODE, TILE), I16),
        compiler_params=pltpu.CompilerParams(vmem_limit_bytes=32 * MIB),
        cost_estimate=pl.CostEstimate(flops=0, bytes_accessed=8 * MIB, transcendentals=0),
    )(ids, slots, where, own, other)


def decode_strip(ref, lead=()):
    q = ref[lead + (slice(0, RT * STRIP), slice(None))]
    codes = ref[lead + (slice(RT * STRIP, SROWS), slice(None))]
    return as_float(q) * column_scale(codes)


def nt(a, b):
    return lax.dot_general(
        a, b, (((1,), (1,)), ((), ())), precision=HIGHEST, preferred_element_type=F32
    )


def nn(a, b):
    return lax.dot_general(
        a, b, (((1,), (0,)), ((), ())), precision=HIGHEST, preferred_element_type=F32
    )


NB = 128
WAYS = 4


def inverse_kernel(a_ref, out, w, f):
    n = PANEL // NB
    out[...] = jnp.zeros_like(out)
    row = lax.broadcasted_iota(I32, (NB, NB), 0)
    col = lax.broadcasted_iota(I32, (NB, NB), 1)
    eye = row == col
    lanes = lax.broadcasted_iota(I32, (1, 2 * NB), 1)
    sub = lax.broadcasted_iota(I32, (NB, 1), 0)

    def blk(i):
        return slice(i * NB, (i + 1) * NB)

    f[...] = a_ref[...]
    for k in range(n):
        w[:, :NB] = f[blk(k), blk(k)]
        w[:, NB:] = jnp.where(eye, 1.0, 0.0).astype(F32)

        def step(n4, _):
            j = n4 * WAYS
            lines = [w[pl.ds(j + a, 1), :] for a in range(WAYS)]
            square = w[:, :NB]
            columns = [
                jnp.sum(jnp.where(col == j + a, square, 0.0), axis=1, keepdims=True)
                for a in range(WAYS)
            ]
            small = [
                [
                    jnp.sum(jnp.where(lanes == j + b, lines[a], 0.0), axis=1, keepdims=True)
                    if b >= a
                    else None
                    for b in range(WAYS)
                ]
                for a in range(WAYS)
            ]
            factors = []
            for a in range(WAYS):
                inverse = 1.0 / small[a][a]
                for b in range(a + 1, WAYS):
                    times = small[a][b] * inverse
                    for d in range(b, WAYS):
                        small[b][d] = small[b][d] - times * small[a][d]
                    lines[b] = lines[b] - times * lines[a]
                    columns[b] = columns[b] - times * columns[a]
                factors.append(jnp.where(sub >= j + WAYS, columns[a] * inverse, 0.0))
            total = w[...]
            for a in range(WAYS):
                total = total - factors[a] * lines[a]
            w[...] = total
            for a in range(1, WAYS):
                w[pl.ds(j + a, 1), :] = lines[a]
            return 0

        lax.fori_loop(0, NB // WAYS, step, 0)
        d = jnp.sum(jnp.where(eye, w[:, :NB], 0.0), axis=1, keepdims=True)
        inv = w[:, NB:] * (1.0 / jnp.sqrt(d))
        out[blk(k), blk(k)] = inv
        rest = (k + 1) * NB
        if rest < PANEL:
            below = nt(f[rest:, blk(k)], inv)
            f[rest:, blk(k)] = below
            f[rest:, rest:] = f[rest:, rest:] - nt(below, below)
    for k in range(1, n):
        acc = nn(f[blk(k), : k * NB], out[: k * NB, : k * NB])
        out[blk(k), : k * NB] = -nn(out[blk(k), blk(k)], acc)


def inverse_factor(a):
    return pl.pallas_call(
        inverse_kernel,
        out_shape=jax.ShapeDtypeStruct((PANEL, PANEL), F32),
        scratch_shapes=[pltpu.VMEM((NB, 2 * NB), F32), pltpu.VMEM((PANEL, PANEL), F32)],
        compiler_params=pltpu.CompilerParams(vmem_limit_bytes=24 * MIB),
        cost_estimate=pl.CostEstimate(flops=1 << 34, bytes_accessed=2 * MIB, transcendentals=0),
    )(a)


def split(v):
    hi = v.astype(BF16)
    return hi, (v - hi.astype(F32)).astype(BF16)


def dot3(a, b):
    def one(x, y):
        return lax.dot_general(x, y, (((1,), (1,)), ((), ())), preferred_element_type=F32)

    return one(a[0], b[0]) + (one(a[0], b[1]) + one(a[1], b[0]))


def panel_kernel(ids, diag, inv, gx, goth, ph, plo, rows_f, gbuf):
    c, g, core = ids[2], ids[3], ids[4]
    inv2 = split(inv[...])

    def fill(base, ref, lead, first):
        for s in range(8):
            v = decode_strip(ref, lead(s))
            for t in range(RT):
                gbuf[base + t * TILE + s * STRIP : base + t * TILE + (s + 1) * STRIP, :] = v[
                    t * STRIP : (t + 1) * STRIP, :
                ]
        for t in range(RT):
            for a in range(2):

                @pl.when(first + t == ids[8 + a])
                def _():
                    gbuf[base + t * TILE : base + (t + 1) * TILE, :] = diag[
                        a * TILE : (a + 1) * TILE, :
                    ]

    fill(0, gx, lambda s: (s, 0), g * RT)
    for b in range(2):
        base = RT * TILE * (1 + b)

        @pl.when(core == b)
        def _():
            fill(base, gx, lambda s: (s, 1), c * QT + b * RT)

        @pl.when(core != b)
        def _():
            fill(base, goth, lambda s: (s,), c * QT + b * RT)

    for t in range(3):
        rows = slice(t * RT * TILE, (t + 1) * RT * TILE)
        v = dot3(split(gbuf[rows, :]), inv2)
        hi, lo = split(v)
        ph[rows, :] = hi
        plo[rows, :] = lo
        if t == 0:
            rows_f[...] = v


def panel_rows(ids, diag, inv, gx, goth):
    def whole(*shape):
        return pl.BlockSpec(shape, lambda i, *s: (0,) * len(shape))

    return pl.pallas_call(
        panel_kernel,
        grid_spec=pltpu.PrefetchScalarGridSpec(
            num_scalar_prefetch=1,
            grid=(1,),
            in_specs=[whole(PANEL, PANEL)] * 2
            + [whole(8, 2, SROWS, PANEL), whole(8, SROWS, PANEL)],
            out_specs=[whole(9 * TILE, PANEL)] * 2 + [whole(RT * TILE, PANEL)],
            scratch_shapes=[pltpu.VMEM((9 * TILE, PANEL), F32)],
        ),
        out_shape=[jax.ShapeDtypeStruct((9 * TILE, PANEL), BF16)] * 2
        + [jax.ShapeDtypeStruct((RT * TILE, PANEL), F32)],
        compiler_params=pltpu.CompilerParams(vmem_limit_bytes=52 * MIB),
        cost_estimate=pl.CostEstimate(flops=1 << 33, bytes_accessed=16 * MIB, transcendentals=0),
    )(ids, diag, inv, gx, goth)


def final_kernel(ids, where, lh, ll, rh, rl, rows_f, recv, front, out, tiles, tsem):
    t = pl.program_id(0)
    c, g = ids[2], ids[3]
    col = c * QT + t
    js = [where[ch, col] for ch in range(2)]
    there = [[where[ch, g * RT + p] >= 0 for p in range(RT)] for ch in range(2)]

    def each(act):
        for ch in range(2):
            for p in range(RT):

                @pl.when(there[ch][p] & (js[ch] >= 0))
                def _():
                    act(
                        pltpu.make_async_copy(
                            recv.at[js[ch] // CT, ch * RT + p],
                            tiles.at[ch * RT + p],
                            tsem.at[ch * RT + p],
                        )
                    )

    each(lambda copy: copy.start())
    out[...] = front[...] - dot3((lh[...], ll[...]), (rh[...], rl[...]))
    each(lambda copy: copy.wait())
    for p in range(RT):
        rows = slice(p * TILE, (p + 1) * TILE)
        for ch in range(2):

            @pl.when(there[ch][p] & (js[ch] >= 0))
            def _():
                out[rows, :] += as_float(tiles[ch * RT + p, 0:TILE, :]) * column_scale(
                    tiles[ch * RT + p, TILE:, :]
                )

    for a in range(2):

        @pl.when(col == ids[8 + a])
        def _():
            out[...] = rows_f[:, a * TILE : (a + 1) * TILE]


def final(ids, where, ph, plo, rows_f, recv, front):
    line = pl.BlockSpec((RT * TILE, TILE), lambda i, *s: (0, i))
    left = pl.BlockSpec((RT * TILE, PANEL), lambda i, *s: (0, 0))
    right = pl.BlockSpec((TILE, PANEL), lambda i, *s: (RT + i, 0))
    return pl.pallas_call(
        final_kernel,
        grid_spec=pltpu.PrefetchScalarGridSpec(
            num_scalar_prefetch=2,
            grid=(QT,),
            in_specs=[
                left,
                left,
                right,
                right,
                left,
                pl.BlockSpec(memory_space=pl.ANY),
                line,
            ],
            out_specs=line,
            scratch_shapes=[
                pltpu.VMEM((2 * RT, TILE + CODE, TILE), I16),
                pltpu.SemaphoreType.DMA((2 * RT,)),
            ],
        ),
        out_shape=jax.ShapeDtypeStruct((RT * TILE, QT * TILE), F32),
        compiler_params=pltpu.CompilerParams(vmem_limit_bytes=52 * MIB),
        cost_estimate=pl.CostEstimate(flops=1 << 32, bytes_accessed=20 * MIB, transcendentals=0),
    )(ids, where, ph, plo, ph, plo, rows_f, recv, front)


def pick(v, at):
    return lax.dynamic_index_in_dim(v, at, 0, keepdims=False)


def fetch_partner(panel, x, core, z, yh):
    tiles = panel.reshape(4, TILE, 1024)
    piece = pick(tiles, (z - x) % 4)
    halves = []
    for h in range(2):
        came = []
        for dx in (1, 2, 3):
            pairs = [
                (flat(c, xs, y, (xs + 2 * h + b) % 4, y), flat(c, (xs + dx) % 4, b, xs, y))
                for c in range(2)
                for xs in range(4)
                for y in range(2)
                for b in range(2)
            ]
            came.append(lax.ppermute(piece, AXES, pairs))
        halves.append(came)
    two = jnp.stack([pick(tiles, 1 - core), pick(tiles, 3 - core)])
    pairs = [
        (flat(c, x, y, x, y), flat(c, x, 1 - y, x, y))
        for c in range(2)
        for x in range(4)
        for y in range(2)
    ]
    beside = lax.ppermute(two, AXES, pairs)
    owner = (x == z) & (core == yh)
    way = (x - z) % 4
    mine = []
    for h in range(2):
        a, b, d = halves[h]
        got = jnp.where(way == 1, a, jnp.where(way == 2, b, jnp.where(way == 3, d, beside[h])))
        mine.append(jnp.where(owner, pick(tiles, core + 2 * h), got))
    mine = jnp.stack(mine)
    other = shift(mine, dk=1)
    even = jnp.where(core == 0, mine, other)
    odd = jnp.where(core == 0, other, mine)
    return jnp.stack([even[0], odd[0], even[1], odd[1]]).reshape(1024, 1024)


def sum_first(v, core, z):
    v = v.reshape(2, 256, PANEL)
    v = pick(v, core) + shift(pick(v, 1 - core), dk=1)
    v = v.reshape(4, 64, PANEL)
    got = [shift(pick(v, (z + d) % 4), dz=d) for d in (1, 3, 2)]
    return pick(v, z) + got[0] + got[1] + got[2]


def gathered(v, at, **axis):
    (name,) = axis
    full = jnp.zeros((4,) + v.shape, v.dtype)
    full = lax.dynamic_update_index_in_dim(full, v, at, 0)
    for d in (1, 3, 2):
        full = lax.dynamic_update_index_in_dim(full, shift(v, **{name: d}), (at - d) % 4, 0)
    return full


def sum_second(v, x, z):
    v = v.reshape(4, 16, PANEL)
    got = [shift(pick(v, (x + d) % 4), dx=d) for d in (1, 3, 2)]
    v = pick(v, x) + got[0] + got[1] + got[2]
    v = (v + shift(v, dc=1, dy=1)) + (shift(v, dc=1) + shift(v, dy=1))
    return gathered(v, z, dz=0)


def sum_third(v, x, core):
    v = gathered(v, x, dx=0)
    v = jnp.transpose(v, (1, 0, 2, 3)).reshape(256, PANEL)
    other = shift(v, dk=1)
    return jnp.concatenate([jnp.where(core == 0, v, other), jnp.where(core == 0, other, v)])


def tables(child_maps, parent_place):
    hit = child_maps[:, :, None] == jnp.arange(48, dtype=I32)
    slots = jnp.sum(jnp.where(hit, parent_place, 0), axis=2)
    hit = slots[:, :, None] == jnp.arange(48, dtype=I32)
    where = jnp.max(jnp.where(hit, jnp.arange(32, dtype=I32)[None, :, None], -1), axis=1)
    return slots, where


def body(child_blocks, child_panels, child_patterns, child_maps, parent_place, parent_front):
    ch, x, core, z, yh = (lax.axis_index(n).astype(I32) for n in AXES)
    r, c = x * 2 + core, z * 2 + yh
    slots, where = tables(child_maps, parent_place)
    e = parent_place[0], parent_place[1]
    ids = jnp.stack([ch, r, c, ch * 8 + r, core, z, yh, ch * 4 + x, e[0], e[1], x])
    panel = child_panels[0]
    partner = fetch_partner(panel, x, core, z, yh)
    send, diag, gcol = update(
        ids, slots, child_patterns, child_blocks[0], panel, partner, parent_front
    )
    own = lax.all_to_all(send, ("child", "x"), split_axis=0, concat_axis=0, tiled=True)

    diag = sum_first(diag, core, z)
    parts = strips(ids, gcol, parent_front)
    held = [pick(pick(where, ch), e[a]) // CT for a in range(2)]
    fronts = [e[a] // QT for a in range(2)]
    row = lax.broadcasted_iota(I32, (TILE, PANEL), 0)
    first = lax.broadcasted_iota(I32, (TILE, PANEL), 1) < TILE
    holder = jnp.where(
        row < FRONT,
        jnp.where(first, held[0], held[1]),
        jnp.where(first, fronts[0], fronts[1]),
    )
    away = (z - holder // 2 + 4) % 4
    strip = parts[0]
    for d in (1, 3, 2):
        strip = jnp.where(away == d, shift(parts[d], dz=d), strip)
    own, diag, strip = lax.optimization_barrier((own, diag, strip))

    other = shift(own, dk=1)
    send = route(ids, slots, where, own, other)
    kept, moved = pick(strip, yh), shift(pick(strip, 1 - yh), dy=1)
    strip = jnp.where(holder % 2 == yh, kept, moved)
    strip = jnp.stack([strip, shift(strip, dc=1)])
    diag = sum_second(diag, x, z)
    send, diag, strip = lax.optimization_barrier((send, diag, strip))
    recv = lax.all_to_all(send, ("z", "yh"), split_axis=0, concat_axis=0, tiled=True)

    diag = sum_third(diag, x, core)
    line = jnp.stack([strip] + [shift(strip, dx=d) for d in range(1, 4)])
    inv = inverse_factor(diag)
    gsend = compose(ids, where, line, shift(line, dk=1))
    recv, inv, gsend = lax.optimization_barrier((recv, inv, gsend))
    gx = lax.all_to_all(gsend, ("z", "yh"), split_axis=0, concat_axis=0, tiled=True)
    ph, plo, rows_f = panel_rows(ids, diag, inv, gx, shift(gx[:, 1], dk=1))
    return final(ids, where, ph, plo, rows_f, recv, parent_front)


def solution(mesh):
    fine = Mesh(mesh.devices.reshape(SIZES), AXES)
    rows, cols = ("x", "core"), ("z", "yh")
    return jax.shard_map(
        body,
        mesh=fine,
        in_specs=(
            P("child", rows, cols),
            P("child", rows, None),
            P(),
            P(),
            P(),
            P(("child", "x", "core"), cols),
        ),
        out_specs=P(("child", "x", "core"), cols),
        check_vma=False,
    )
```

```python
import jax
import jax.numpy as jnp
from jax import lax
from jax.experimental import pallas as pl
from jax.experimental.pallas import tpu as pltpu
from jax.sharding import Mesh
from jax.sharding import PartitionSpec as P

TILE = 256
PANEL = 512
CODE = 16
CT = 4
RT = 3
QT = 6
STRIP = 32
GROWS = 2 * RT * STRIP + CODE
CROWS = 2 * RT * TILE + CODE
AXES = ("child", "x", "core", "z", "yh")
SIZES = (2, 4, 2, 4, 2)
MIB = 1 << 20
F32 = jnp.float32
I32 = jnp.int32
I16 = jnp.int16
BF16 = jnp.bfloat16
HIGHEST = lax.Precision.HIGHEST


def flat(c, x, k, z, y):
    return (((c * 4 + x) * 2 + k) * 4 + z) * 2 + y


def everyone():
    return [
        (c, x, k, z, y)
        for c in range(2)
        for x in range(4)
        for k in range(2)
        for z in range(4)
        for y in range(2)
    ]


def shift(v, dc=0, dx=0, dk=0, dz=0, dy=0):
    pairs = [
        (flat(c, x, k, z, y), flat(c ^ dc, (x + dx) % 4, k ^ dk, (z + dz) % 4, y ^ dy))
        for c, x, k, z, y in everyone()
    ]
    return lax.ppermute(v, AXES, pairs)


def encode(u):
    top = jnp.max(jnp.abs(u), axis=0, keepdims=True)
    code = jnp.ceil(jnp.log2(jnp.maximum(top, 1e-30)) * 128.0)
    scale = jnp.exp2(15.0 - code * (1.0 / 128.0)) * (32766.0 / 32768.0)
    q = (u * scale + 32768.5).astype(I32) - 32768
    return q.astype(I16), code


def scale_rows(code):
    return jnp.broadcast_to(code, (CODE, code.shape[1])).astype(I32).astype(I16)


def as_float(q):
    return q.astype(I32).astype(F32)


def column_scale(codes, row=0):
    code = as_float(codes)[row : row + 1, :]
    return jnp.exp2(code * (1.0 / 128.0) - 15.0) * (32768.0 / 32766.0)


def update_kernel(ids, slots, pat, blk, pan, mine, other, front, send, diag, gcol, tile, sem):
    i = pl.program_id(0)
    ch, r, c, g = ids[0], ids[1], ids[2], ids[3]
    e = (ids[8], ids[9])

    @pl.when(i == 0)
    def _():
        diag[...] = jnp.zeros_like(diag)
        for a in range(2):
            for b in range(2):

                @pl.when((e[a] // RT == g) & (e[b] // QT == c))
                def _():
                    rows = pl.multiple_of((e[a] % RT) * TILE, TILE)
                    cols = pl.multiple_of((e[b] % QT) * TILE, TILE)
                    copy = pltpu.make_async_copy(
                        front.at[pl.ds(rows, TILE), pl.ds(cols, TILE)], tile, sem
                    )
                    copy.start()
                    copy.wait()
                    diag[a * TILE : (a + 1) * TILE, b * TILE : (b + 1) * TILE] = tile[...]

    si = slots[ch, r * CT + i]
    for n in range(CT):
        half = mine if n < 2 else other
        j = (ids[4] if n < 2 else 1 - ids[4]) * 2 + n % 2
        cols = pl.ds(pl.multiple_of(j * TILE, TILE), TILE)
        prod = lax.dot_general(
            pan[...],
            half[(n % 2) * TILE : (n % 2 + 1) * TILE, :],
            (((1,), (1,)), ((), ())),
            preferred_element_type=F32,
        )
        u = (blk[:, cols] - prod) * pat[ch, r * CT + i, c * CT + j].astype(F32)
        q, code = encode(u)
        send[0, 0:TILE, cols] = q
        send[0, TILE:, cols] = scale_rows(code)
        sj = slots[ch, c * CT + j]
        for b in range(2):
            at = slice(b * TILE, (b + 1) * TILE)

            @pl.when(sj == e[b])
            def _():
                gcol[:, at] = u
                for a in range(2):

                    @pl.when(si == e[a])
                    def _():
                        diag[a * TILE : (a + 1) * TILE, at] += u


def update(ids, slots, pat, blk, pan, mine, other, front):
    def slot(i, ids, slots, pat):
        return slots[ids[0], ids[1] * CT + i] // QT, 0, 0

    return pl.pallas_call(
        update_kernel,
        grid_spec=pltpu.PrefetchScalarGridSpec(
            num_scalar_prefetch=3,
            grid=(CT,),
            in_specs=[
                pl.BlockSpec((TILE, 1024), lambda i, *s: (i, 0)),
                pl.BlockSpec((TILE, 1024), lambda i, *s: (i, 0)),
                pl.BlockSpec((512, 1024), lambda i, *s: (0, 0)),
                pl.BlockSpec((512, 1024), lambda i, *s: (0, 0)),
                pl.BlockSpec(memory_space=pl.ANY),
            ],
            out_specs=[
                pl.BlockSpec((1, TILE + CODE, 1024), slot),
                pl.BlockSpec((PANEL, PANEL), lambda i, *s: (0, 0)),
                pl.BlockSpec((TILE, PANEL), lambda i, *s: (i, 0)),
            ],
            scratch_shapes=[pltpu.VMEM((TILE, TILE), F32), pltpu.SemaphoreType.DMA],
        ),
        out_shape=[
            pltpu.HBM((8, TILE + CODE, 1024), I16),
            pltpu.HBM((PANEL, PANEL), F32),
            pltpu.HBM((CT * TILE, PANEL), F32),
        ],
        compiler_params=pltpu.CompilerParams(vmem_limit_bytes=40 * MIB),
        cost_estimate=pl.CostEstimate(flops=1 << 31, bytes_accessed=14 * MIB, transcendentals=0),
    )(ids, slots, pat, blk, pan, mine, other, front)


def strips_kernel(ids, gcol, front, *rest):
    outs, (wide, sem) = rest[:4], rest[4:]
    c, z = ids[2], ids[5]
    for a in range(2):
        e = ids[8 + a]

        @pl.when(e // QT == c)
        def _():
            at = pl.multiple_of((e % QT) * TILE, TILE)
            copy = pltpu.make_async_copy(
                front.at[:, pl.ds(at, TILE)], wide.at[:, pl.ds(a * TILE, TILE)], sem
            )
            copy.start()
            copy.wait()

    for d in range(4):
        for f in range(2):
            s = ((z + d) % 4) * 2 + f
            at = 0
            for ref, n in ((gcol, CT), (wide, RT)):
                parts = [
                    ref[pl.ds(pl.multiple_of(p * TILE + s * STRIP, STRIP), STRIP), :]
                    for p in range(n)
                ]
                q, code = encode(jnp.concatenate(parts, 0))
                outs[d][f, at : at + n * STRIP, :] = q
                outs[d][f, at + n * STRIP : at + n * STRIP + CODE, :] = scale_rows(code)
                at += n * STRIP + CODE


def strips(ids, gcol, front):
    return pl.pallas_call(
        strips_kernel,
        grid_spec=pltpu.PrefetchScalarGridSpec(
            num_scalar_prefetch=1,
            grid=(1,),
            in_specs=[
                pl.BlockSpec((CT * TILE, PANEL), lambda i, *s: (0, 0)),
                pl.BlockSpec(memory_space=pl.ANY),
            ],
            out_specs=[pl.BlockSpec((2, TILE, PANEL), lambda i, *s: (0, 0, 0))] * 4,
            scratch_shapes=[pltpu.VMEM((RT * TILE, PANEL), F32), pltpu.SemaphoreType.DMA],
        ),
        out_shape=[jax.ShapeDtypeStruct((2, TILE, PANEL), I16)] * 4,
        compiler_params=pltpu.CompilerParams(vmem_limit_bytes=24 * MIB),
        cost_estimate=pl.CostEstimate(flops=0, bytes_accessed=6 * MIB, transcendentals=0),
    )(ids, gcol, front)


CHILD_CODE = CT * STRIP
FRONT = CHILD_CODE + CODE
FRONT_CODE = FRONT + RT * STRIP


def compose_kernel(ids, where, own, other, out, acc, kept, kcode):
    q = pl.program_id(0)
    ch, core, k, x = ids[0], ids[4], ids[7], ids[10]
    half = lax.broadcasted_iota(I32, (STRIP, PANEL), 1) < TILE

    def group(q):
        first = q * QT + core * RT
        d, f = lax.rem(x - q % 4 + 4, 4), lax.rem(ch + q // 4, 2)
        acc[...] = as_float(own[d, f, FRONT:FRONT_CODE, :]) * column_scale(
            own[d, f, FRONT_CODE:, :]
        )
        for m in range(2):
            known = [(where[m, ids[8 + a]] >= 0).astype(I32) for a in range(2)]
            mask = jnp.where(half, known[0], known[1]) > 0
            for p in range(RT):
                i = where[m, first + p]
                for here, ref in ((True, own), (False, other)):

                    @pl.when((i >= 0) & (((i // CT) % 2 == core) == here))
                    def _():
                        dm, fm = lax.rem(x - i // 8 + 4, 4), lax.rem(ch + m, 2)
                        row = pl.multiple_of((i % CT) * STRIP, STRIP)
                        v = as_float(ref[dm, fm, pl.ds(row, STRIP), :]) * column_scale(
                            ref[dm, fm, CHILD_CODE:FRONT, :]
                        )
                        acc[p * STRIP : (p + 1) * STRIP, :] += jnp.where(mask, v, 0.0)

        return encode(acc[...])

    @pl.when(q == 0)
    def _():
        v, code = group(k)
        kept[...] = v
        kcode[...] = jnp.broadcast_to(code, kcode.shape)

    v, code = group(q)
    out[0, 0 : RT * STRIP, :] = kept[...]
    out[0, RT * STRIP : 2 * RT * STRIP, :] = v
    row = lax.broadcasted_iota(I32, (CODE, PANEL), 0)
    both = jnp.where(row == 0, kcode[0:1, :], code)
    out[0, 2 * RT * STRIP :, :] = both.astype(I32).astype(I16)


def compose(ids, where, own, other):
    whole = pl.BlockSpec((4, 2, TILE, PANEL), lambda i, *s: (0, 0, 0, 0))
    return pl.pallas_call(
        compose_kernel,
        grid_spec=pltpu.PrefetchScalarGridSpec(
            num_scalar_prefetch=2,
            grid=(8,),
            in_specs=[whole] * 2,
            out_specs=pl.BlockSpec((1, GROWS, PANEL), lambda i, *s: (i, 0, 0)),
            scratch_shapes=[
                pltpu.VMEM((RT * STRIP, PANEL), F32),
                pltpu.VMEM((RT * STRIP, PANEL), I16),
                pltpu.VMEM((8, PANEL), F32),
            ],
        ),
        out_shape=pltpu.HBM((8, GROWS, PANEL), I16),
        compiler_params=pltpu.CompilerParams(vmem_limit_bytes=24 * MIB),
        cost_estimate=pl.CostEstimate(flops=0, bytes_accessed=6 * MIB, transcendentals=0),
    )(ids, where, own, other)


def route_kernel(ids, slots, where, own, other, send, codes, sems):
    c, g, core = ids[2], ids[3], ids[4]
    rows = [where[ch, g * RT + p] for ch in range(2) for p in range(RT)]

    def each(act):
        for m in range(2 * RT):
            i = rows[m]
            src = (m // RT) * 4 + i // 8
            for here, buf in ((True, own), (False, other)):

                @pl.when((i >= 0) & (((i // CT) % 2 == core) == here))
                def _():
                    act(
                        pltpu.make_async_copy(
                            buf.at[src, pl.ds(TILE, CODE), :], codes.at[m], sems.at[m * 5 + CT]
                        )
                    )
                    for j in range(CT):
                        q = slots[m // RT, c * CT + j] // QT
                        act(
                            pltpu.make_async_copy(
                                buf.at[src, pl.ds(0, TILE), pl.ds(j * TILE, TILE)],
                                send.at[q, pl.ds(m * TILE, TILE), :],
                                sems.at[m * 5 + j],
                            )
                        )

    each(lambda copy: copy.start())
    each(lambda copy: copy.wait())
    line = lax.broadcasted_iota(I32, (CODE, TILE), 0)
    for ch in range(2):
        for j in range(CT):
            q = slots[ch, c * CT + j] // QT
            at = (q, slice(2 * RT * TILE, CROWS), slice(None))
            v = send[at].astype(I32)
            for p in range(RT):
                m = ch * RT + p
                own_codes = codes[m, :, j * TILE : (j + 1) * TILE].astype(I32)
                v = jnp.where(line == m, own_codes, v)
            send[at] = v.astype(I16)


def route(ids, slots, where, own, other):
    return pl.pallas_call(
        route_kernel,
        grid_spec=pltpu.PrefetchScalarGridSpec(
            num_scalar_prefetch=3,
            grid=(1,),
            in_specs=[pl.BlockSpec(memory_space=pl.ANY)] * 2,
            out_specs=pl.BlockSpec((8, CROWS, TILE), lambda i, *s: (0, 0, 0)),
            scratch_shapes=[
                pltpu.VMEM((2 * RT, CODE, 1024), I16),
                pltpu.SemaphoreType.DMA((2 * RT * 5,)),
            ],
        ),
        out_shape=pltpu.HBM((8, CROWS, TILE), I16),
        compiler_params=pltpu.CompilerParams(vmem_limit_bytes=32 * MIB),
        cost_estimate=pl.CostEstimate(flops=0, bytes_accessed=8 * MIB, transcendentals=0),
    )(ids, slots, where, own, other)


def nt(a, b):
    return lax.dot_general(
        a, b, (((1,), (1,)), ((), ())), precision=HIGHEST, preferred_element_type=F32
    )


def nn(a, b):
    return lax.dot_general(
        a, b, (((1,), (0,)), ((), ())), precision=HIGHEST, preferred_element_type=F32
    )


NB = 128
WAYS = 4


def inverse_kernel(a_ref, out, w, f):
    n = PANEL // NB
    out[...] = jnp.zeros_like(out)
    row = lax.broadcasted_iota(I32, (NB, NB), 0)
    col = lax.broadcasted_iota(I32, (NB, NB), 1)
    eye = row == col
    lanes = lax.broadcasted_iota(I32, (1, 2 * NB), 1)
    sub = lax.broadcasted_iota(I32, (NB, 1), 0)

    def blk(i):
        return slice(i * NB, (i + 1) * NB)

    f[...] = a_ref[...]
    for k in range(n):
        w[:, :NB] = f[blk(k), blk(k)]
        w[:, NB:] = jnp.where(eye, 1.0, 0.0).astype(F32)

        def step(n4, _):
            j = n4 * WAYS
            lines = [w[pl.ds(j + a, 1), :] for a in range(WAYS)]
            square = w[:, :NB]
            columns = [
                jnp.sum(jnp.where(col == j + a, square, 0.0), axis=1, keepdims=True)
                for a in range(WAYS)
            ]
            small = [
                [
                    jnp.sum(jnp.where(lanes == j + b, lines[a], 0.0), axis=1, keepdims=True)
                    if b >= a
                    else None
                    for b in range(WAYS)
                ]
                for a in range(WAYS)
            ]
            factors = []
            for a in range(WAYS):
                inverse = 1.0 / small[a][a]
                for b in range(a + 1, WAYS):
                    times = small[a][b] * inverse
                    for d in range(b, WAYS):
                        small[b][d] = small[b][d] - times * small[a][d]
                    lines[b] = lines[b] - times * lines[a]
                    columns[b] = columns[b] - times * columns[a]
                factors.append(jnp.where(sub >= j + WAYS, columns[a] * inverse, 0.0))
            total = w[...]
            for a in range(WAYS):
                total = total - factors[a] * lines[a]
            w[...] = total
            for a in range(1, WAYS):
                w[pl.ds(j + a, 1), :] = lines[a]
            return 0

        lax.fori_loop(0, NB // WAYS, step, 0)
        d = jnp.sum(jnp.where(eye, w[:, :NB], 0.0), axis=1, keepdims=True)
        inv = w[:, NB:] * (1.0 / jnp.sqrt(d))
        out[blk(k), blk(k)] = inv
        rest = (k + 1) * NB
        if rest < PANEL:
            below = nt(f[rest:, blk(k)], inv)
            f[rest:, blk(k)] = below
            f[rest:, rest:] = f[rest:, rest:] - nt(below, below)
    for k in range(1, n):
        acc = nn(f[blk(k), : k * NB], out[: k * NB, : k * NB])
        out[blk(k), : k * NB] = -nn(out[blk(k), blk(k)], acc)


def inverse_factor(a):
    return pl.pallas_call(
        inverse_kernel,
        out_shape=jax.ShapeDtypeStruct((PANEL, PANEL), F32),
        scratch_shapes=[pltpu.VMEM((NB, 2 * NB), F32), pltpu.VMEM((PANEL, PANEL), F32)],
        compiler_params=pltpu.CompilerParams(vmem_limit_bytes=24 * MIB),
        cost_estimate=pl.CostEstimate(flops=1 << 34, bytes_accessed=2 * MIB, transcendentals=0),
    )(a)


def split(v):
    hi = v.astype(BF16)
    return hi, (v - hi.astype(F32)).astype(BF16)


def dot3(a, b):
    def one(x, y):
        return lax.dot_general(x, y, (((1,), (1,)), ((), ())), preferred_element_type=F32)

    return one(a[0], b[0]) + (one(a[0], b[1]) + one(a[1], b[0]))


def final_kernel(
    ids, where, diag, inv, gx, goth, recv, front, out,
    gbuf, rows_f, lh, ll, ih, il, tiles, codes, tsem,
):
    t = pl.program_id(0)
    c, g, core = ids[2], ids[3], ids[4]
    col = c * QT + t
    js = [where[ch, col] for ch in range(2)]
    there = [[where[ch, g * RT + p] >= 0 for p in range(RT)] for ch in range(2)]

    def each(act):
        for ch in range(2):
            src = js[ch] // CT

            @pl.when(js[ch] >= 0)
            def _():
                act(
                    pltpu.make_async_copy(
                        recv.at[src, pl.ds(2 * RT * TILE, CODE), :],
                        codes.at[ch],
                        tsem.at[2 * RT + ch],
                    )
                )

            for p in range(RT):
                m = ch * RT + p

                @pl.when(there[ch][p] & (js[ch] >= 0))
                def _():
                    act(
                        pltpu.make_async_copy(
                            recv.at[src, pl.ds(m * TILE, TILE), :], tiles.at[m], tsem.at[m]
                        )
                    )

    each(lambda copy: copy.start())

    @pl.when(t == 0)
    def _():
        hi, lo = split(inv[...])
        ih[...] = hi
        il[...] = lo
        for s in range(8):
            scale = column_scale(gx[s, 2 * RT * STRIP :, :], 0)
            v = as_float(gx[s, 0 : RT * STRIP, :]) * scale
            for p in range(RT):
                gbuf[p * TILE + s * STRIP : p * TILE + (s + 1) * STRIP, :] = v[
                    p * STRIP : (p + 1) * STRIP, :
                ]
        for p in range(RT):
            for a in range(2):

                @pl.when(g * RT + p == ids[8 + a])
                def _():
                    gbuf[p * TILE : (p + 1) * TILE, :] = diag[a * TILE : (a + 1) * TILE, :]

        v = dot3(split(gbuf[...]), (ih[...], il[...]))
        rows_f[...] = v
        hi, lo = split(v)
        lh[...] = hi
        ll[...] = lo

    side = pl.multiple_of((t % RT) * STRIP, STRIP)

    @pl.when(t // RT == core)
    def _():
        for s in range(8):
            gbuf[s * STRIP : (s + 1) * STRIP, :] = as_float(
                gx[s, pl.ds(RT * STRIP + side, STRIP), :]
            ) * column_scale(gx[s, 2 * RT * STRIP :, :], 1)

    @pl.when(t // RT != core)
    def _():
        for s in range(8):
            gbuf[s * STRIP : (s + 1) * STRIP, :] = as_float(
                goth[s, pl.ds(side, STRIP), :]
            ) * column_scale(goth[s, RT * STRIP :, :], 1)

    for a in range(2):

        @pl.when(col == ids[8 + a])
        def _():
            gbuf[0:TILE, :] = diag[a * TILE : (a + 1) * TILE, :]

    right = split(dot3(split(gbuf[0:TILE, :]), (ih[...], il[...])))
    out[...] = front[...] - dot3((lh[...], ll[...]), right)
    each(lambda copy: copy.wait())
    for p in range(RT):
        rows = slice(p * TILE, (p + 1) * TILE)
        for ch in range(2):
            m = ch * RT + p

            @pl.when(there[ch][p] & (js[ch] >= 0))
            def _():
                out[rows, :] += as_float(tiles[m]) * column_scale(codes[ch], m)

    for a in range(2):

        @pl.when(col == ids[8 + a])
        def _():
            out[...] = rows_f[:, a * TILE : (a + 1) * TILE]


def final(ids, where, diag, inv, gx, goth, recv, front):
    def whole(*shape):
        return pl.BlockSpec(shape, lambda i, *s: (0,) * len(shape))

    line = pl.BlockSpec((RT * TILE, TILE), lambda i, *s: (0, i))
    return pl.pallas_call(
        final_kernel,
        grid_spec=pltpu.PrefetchScalarGridSpec(
            num_scalar_prefetch=2,
            grid=(QT,),
            in_specs=[
                whole(PANEL, PANEL),
                whole(PANEL, PANEL),
                whole(8, GROWS, PANEL),
                whole(8, GROWS - RT * STRIP, PANEL),
                pl.BlockSpec(memory_space=pl.ANY),
                line,
            ],
            out_specs=line,
            scratch_shapes=[
                pltpu.VMEM((RT * TILE, PANEL), F32),
                pltpu.VMEM((RT * TILE, PANEL), F32),
                pltpu.VMEM((RT * TILE, PANEL), BF16),
                pltpu.VMEM((RT * TILE, PANEL), BF16),
                pltpu.VMEM((PANEL, PANEL), BF16),
                pltpu.VMEM((PANEL, PANEL), BF16),
                pltpu.VMEM((2 * RT, TILE, TILE), I16),
                pltpu.VMEM((2, CODE, TILE), I16),
                pltpu.SemaphoreType.DMA((2 * RT + 2,)),
            ],
        ),
        out_shape=jax.ShapeDtypeStruct((RT * TILE, QT * TILE), F32),
        compiler_params=pltpu.CompilerParams(vmem_limit_bytes=52 * MIB),
        cost_estimate=pl.CostEstimate(flops=1 << 33, bytes_accessed=20 * MIB, transcendentals=0),
    )(ids, where, diag, inv, gx, goth, recv, front)


def pick(v, at):
    return lax.dynamic_index_in_dim(v, at, 0, keepdims=False)


def fetch_partner(panel, x, core, z, yh):
    halves = panel.reshape(2, 512, 1024)
    piece = pick(halves, ((z - x + 4) % 4) // 2)
    came = []
    for dx in (1, 2, 3):
        pairs = [
            (flat(c, xs, y, (xs + 2 * b) % 4, y), flat(c, (xs + dx) % 4, b, xs, y))
            for c in range(2)
            for xs in range(4)
            for y in range(2)
            for b in range(2)
        ]
        came.append(lax.ppermute(piece, AXES, pairs))
    pairs = [
        (flat(c, x, y, x, y), flat(c, x, 1 - y, x, y))
        for c in range(2)
        for x in range(4)
        for y in range(2)
    ]
    beside = lax.ppermute(pick(halves, 1 - core), AXES, pairs)
    way = (x - z + 4) % 4
    mine = jnp.where(way == 1, came[0], jnp.where(way == 2, came[1], came[2]))
    mine = jnp.where(way == 0, jnp.where(core == yh, pick(halves, core), beside), mine)
    return mine, shift(mine, dk=1)


def sum_first(v, core, z):
    v = v.reshape(2, 256, PANEL)
    v = pick(v, core) + shift(pick(v, 1 - core), dk=1)
    v = v.reshape(4, 64, PANEL)
    got = [shift(pick(v, (z + d) % 4), dz=d) for d in (1, 3, 2)]
    v = pick(v, z) + got[0] + got[1] + got[2]
    return gathered(v, z, dz=0).reshape(256, PANEL)


def gathered(v, at, **axis):
    (name,) = axis
    full = jnp.zeros((4,) + v.shape, v.dtype)
    full = lax.dynamic_update_index_in_dim(full, v, at, 0)
    for d in (1, 3, 2):
        full = lax.dynamic_update_index_in_dim(full, shift(v, **{name: d}), (at - d) % 4, 0)
    return full


def sum_second(v, x):
    v = v.reshape(4, 64, PANEL)
    got = [shift(pick(v, (x + d) % 4), dx=d) for d in (1, 3, 2)]
    v = pick(v, x) + got[0] + got[1] + got[2]
    return (v + shift(v, dc=1, dy=1)) + (shift(v, dc=1) + shift(v, dy=1))


def sum_third(v, x, core):
    v = gathered(v, x, dx=0).reshape(256, PANEL)
    other = shift(v, dk=1)
    return jnp.concatenate([jnp.where(core == 0, v, other), jnp.where(core == 0, other, v)])


def tables(child_maps, parent_place):
    hit = child_maps[:, :, None] == jnp.arange(48, dtype=I32)
    slots = jnp.sum(jnp.where(hit, parent_place, 0), axis=2)
    hit = slots[:, :, None] == jnp.arange(48, dtype=I32)
    where = jnp.max(jnp.where(hit, jnp.arange(32, dtype=I32)[None, :, None], -1), axis=1)
    return slots, where


def body(child_blocks, child_panels, child_patterns, child_maps, parent_place, parent_front):
    ch, x, core, z, yh = (lax.axis_index(n).astype(I32) for n in AXES)
    r, c = x * 2 + core, z * 2 + yh
    slots, where = tables(child_maps, parent_place)
    e = parent_place[0], parent_place[1]
    ids = jnp.stack([ch, r, c, ch * 8 + r, core, z, yh, ch * 4 + x, e[0], e[1], x])
    panel = child_panels[0]
    parent_front = pltpu.with_memory_space_constraint(parent_front, pltpu.HBM)
    block = pltpu.with_memory_space_constraint(child_blocks[0], pltpu.HBM)
    mine, theirs = fetch_partner(panel, x, core, z, yh)
    send, diag, gcol = update(
        ids, slots, child_patterns, block, panel, mine, theirs, parent_front
    )
    own = lax.all_to_all(send, ("child", "x"), split_axis=0, concat_axis=0, tiled=True)

    diag = sum_first(diag, core, z)
    parts = strips(ids, gcol, parent_front)
    held = [pick(pick(where, ch), e[a]) // CT for a in range(2)]
    fronts = [e[a] // QT for a in range(2)]
    row = lax.broadcasted_iota(I32, (TILE, PANEL), 0)
    first = lax.broadcasted_iota(I32, (TILE, PANEL), 1) < TILE
    holder = jnp.where(
        row < FRONT,
        jnp.where(first, held[0], held[1]),
        jnp.where(first, fronts[0], fronts[1]),
    )
    away = (z - holder // 2 + 4) % 4
    strip = parts[0]
    for d in (1, 3, 2):
        strip = jnp.where(away == d, shift(parts[d], dz=d), strip)
    own, diag, strip = lax.optimization_barrier((own, diag, strip))

    other = shift(own, dk=1)
    send = route(ids, slots, where, own, other)
    kept, moved = pick(strip, yh), shift(pick(strip, 1 - yh), dy=1)
    strip = jnp.where(holder % 2 == yh, kept, moved)
    strip = jnp.stack([strip, shift(strip, dc=1)])
    diag = sum_second(diag, x)
    send, diag, strip = lax.optimization_barrier((send, diag, strip))
    recv = lax.all_to_all(send, ("z", "yh"), split_axis=0, concat_axis=0, tiled=True)

    diag = sum_third(diag, x, core)
    line = jnp.stack([strip] + [shift(strip, dx=d) for d in range(1, 4)])
    inv = inverse_factor(diag)
    gsend = compose(ids, where, line, shift(line, dk=1))
    recv, inv, gsend = lax.optimization_barrier((recv, inv, gsend))
    gx = lax.all_to_all(gsend, ("z", "yh"), split_axis=0, concat_axis=0, tiled=True)
    goth = shift(gx[:, RT * STRIP :], dk=1)
    return final(ids, where, diag, inv, gx, goth, recv, parent_front)


def solution(mesh):
    fine = Mesh(mesh.devices.reshape(SIZES), AXES)
    rows, cols = ("x", "core"), ("z", "yh")
    return jax.shard_map(
        body,
        mesh=fine,
        in_specs=(
            P("child", rows, cols),
            P("child", rows, None),
            P(),
            P(),
            P(),
            P(("child", "x", "core"), cols),
        ),
        out_specs=P(("child", "x", "core"), cols),
        check_vma=False,
    )
```

```python
import jax
import jax.numpy as jnp
from jax import lax
from jax.experimental import pallas as pl
from jax.experimental.pallas import tpu as pltpu
from jax.sharding import Mesh
from jax.sharding import PartitionSpec as P

TILE = 256
PANEL = 512
CODE = 16
CT = 4
RT = 3
QT = 6
STRIP = 32
GROWS = 2 * RT * STRIP + CODE
CROWS = 2 * RT * TILE + CODE
AXES = ("child", "x", "core", "z", "yh")
SIZES = (2, 4, 2, 4, 2)
MIB = 1 << 20
F32 = jnp.float32
I32 = jnp.int32
I16 = jnp.int16
BF16 = jnp.bfloat16
HIGHEST = lax.Precision.HIGHEST


def flat(c, x, k, z, y):
    return (((c * 4 + x) * 2 + k) * 4 + z) * 2 + y


def everyone():
    return [
        (c, x, k, z, y)
        for c in range(2)
        for x in range(4)
        for k in range(2)
        for z in range(4)
        for y in range(2)
    ]


def shift(v, dc=0, dx=0, dk=0, dz=0, dy=0):
    pairs = [
        (flat(c, x, k, z, y), flat(c ^ dc, (x + dx) % 4, k ^ dk, (z + dz) % 4, y ^ dy))
        for c, x, k, z, y in everyone()
    ]
    return lax.ppermute(v, AXES, pairs)


def encode(u):
    top = jnp.max(jnp.abs(u), axis=0, keepdims=True)
    code = jnp.ceil(jnp.log2(jnp.maximum(top, 1e-30)) * 128.0)
    scale = jnp.exp2(15.0 - code * (1.0 / 128.0)) * (32766.0 / 32768.0)
    return jnp.floor(u * scale + 0.5).astype(I32).astype(I16), code


def scale_rows(code):
    return jnp.broadcast_to(code, (CODE, code.shape[1])).astype(I32).astype(I16)


def as_float(q):
    return q.astype(I32).astype(F32)


def column_scale(codes, row=0):
    code = as_float(codes)[row : row + 1, :]
    return jnp.exp2(code * (1.0 / 128.0) - 15.0) * (32768.0 / 32766.0)


def update_kernel(ids, slots, pat, blk, pan, mine, other, front, send, diag, gcol, tile, sem):
    i = pl.program_id(0)
    ch, r, c, g = ids[0], ids[1], ids[2], ids[3]
    e = (ids[8], ids[9])

    @pl.when(i == 0)
    def _():
        diag[...] = jnp.zeros_like(diag)
        for a in range(2):
            for b in range(2):

                @pl.when((e[a] // RT == g) & (e[b] // QT == c))
                def _():
                    rows = pl.multiple_of((e[a] % RT) * TILE, TILE)
                    cols = pl.multiple_of((e[b] % QT) * TILE, TILE)
                    copy = pltpu.make_async_copy(
                        front.at[pl.ds(rows, TILE), pl.ds(cols, TILE)], tile, sem
                    )
                    copy.start()
                    copy.wait()
                    diag[a * TILE : (a + 1) * TILE, b * TILE : (b + 1) * TILE] = tile[...]

    si = slots[ch, r * CT + i]
    for n in range(CT):
        half = mine if n < 2 else other
        j = (ids[4] if n < 2 else 1 - ids[4]) * 2 + n % 2
        cols = pl.ds(pl.multiple_of(j * TILE, TILE), TILE)
        prod = lax.dot_general(
            pan[...],
            half[(n % 2) * TILE : (n % 2 + 1) * TILE, :],
            (((1,), (1,)), ((), ())),
            preferred_element_type=F32,
        )
        u = (blk[:, cols] - prod) * pat[ch, r * CT + i, c * CT + j].astype(F32)
        q, code = encode(u)
        send[0, 0:TILE, cols] = q
        send[0, TILE:, cols] = scale_rows(code)
        sj = slots[ch, c * CT + j]
        for b in range(2):
            at = slice(b * TILE, (b + 1) * TILE)

            @pl.when(sj == e[b])
            def _():
                gcol[:, at] = u
                for a in range(2):

                    @pl.when(si == e[a])
                    def _():
                        diag[a * TILE : (a + 1) * TILE, at] += u


def update(ids, slots, pat, blk, pan, mine, other, front):
    def slot(i, ids, slots, pat):
        return slots[ids[0], ids[1] * CT + i] // QT, 0, 0

    return pl.pallas_call(
        update_kernel,
        grid_spec=pltpu.PrefetchScalarGridSpec(
            num_scalar_prefetch=3,
            grid=(CT,),
            in_specs=[
                pl.BlockSpec((TILE, 1024), lambda i, *s: (i, 0)),
                pl.BlockSpec((TILE, 1024), lambda i, *s: (i, 0)),
                pl.BlockSpec((512, 1024), lambda i, *s: (0, 0)),
                pl.BlockSpec((512, 1024), lambda i, *s: (0, 0)),
                pl.BlockSpec(memory_space=pl.ANY),
            ],
            out_specs=[
                pl.BlockSpec((1, TILE + CODE, 1024), slot),
                pl.BlockSpec((PANEL, PANEL), lambda i, *s: (0, 0)),
                pl.BlockSpec((TILE, PANEL), lambda i, *s: (i, 0)),
            ],
            scratch_shapes=[pltpu.VMEM((TILE, TILE), F32), pltpu.SemaphoreType.DMA],
        ),
        out_shape=[
            pltpu.HBM((8, TILE + CODE, 1024), I16),
            pltpu.HBM((PANEL, PANEL), F32),
            pltpu.HBM((CT * TILE, PANEL), F32),
        ],
        compiler_params=pltpu.CompilerParams(vmem_limit_bytes=40 * MIB),
        cost_estimate=pl.CostEstimate(flops=1 << 31, bytes_accessed=14 * MIB, transcendentals=0),
    )(ids, slots, pat, blk, pan, mine, other, front)


def strips_kernel(ids, gcol, front, *rest):
    outs, (wide, sem) = rest[:4], rest[4:]
    c, z = ids[2], ids[5]
    for a in range(2):
        e = ids[8 + a]

        @pl.when(e // QT == c)
        def _():
            at = pl.multiple_of((e % QT) * TILE, TILE)
            copy = pltpu.make_async_copy(
                front.at[:, pl.ds(at, TILE)], wide.at[:, pl.ds(a * TILE, TILE)], sem
            )
            copy.start()
            copy.wait()

    for d in range(4):
        for f in range(2):
            s = ((z + d) % 4) * 2 + f
            at = 0
            for ref, n in ((gcol, CT), (wide, RT)):
                parts = [
                    ref[pl.ds(pl.multiple_of(p * TILE + s * STRIP, STRIP), STRIP), :]
                    for p in range(n)
                ]
                q, code = encode(jnp.concatenate(parts, 0))
                outs[d][f, at : at + n * STRIP, :] = q
                outs[d][f, at + n * STRIP : at + n * STRIP + CODE, :] = scale_rows(code)
                at += n * STRIP + CODE


def strips(ids, gcol, front):
    return pl.pallas_call(
        strips_kernel,
        grid_spec=pltpu.PrefetchScalarGridSpec(
            num_scalar_prefetch=1,
            grid=(1,),
            in_specs=[
                pl.BlockSpec((CT * TILE, PANEL), lambda i, *s: (0, 0)),
                pl.BlockSpec(memory_space=pl.ANY),
            ],
            out_specs=[pl.BlockSpec((2, TILE, PANEL), lambda i, *s: (0, 0, 0))] * 4,
            scratch_shapes=[pltpu.VMEM((RT * TILE, PANEL), F32), pltpu.SemaphoreType.DMA],
        ),
        out_shape=[jax.ShapeDtypeStruct((2, TILE, PANEL), I16)] * 4,
        compiler_params=pltpu.CompilerParams(vmem_limit_bytes=24 * MIB),
        cost_estimate=pl.CostEstimate(flops=0, bytes_accessed=6 * MIB, transcendentals=0),
    )(ids, gcol, front)


CHILD_CODE = CT * STRIP
FRONT = CHILD_CODE + CODE
FRONT_CODE = FRONT + RT * STRIP


def regions(ids, where, child):
    for a in range(2):
        cols = slice(a * TILE, (a + 1) * TILE)
        yield slice(0, FRONT), cols, where[child, ids[8 + a]] // CT
        yield slice(FRONT, TILE), cols, ids[8 + a] // QT


def choose_z_kernel(ids, where, *refs):
    for rows, cols, holder in regions(ids, where, ids[0]):
        for d in range(4):

            @pl.when(lax.rem(ids[5] - holder // 2 + 4, 4) == d)
            def _():
                refs[4][:, rows, cols] = refs[d][:, rows, cols]


def choose_z(ids, where, parts):
    whole = pl.BlockSpec((2, TILE, PANEL), lambda i, *s: (0, 0, 0))
    return pl.pallas_call(
        choose_z_kernel,
        grid_spec=pltpu.PrefetchScalarGridSpec(
            num_scalar_prefetch=2, grid=(1,), in_specs=[whole] * 4, out_specs=whole
        ),
        out_shape=jax.ShapeDtypeStruct((2, TILE, PANEL), I16),
        cost_estimate=pl.CostEstimate(flops=0, bytes_accessed=3 * MIB, transcendentals=0),
    )(ids, where, *parts)


def choose_y_kernel(ids, where, kept, beside, across, both, out):
    for n, (near, far) in enumerate(((kept, beside), (across, both))):
        child = lax.rem(ids[0] + n, 2)
        for rows, cols, holder in regions(ids, where, child):
            here = lax.rem(holder + 8, 2) == ids[6]

            @pl.when(here)
            def _():
                out[n, rows, cols] = near[rows, cols]

            @pl.when(jnp.logical_not(here))
            def _():
                out[n, rows, cols] = far[rows, cols]


def choose_y(ids, where, parts):
    whole = pl.BlockSpec((TILE, PANEL), lambda i, *s: (0, 0))
    return pl.pallas_call(
        choose_y_kernel,
        grid_spec=pltpu.PrefetchScalarGridSpec(
            num_scalar_prefetch=2,
            grid=(1,),
            in_specs=[whole] * 4,
            out_specs=pl.BlockSpec((2, TILE, PANEL), lambda i, *s: (0, 0, 0)),
        ),
        out_shape=jax.ShapeDtypeStruct((2, TILE, PANEL), I16),
        cost_estimate=pl.CostEstimate(flops=0, bytes_accessed=2 * MIB, transcendentals=0),
    )(ids, where, *parts)


def compose_kernel(ids, where, own, other, out, acc, kept, kcode):
    q = pl.program_id(0)
    ch, core, k, x = ids[0], ids[4], ids[7], ids[10]
    half = lax.broadcasted_iota(I32, (STRIP, PANEL), 1) < TILE

    def group(q):
        first = q * QT + core * RT
        d, f = lax.rem(x - q % 4 + 4, 4), lax.rem(ch + q // 4, 2)
        acc[...] = as_float(own[d, f, FRONT:FRONT_CODE, :]) * column_scale(
            own[d, f, FRONT_CODE:, :]
        )
        for m in range(2):
            known = [(where[m, ids[8 + a]] >= 0).astype(I32) for a in range(2)]
            mask = jnp.where(half, known[0], known[1]) > 0
            for p in range(RT):
                i = where[m, first + p]
                for here, ref in ((True, own), (False, other)):

                    @pl.when((i >= 0) & (((i // CT) % 2 == core) == here))
                    def _():
                        dm, fm = lax.rem(x - i // 8 + 4, 4), lax.rem(ch + m, 2)
                        row = pl.multiple_of((i % CT) * STRIP, STRIP)
                        v = as_float(ref[dm, fm, pl.ds(row, STRIP), :]) * column_scale(
                            ref[dm, fm, CHILD_CODE:FRONT, :]
                        )
                        acc[p * STRIP : (p + 1) * STRIP, :] += jnp.where(mask, v, 0.0)

        return encode(acc[...])

    @pl.when(q == 0)
    def _():
        v, code = group(k)
        kept[...] = v
        kcode[...] = jnp.broadcast_to(code, kcode.shape)

    v, code = group(q)
    out[0, 0 : RT * STRIP, :] = kept[...]
    out[0, RT * STRIP : 2 * RT * STRIP, :] = v
    row = lax.broadcasted_iota(I32, (CODE, PANEL), 0)
    both = jnp.where(row == 0, kcode[0:1, :], code)
    out[0, 2 * RT * STRIP :, :] = both.astype(I32).astype(I16)


def compose(ids, where, own, other):
    whole = pl.BlockSpec((4, 2, TILE, PANEL), lambda i, *s: (0, 0, 0, 0))
    return pl.pallas_call(
        compose_kernel,
        grid_spec=pltpu.PrefetchScalarGridSpec(
            num_scalar_prefetch=2,
            grid=(8,),
            in_specs=[whole] * 2,
            out_specs=pl.BlockSpec((1, GROWS, PANEL), lambda i, *s: (i, 0, 0)),
            scratch_shapes=[
                pltpu.VMEM((RT * STRIP, PANEL), F32),
                pltpu.VMEM((RT * STRIP, PANEL), I16),
                pltpu.VMEM((8, PANEL), F32),
            ],
        ),
        out_shape=pltpu.HBM((8, GROWS, PANEL), I16),
        compiler_params=pltpu.CompilerParams(vmem_limit_bytes=24 * MIB),
        cost_estimate=pl.CostEstimate(flops=0, bytes_accessed=6 * MIB, transcendentals=0),
    )(ids, where, own, other)


def route_kernel(ids, slots, where, own, other, send, codes, sems):
    c, g, core = ids[2], ids[3], ids[4]
    rows = [where[ch, g * RT + p] for ch in range(2) for p in range(RT)]

    def each(act):
        for m in range(2 * RT):
            i = rows[m]
            src = (m // RT) * 4 + i // 8
            for here, buf in ((True, own), (False, other)):

                @pl.when((i >= 0) & (((i // CT) % 2 == core) == here))
                def _():
                    act(
                        pltpu.make_async_copy(
                            buf.at[src, pl.ds(TILE, CODE), :], codes.at[m], sems.at[m * 5 + CT]
                        )
                    )
                    for j in range(CT):
                        q = slots[m // RT, c * CT + j] // QT
                        act(
                            pltpu.make_async_copy(
                                buf.at[src, pl.ds(0, TILE), pl.ds(j * TILE, TILE)],
                                send.at[q, pl.ds(m * TILE, TILE), :],
                                sems.at[m * 5 + j],
                            )
                        )

    each(lambda copy: copy.start())
    each(lambda copy: copy.wait())
    line = lax.broadcasted_iota(I32, (CODE, TILE), 0)
    for ch in range(2):
        for j in range(CT):
            q = slots[ch, c * CT + j] // QT
            at = (q, slice(2 * RT * TILE, CROWS), slice(None))
            v = send[at].astype(I32)
            for p in range(RT):
                m = ch * RT + p
                own_codes = codes[m, :, j * TILE : (j + 1) * TILE].astype(I32)
                v = jnp.where(line == m, own_codes, v)
            send[at] = v.astype(I16)


def route(ids, slots, where, own, other):
    return pl.pallas_call(
        route_kernel,
        grid_spec=pltpu.PrefetchScalarGridSpec(
            num_scalar_prefetch=3,
            grid=(1,),
            in_specs=[pl.BlockSpec(memory_space=pl.ANY)] * 2,
            out_specs=pl.BlockSpec((8, CROWS, TILE), lambda i, *s: (0, 0, 0)),
            scratch_shapes=[
                pltpu.VMEM((2 * RT, CODE, 1024), I16),
                pltpu.SemaphoreType.DMA((2 * RT * 5,)),
            ],
        ),
        out_shape=pltpu.HBM((8, CROWS, TILE), I16),
        compiler_params=pltpu.CompilerParams(vmem_limit_bytes=32 * MIB),
        cost_estimate=pl.CostEstimate(flops=0, bytes_accessed=8 * MIB, transcendentals=0),
    )(ids, slots, where, own, other)


def nt(a, b):
    return lax.dot_general(
        a, b, (((1,), (1,)), ((), ())), precision=HIGHEST, preferred_element_type=F32
    )


def nn(a, b):
    return lax.dot_general(
        a, b, (((1,), (0,)), ((), ())), precision=HIGHEST, preferred_element_type=F32
    )


NB = 128
WAYS = 4


def inverse_kernel(a_ref, out, w, f):
    n = PANEL // NB
    out[...] = jnp.zeros_like(out)
    row = lax.broadcasted_iota(I32, (NB, NB), 0)
    col = lax.broadcasted_iota(I32, (NB, NB), 1)
    eye = row == col
    lanes = lax.broadcasted_iota(I32, (1, 2 * NB), 1)
    sub = lax.broadcasted_iota(I32, (NB, 1), 0)

    def blk(i):
        return slice(i * NB, (i + 1) * NB)

    f[...] = a_ref[...]
    for k in range(n):
        w[:, :NB] = f[blk(k), blk(k)]
        w[:, NB:] = jnp.where(eye, 1.0, 0.0).astype(F32)

        def step(n4, _):
            j = n4 * WAYS
            lines = [w[pl.ds(j + a, 1), :] for a in range(WAYS)]
            square = w[:, :NB]
            columns = [
                jnp.sum(jnp.where(col == j + a, square, 0.0), axis=1, keepdims=True)
                for a in range(WAYS)
            ]
            small = [
                [
                    jnp.sum(jnp.where(lanes == j + b, lines[a], 0.0), axis=1, keepdims=True)
                    if b >= a
                    else None
                    for b in range(WAYS)
                ]
                for a in range(WAYS)
            ]
            factors = []
            for a in range(WAYS):
                inverse = 1.0 / small[a][a]
                for b in range(a + 1, WAYS):
                    times = small[a][b] * inverse
                    for d in range(b, WAYS):
                        small[b][d] = small[b][d] - times * small[a][d]
                    lines[b] = lines[b] - times * lines[a]
                    columns[b] = columns[b] - times * columns[a]
                factors.append(jnp.where(sub >= j + WAYS, columns[a] * inverse, 0.0))
            total = w[...]
            for a in range(WAYS):
                total = total - factors[a] * lines[a]
            w[...] = total
            for a in range(1, WAYS):
                w[pl.ds(j + a, 1), :] = lines[a]
            return 0

        lax.fori_loop(0, NB // WAYS, step, 0)
        d = jnp.sum(jnp.where(eye, w[:, :NB], 0.0), axis=1, keepdims=True)
        inv = w[:, NB:] * (1.0 / jnp.sqrt(d))
        out[blk(k), blk(k)] = inv
        rest = (k + 1) * NB
        if rest < PANEL:
            below = nt(f[rest:, blk(k)], inv)
            f[rest:, blk(k)] = below
            f[rest:, rest:] = f[rest:, rest:] - nt(below, below)
    for k in range(1, n):
        acc = nn(f[blk(k), : k * NB], out[: k * NB, : k * NB])
        out[blk(k), : k * NB] = -nn(out[blk(k), blk(k)], acc)


def inverse_factor(a):
    return pl.pallas_call(
        inverse_kernel,
        out_shape=jax.ShapeDtypeStruct((PANEL, PANEL), F32),
        scratch_shapes=[pltpu.VMEM((NB, 2 * NB), F32), pltpu.VMEM((PANEL, PANEL), F32)],
        compiler_params=pltpu.CompilerParams(vmem_limit_bytes=24 * MIB),
        cost_estimate=pl.CostEstimate(flops=1 << 34, bytes_accessed=2 * MIB, transcendentals=0),
    )(a)


def split(v):
    hi = v.astype(BF16)
    return hi, (v - hi.astype(F32)).astype(BF16)


def dot3(a, b):
    def one(x, y):
        return lax.dot_general(x, y, (((1,), (1,)), ((), ())), preferred_element_type=F32)

    return one(a[0], b[0]) + (one(a[0], b[1]) + one(a[1], b[0]))


def final_kernel(
    ids, where, diag, inv, gx, goth, recv, front, out,
    gbuf, rows_f, lh, ll, ih, il, tiles, codes, tsem,
):
    t = pl.program_id(0)
    c, g, core = ids[2], ids[3], ids[4]
    col = c * QT + t
    js = [where[ch, col] for ch in range(2)]
    there = [[where[ch, g * RT + p] >= 0 for p in range(RT)] for ch in range(2)]

    def each(act):
        for ch in range(2):
            src = js[ch] // CT

            @pl.when(js[ch] >= 0)
            def _():
                act(
                    pltpu.make_async_copy(
                        recv.at[src, pl.ds(2 * RT * TILE, CODE), :],
                        codes.at[ch],
                        tsem.at[2 * RT + ch],
                    )
                )

            for p in range(RT):
                m = ch * RT + p

                @pl.when(there[ch][p] & (js[ch] >= 0))
                def _():
                    act(
                        pltpu.make_async_copy(
                            recv.at[src, pl.ds(m * TILE, TILE), :], tiles.at[m], tsem.at[m]
                        )
                    )

    each(lambda copy: copy.start())

    @pl.when(t == 0)
    def _():
        hi, lo = split(inv[...])
        ih[...] = hi
        il[...] = lo
        for s in range(8):
            scale = column_scale(gx[s, 2 * RT * STRIP :, :], 0)
            v = as_float(gx[s, 0 : RT * STRIP, :]) * scale
            for p in range(RT):
                gbuf[p * TILE + s * STRIP : p * TILE + (s + 1) * STRIP, :] = v[
                    p * STRIP : (p + 1) * STRIP, :
                ]
        for p in range(RT):
            for a in range(2):

                @pl.when(g * RT + p == ids[8 + a])
                def _():
                    gbuf[p * TILE : (p + 1) * TILE, :] = diag[a * TILE : (a + 1) * TILE, :]

        v = dot3(split(gbuf[...]), (ih[...], il[...]))
        rows_f[...] = v
        hi, lo = split(v)
        lh[...] = hi
        ll[...] = lo

    side = pl.multiple_of((t % RT) * STRIP, STRIP)

    @pl.when(t // RT == core)
    def _():
        for s in range(8):
            gbuf[s * STRIP : (s + 1) * STRIP, :] = as_float(
                gx[s, pl.ds(RT * STRIP + side, STRIP), :]
            ) * column_scale(gx[s, 2 * RT * STRIP :, :], 1)

    @pl.when(t // RT != core)
    def _():
        for s in range(8):
            gbuf[s * STRIP : (s + 1) * STRIP, :] = as_float(
                goth[s, pl.ds(side, STRIP), :]
            ) * column_scale(goth[s, RT * STRIP :, :], 1)

    for a in range(2):

        @pl.when(col == ids[8 + a])
        def _():
            gbuf[0:TILE, :] = diag[a * TILE : (a + 1) * TILE, :]

    right = split(dot3(split(gbuf[0:TILE, :]), (ih[...], il[...])))
    out[...] = front[...] - dot3((lh[...], ll[...]), right)
    each(lambda copy: copy.wait())
    for p in range(RT):
        rows = slice(p * TILE, (p + 1) * TILE)
        for ch in range(2):
            m = ch * RT + p

            @pl.when(there[ch][p] & (js[ch] >= 0))
            def _():
                out[rows, :] += as_float(tiles[m]) * column_scale(codes[ch], m)

    for a in range(2):

        @pl.when(col == ids[8 + a])
        def _():
            out[...] = rows_f[:, a * TILE : (a + 1) * TILE]


def final(ids, where, diag, inv, gx, goth, recv, front):
    def whole(*shape):
        return pl.BlockSpec(shape, lambda i, *s: (0,) * len(shape))

    line = pl.BlockSpec((RT * TILE, TILE), lambda i, *s: (0, i))
    return pl.pallas_call(
        final_kernel,
        grid_spec=pltpu.PrefetchScalarGridSpec(
            num_scalar_prefetch=2,
            grid=(QT,),
            in_specs=[
                whole(PANEL, PANEL),
                whole(PANEL, PANEL),
                whole(8, GROWS, PANEL),
                whole(8, GROWS - RT * STRIP, PANEL),
                pl.BlockSpec(memory_space=pl.ANY),
                line,
            ],
            out_specs=line,
            scratch_shapes=[
                pltpu.VMEM((RT * TILE, PANEL), F32),
                pltpu.VMEM((RT * TILE, PANEL), F32),
                pltpu.VMEM((RT * TILE, PANEL), BF16),
                pltpu.VMEM((RT * TILE, PANEL), BF16),
                pltpu.VMEM((PANEL, PANEL), BF16),
                pltpu.VMEM((PANEL, PANEL), BF16),
                pltpu.VMEM((2 * RT, TILE, TILE), I16),
                pltpu.VMEM((2, CODE, TILE), I16),
                pltpu.SemaphoreType.DMA((2 * RT + 2,)),
            ],
        ),
        out_shape=jax.ShapeDtypeStruct((RT * TILE, QT * TILE), F32),
        compiler_params=pltpu.CompilerParams(vmem_limit_bytes=52 * MIB),
        cost_estimate=pl.CostEstimate(flops=1 << 33, bytes_accessed=20 * MIB, transcendentals=0),
    )(ids, where, diag, inv, gx, goth, recv, front)


def pick(v, at):
    return lax.dynamic_index_in_dim(v, at, 0, keepdims=False)


def fetch_partner(panel, x, core, z, yh):
    halves = panel.reshape(2, 512, 1024)
    piece = pick(halves, ((z - x + 4) % 4) // 2)
    came = []
    for dx in (1, 2, 3):
        pairs = [
            (flat(c, xs, y, (xs + 2 * b) % 4, y), flat(c, (xs + dx) % 4, b, xs, y))
            for c in range(2)
            for xs in range(4)
            for y in range(2)
            for b in range(2)
        ]
        came.append(lax.ppermute(piece, AXES, pairs))
    pairs = [
        (flat(c, x, y, x, y), flat(c, x, 1 - y, x, y))
        for c in range(2)
        for x in range(4)
        for y in range(2)
    ]
    beside = lax.ppermute(pick(halves, 1 - core), AXES, pairs)
    way = (x - z + 4) % 4
    mine = jnp.where(way == 1, came[0], jnp.where(way == 2, came[1], came[2]))
    mine = jnp.where(way == 0, jnp.where(core == yh, pick(halves, core), beside), mine)
    return mine, shift(mine, dk=1)


def sum_first(v, core, z):
    v = v.reshape(2, 256, PANEL)
    v = pick(v, core) + shift(pick(v, 1 - core), dk=1)
    v = v.reshape(4, 64, PANEL)
    got = [shift(pick(v, (z + d) % 4), dz=d) for d in (1, 3, 2)]
    return pick(v, z) + got[0] + got[1] + got[2]


def gathered(v, at, **axis):
    (name,) = axis
    full = jnp.zeros((4,) + v.shape, v.dtype)
    full = lax.dynamic_update_index_in_dim(full, v, at, 0)
    for d in (1, 3, 2):
        full = lax.dynamic_update_index_in_dim(full, shift(v, **{name: d}), (at - d) % 4, 0)
    return full


def sum_second(v, x):
    v = v.reshape(4, 64, PANEL)
    got = [shift(pick(v, (x + d) % 4), dx=d) for d in (1, 3, 2)]
    v = pick(v, x) + got[0] + got[1] + got[2]
    return (v + shift(v, dc=1, dy=1)) + (shift(v, dc=1) + shift(v, dy=1))


def sum_third(v, x, core):
    v = gathered(v, x, dx=0).reshape(256, PANEL)
    other = shift(v, dk=1)
    return jnp.concatenate([jnp.where(core == 0, v, other), jnp.where(core == 0, other, v)])


def tables(child_maps, parent_place):
    hit = child_maps[:, :, None] == jnp.arange(48, dtype=I32)
    slots = jnp.sum(jnp.where(hit, parent_place, 0), axis=2)
    hit = slots[:, :, None] == jnp.arange(48, dtype=I32)
    where = jnp.max(jnp.where(hit, jnp.arange(32, dtype=I32)[None, :, None], -1), axis=1)
    return slots, where


def body(child_blocks, child_panels, child_patterns, child_maps, parent_place, parent_front):
    ch, x, core, z, yh = (lax.axis_index(n).astype(I32) for n in AXES)
    r, c = x * 2 + core, z * 2 + yh
    slots, where = tables(child_maps, parent_place)
    e = parent_place[0], parent_place[1]
    ids = jnp.stack([ch, r, c, ch * 8 + r, core, z, yh, ch * 4 + x, e[0], e[1], x])
    panel = child_panels[0]
    parent_front = pltpu.with_memory_space_constraint(parent_front, pltpu.HBM)
    block = pltpu.with_memory_space_constraint(child_blocks[0], pltpu.HBM)
    mine, theirs = fetch_partner(panel, x, core, z, yh)
    mine, theirs, ids, slots, where = lax.optimization_barrier((mine, theirs, ids, slots, where))
    send, diag, gcol = update(
        ids, slots, child_patterns, block, panel, mine, theirs, parent_front
    )
    own = lax.all_to_all(send, ("child", "x"), split_axis=0, concat_axis=0, tiled=True)

    diag = sum_first(diag, core, z)
    diag, gcol = lax.optimization_barrier((diag, gcol))
    parts = strips(ids, gcol, parent_front)
    parts = [parts[0]] + [shift(parts[d], dz=d) for d in range(1, 4)]
    diag = gathered(diag, z, dz=0).reshape(256, PANEL)
    strip = choose_z(ids, where, parts)
    own, diag, strip = lax.optimization_barrier((own, diag, strip))

    other = shift(own, dk=1)
    send = route(ids, slots, where, own, other)
    kept, moved = pick(strip, yh), pick(strip, 1 - yh)
    moves = [shift(moved, dy=1), shift(kept, dc=1), shift(moved, dc=1, dy=1)]
    strip = choose_y(ids, where, [kept] + moves)
    diag = sum_second(diag, x)
    send, diag, strip = lax.optimization_barrier((send, diag, strip))
    recv = lax.all_to_all(send, ("z", "yh"), split_axis=0, concat_axis=0, tiled=True)

    diag = sum_third(diag, x, core)
    line = jnp.stack([strip] + [shift(strip, dx=d) for d in range(1, 4)])
    inv = inverse_factor(diag)
    gsend = compose(ids, where, line, shift(line, dk=1))
    recv, inv, gsend = lax.optimization_barrier((recv, inv, gsend))
    gx = lax.all_to_all(gsend, ("z", "yh"), split_axis=0, concat_axis=0, tiled=True)
    goth = shift(gx[:, RT * STRIP :], dk=1)
    return final(ids, where, diag, inv, gx, goth, recv, parent_front)


def solution(mesh):
    fine = Mesh(mesh.devices.reshape(SIZES), AXES)
    rows, cols = ("x", "core"), ("z", "yh")
    return jax.shard_map(
        body,
        mesh=fine,
        in_specs=(
            P("child", rows, cols),
            P("child", rows, None),
            P(),
            P(),
            P(),
            P(("child", "x", "core"), cols),
        ),
        out_specs=P(("child", "x", "core"), cols),
        check_vma=False,
    )
```

```python
import jax
import jax.numpy as jnp
from jax import lax
from jax.experimental import pallas as pl
from jax.experimental.pallas import tpu as pltpu
from jax.sharding import Mesh
from jax.sharding import PartitionSpec as P

TILE = 256
PANEL = 512
CODE = 16
CT = 4
RT = 3
QT = 6
STRIP = 32
GROWS = 2 * RT * STRIP + CODE
CROWS = 2 * RT * TILE + CODE
AXES = ("child", "x", "core", "z", "yh")
SIZES = (2, 4, 2, 4, 2)
MIB = 1 << 20
F32 = jnp.float32
I32 = jnp.int32
I16 = jnp.int16
BF16 = jnp.bfloat16
HIGHEST = lax.Precision.HIGHEST


def flat(c, x, k, z, y):
    return (((c * 4 + x) * 2 + k) * 4 + z) * 2 + y


def everyone():
    return [
        (c, x, k, z, y)
        for c in range(2)
        for x in range(4)
        for k in range(2)
        for z in range(4)
        for y in range(2)
    ]


def shift(v, dc=0, dx=0, dk=0, dz=0, dy=0):
    pairs = [
        (flat(c, x, k, z, y), flat(c ^ dc, (x + dx) % 4, k ^ dk, (z + dz) % 4, y ^ dy))
        for c, x, k, z, y in everyone()
    ]
    return lax.ppermute(v, AXES, pairs)


def encode(u):
    top = jnp.max(jnp.abs(u), axis=0, keepdims=True)
    code = jnp.ceil(jnp.log2(jnp.maximum(top, 1e-30)) * 128.0)
    scale = jnp.exp2(15.0 - code * (1.0 / 128.0)) * (32766.0 / 32768.0)
    return jnp.floor(u * scale + 0.5).astype(I32).astype(I16), code


def scale_rows(code):
    return jnp.broadcast_to(code, (CODE, code.shape[1])).astype(I32).astype(I16)


def as_float(q):
    return q.astype(I32).astype(F32)


def column_scale(codes, row=0):
    code = as_float(codes)[row : row + 1, :]
    return jnp.exp2(code * (1.0 / 128.0) - 15.0) * (32768.0 / 32766.0)


def update_kernel(ids, slots, pat, blk, pan, mine, other, front, send, diag, gcol, tile, sem):
    i = pl.program_id(0)
    ch, r, c, g = ids[0], ids[1], ids[2], ids[3]
    e = (ids[8], ids[9])

    @pl.when(i == 0)
    def _():
        diag[...] = jnp.zeros_like(diag)
        for a in range(2):
            for b in range(2):

                @pl.when((e[a] // RT == g) & (e[b] // QT == c))
                def _():
                    rows = pl.multiple_of((e[a] % RT) * TILE, TILE)
                    cols = pl.multiple_of((e[b] % QT) * TILE, TILE)
                    copy = pltpu.make_async_copy(
                        front.at[pl.ds(rows, TILE), pl.ds(cols, TILE)], tile, sem
                    )
                    copy.start()
                    copy.wait()
                    diag[a * TILE : (a + 1) * TILE, b * TILE : (b + 1) * TILE] = tile[...]

    si = slots[ch, r * CT + i]
    for n in range(CT):
        half = mine if n < 2 else other
        j = (ids[4] if n < 2 else 1 - ids[4]) * 2 + n % 2
        cols = pl.ds(pl.multiple_of(j * TILE, TILE), TILE)
        prod = lax.dot_general(
            pan[...],
            half[(n % 2) * TILE : (n % 2 + 1) * TILE, :],
            (((1,), (1,)), ((), ())),
            preferred_element_type=F32,
        )
        u = (blk[:, cols] - prod) * pat[ch, r * CT + i, c * CT + j].astype(F32)
        q, code = encode(u)
        send[0, 0:TILE, cols] = q
        send[0, TILE:, cols] = scale_rows(code)
        sj = slots[ch, c * CT + j]
        for b in range(2):
            at = slice(b * TILE, (b + 1) * TILE)

            @pl.when(sj == e[b])
            def _():
                gcol[:, at] = u
                for a in range(2):

                    @pl.when(si == e[a])
                    def _():
                        diag[a * TILE : (a + 1) * TILE, at] += u


def update(ids, slots, pat, blk, pan, mine, other, front):
    def slot(i, ids, slots, pat):
        return slots[ids[0], ids[1] * CT + i] // QT, 0, 0

    return pl.pallas_call(
        update_kernel,
        grid_spec=pltpu.PrefetchScalarGridSpec(
            num_scalar_prefetch=3,
            grid=(CT,),
            in_specs=[
                pl.BlockSpec((TILE, 1024), lambda i, *s: (i, 0)),
                pl.BlockSpec((TILE, 1024), lambda i, *s: (i, 0)),
                pl.BlockSpec((512, 1024), lambda i, *s: (0, 0)),
                pl.BlockSpec((512, 1024), lambda i, *s: (0, 0)),
                pl.BlockSpec(memory_space=pl.ANY),
            ],
            out_specs=[
                pl.BlockSpec((1, TILE + CODE, 1024), slot),
                pl.BlockSpec((PANEL, PANEL), lambda i, *s: (0, 0)),
                pl.BlockSpec((TILE, PANEL), lambda i, *s: (i, 0)),
            ],
            scratch_shapes=[pltpu.VMEM((TILE, TILE), F32), pltpu.SemaphoreType.DMA],
        ),
        out_shape=[
            pltpu.HBM((8, TILE + CODE, 1024), I16),
            pltpu.HBM((PANEL, PANEL), F32),
            pltpu.HBM((CT * TILE, PANEL), F32),
        ],
        compiler_params=pltpu.CompilerParams(vmem_limit_bytes=40 * MIB),
        cost_estimate=pl.CostEstimate(flops=1 << 31, bytes_accessed=14 * MIB, transcendentals=0),
    )(ids, slots, pat, blk, pan, mine, other, front)


def strips_kernel(ids, gcol, front, *rest):
    outs, (wide, sem) = rest[:4], rest[4:]
    c, z = ids[2], ids[5]
    for a in range(2):
        e = ids[8 + a]

        @pl.when(e // QT == c)
        def _():
            at = pl.multiple_of((e % QT) * TILE, TILE)
            copy = pltpu.make_async_copy(
                front.at[:, pl.ds(at, TILE)], wide.at[:, pl.ds(a * TILE, TILE)], sem
            )
            copy.start()
            copy.wait()

    for d in range(4):
        for f in range(2):
            s = ((z + d) % 4) * 2 + f
            at = 0
            for ref, n in ((gcol, CT), (wide, RT)):
                parts = [
                    ref[pl.ds(pl.multiple_of(p * TILE + s * STRIP, STRIP), STRIP), :]
                    for p in range(n)
                ]
                q, code = encode(jnp.concatenate(parts, 0))
                outs[d][f, at : at + n * STRIP, :] = q
                outs[d][f, at + n * STRIP : at + n * STRIP + CODE, :] = scale_rows(code)
                at += n * STRIP + CODE


def strips(ids, gcol, front):
    return pl.pallas_call(
        strips_kernel,
        grid_spec=pltpu.PrefetchScalarGridSpec(
            num_scalar_prefetch=1,
            grid=(1,),
            in_specs=[
                pl.BlockSpec((CT * TILE, PANEL), lambda i, *s: (0, 0)),
                pl.BlockSpec(memory_space=pl.ANY),
            ],
            out_specs=[pl.BlockSpec((2, TILE, PANEL), lambda i, *s: (0, 0, 0))] * 4,
            scratch_shapes=[pltpu.VMEM((RT * TILE, PANEL), F32), pltpu.SemaphoreType.DMA],
        ),
        out_shape=[jax.ShapeDtypeStruct((2, TILE, PANEL), I16)] * 4,
        compiler_params=pltpu.CompilerParams(vmem_limit_bytes=24 * MIB),
        cost_estimate=pl.CostEstimate(flops=0, bytes_accessed=6 * MIB, transcendentals=0),
    )(ids, gcol, front)


CHILD_CODE = CT * STRIP
FRONT = CHILD_CODE + CODE
FRONT_CODE = FRONT + RT * STRIP


def regions(ids, where, child):
    for a in range(2):
        cols = slice(a * TILE, (a + 1) * TILE)
        yield slice(0, FRONT), cols, where[child, ids[8 + a]] // CT
        yield slice(FRONT, TILE), cols, ids[8 + a] // QT


def choose_z_kernel(ids, where, *refs):
    out, sems = refs[4], refs[5]

    def each(act):
        for n, (rows, cols, holder) in enumerate(regions(ids, where, ids[0])):
            for d in range(4):

                @pl.when(lax.rem(ids[5] - holder // 2 + 4, 4) == d)
                def _():
                    act(
                        pltpu.make_async_copy(
                            refs[d].at[:, rows, cols], out.at[:, rows, cols], sems.at[n]
                        )
                    )

    each(lambda copy: copy.start())
    each(lambda copy: copy.wait())


def choose_z(ids, where, parts):
    return pl.pallas_call(
        choose_z_kernel,
        grid_spec=pltpu.PrefetchScalarGridSpec(
            num_scalar_prefetch=2,
            grid=(1,),
            in_specs=[pl.BlockSpec(memory_space=pl.ANY)] * 4,
            out_specs=pl.BlockSpec((2, TILE, PANEL), lambda i, *s: (0, 0, 0)),
            scratch_shapes=[pltpu.SemaphoreType.DMA((4,))],
        ),
        out_shape=jax.ShapeDtypeStruct((2, TILE, PANEL), I16),
        cost_estimate=pl.CostEstimate(flops=0, bytes_accessed=MIB, transcendentals=0),
    )(ids, where, *parts)


def choose_y_kernel(ids, where, kept, beside, across, both, out, sems):
    def each(act):
        for n, (near, far) in enumerate(((kept, beside), (across, both))):
            child = lax.rem(ids[0] + n, 2)
            for m, (rows, cols, holder) in enumerate(regions(ids, where, child)):
                here = lax.rem(holder + 8, 2) == ids[6]
                for side, ref in ((True, near), (False, far)):

                    @pl.when(here == side)
                    def _():
                        act(
                            pltpu.make_async_copy(
                                ref.at[rows, cols], out.at[n, rows, cols], sems.at[n * 4 + m]
                            )
                        )

    each(lambda copy: copy.start())
    each(lambda copy: copy.wait())


def choose_y(ids, where, parts):
    return pl.pallas_call(
        choose_y_kernel,
        grid_spec=pltpu.PrefetchScalarGridSpec(
            num_scalar_prefetch=2,
            grid=(1,),
            in_specs=[pl.BlockSpec(memory_space=pl.ANY)] * 4,
            out_specs=pl.BlockSpec((2, TILE, PANEL), lambda i, *s: (0, 0, 0)),
            scratch_shapes=[pltpu.SemaphoreType.DMA((8,))],
        ),
        out_shape=jax.ShapeDtypeStruct((2, TILE, PANEL), I16),
        cost_estimate=pl.CostEstimate(flops=0, bytes_accessed=MIB, transcendentals=0),
    )(ids, where, *parts)


def compose_kernel(ids, where, own, other, out, acc, kept, kcode):
    q = pl.program_id(0)
    ch, core, k, x = ids[0], ids[4], ids[7], ids[10]
    half = lax.broadcasted_iota(I32, (STRIP, PANEL), 1) < TILE

    def group(q):
        first = q * QT + core * RT
        d, f = lax.rem(x - q % 4 + 4, 4), lax.rem(ch + q // 4, 2)
        acc[...] = as_float(own[d, f, FRONT:FRONT_CODE, :]) * column_scale(
            own[d, f, FRONT_CODE:, :]
        )
        for m in range(2):
            known = [(where[m, ids[8 + a]] >= 0).astype(I32) for a in range(2)]
            mask = jnp.where(half, known[0], known[1]) > 0
            for p in range(RT):
                i = where[m, first + p]
                for here, ref in ((True, own), (False, other)):

                    @pl.when((i >= 0) & (((i // CT) % 2 == core) == here))
                    def _():
                        dm, fm = lax.rem(x - i // 8 + 4, 4), lax.rem(ch + m, 2)
                        row = pl.multiple_of((i % CT) * STRIP, STRIP)
                        v = as_float(ref[dm, fm, pl.ds(row, STRIP), :]) * column_scale(
                            ref[dm, fm, CHILD_CODE:FRONT, :]
                        )
                        acc[p * STRIP : (p + 1) * STRIP, :] += jnp.where(mask, v, 0.0)

        return encode(acc[...])

    @pl.when(q == 0)
    def _():
        v, code = group(k)
        kept[...] = v
        kcode[...] = jnp.broadcast_to(code, kcode.shape)

    v, code = group(q)
    out[0, 0 : RT * STRIP, :] = kept[...]
    out[0, RT * STRIP : 2 * RT * STRIP, :] = v
    row = lax.broadcasted_iota(I32, (CODE, PANEL), 0)
    both = jnp.where(row == 0, kcode[0:1, :], code)
    out[0, 2 * RT * STRIP :, :] = both.astype(I32).astype(I16)


def compose(ids, where, own, other):
    whole = pl.BlockSpec((4, 2, TILE, PANEL), lambda i, *s: (0, 0, 0, 0))
    return pl.pallas_call(
        compose_kernel,
        grid_spec=pltpu.PrefetchScalarGridSpec(
            num_scalar_prefetch=2,
            grid=(8,),
            in_specs=[whole] * 2,
            out_specs=pl.BlockSpec((1, GROWS, PANEL), lambda i, *s: (i, 0, 0)),
            scratch_shapes=[
                pltpu.VMEM((RT * STRIP, PANEL), F32),
                pltpu.VMEM((RT * STRIP, PANEL), I16),
                pltpu.VMEM((8, PANEL), F32),
            ],
        ),
        out_shape=jax.ShapeDtypeStruct((8, GROWS, PANEL), I16),
        compiler_params=pltpu.CompilerParams(vmem_limit_bytes=24 * MIB),
        cost_estimate=pl.CostEstimate(flops=0, bytes_accessed=6 * MIB, transcendentals=0),
    )(ids, where, own, other)


def route_kernel(ids, slots, where, own, other, send, lines, codes, isem, osem, csem):
    c, g, core = ids[2], ids[3], ids[4]
    rows = [where[ch, g * RT + p] for ch in range(2) for p in range(RT)]
    to = [[slots[ch, c * CT + j] // QT for j in range(CT)] for ch in range(2)]

    def come(m, act):
        i = rows[m]
        src = (m // RT) * 4 + i // 8
        for here, buf in ((True, own), (False, other)):

            @pl.when((i >= 0) & (((i // CT) % 2 == core) == here))
            def _():
                act(pltpu.make_async_copy(buf.at[src], lines.at[m], isem.at[m]))

    def leave(m, act):
        @pl.when(rows[m] >= 0)
        def _():
            for j in range(CT):
                act(
                    pltpu.make_async_copy(
                        lines.at[m, pl.ds(0, TILE), pl.ds(j * TILE, TILE)],
                        send.at[to[m // RT][j], pl.ds(m * TILE, TILE), :],
                        osem.at[m * CT + j],
                    )
                )

    for m in range(2 * RT):
        come(m, lambda copy: copy.start())
    for m in range(2 * RT):
        come(m, lambda copy: copy.wait())
        leave(m, lambda copy: copy.start())
    line = lax.broadcasted_iota(I32, (CODE, TILE), 0)
    codes[...] = jnp.zeros_like(codes)
    for ch in range(2):
        for j in range(CT):
            q = to[ch][j]
            v = codes[q].astype(I32)
            for p in range(RT):
                m = ch * RT + p
                mine = lines[m, TILE:, j * TILE : (j + 1) * TILE].astype(I32)
                v = jnp.where(line == m, mine, v)
            codes[q] = v.astype(I16)
    tails = [
        pltpu.make_async_copy(codes.at[q], send.at[q, pl.ds(2 * RT * TILE, CODE), :], csem.at[q])
        for q in range(8)
    ]
    for copy in tails:
        copy.start()
    for m in range(2 * RT):
        leave(m, lambda copy: copy.wait())
    for copy in tails:
        copy.wait()


def route(ids, slots, where, own, other):
    return pl.pallas_call(
        route_kernel,
        grid_spec=pltpu.PrefetchScalarGridSpec(
            num_scalar_prefetch=3,
            grid=(1,),
            in_specs=[pl.BlockSpec(memory_space=pl.ANY)] * 2,
            out_specs=pl.BlockSpec(memory_space=pl.ANY),
            scratch_shapes=[
                pltpu.VMEM((2 * RT, TILE + CODE, 1024), I16),
                pltpu.VMEM((8, CODE, TILE), I16),
                pltpu.SemaphoreType.DMA((2 * RT,)),
                pltpu.SemaphoreType.DMA((2 * RT * CT,)),
                pltpu.SemaphoreType.DMA((8,)),
            ],
        ),
        out_shape=pltpu.HBM((8, CROWS, TILE), I16),
        compiler_params=pltpu.CompilerParams(vmem_limit_bytes=32 * MIB),
        cost_estimate=pl.CostEstimate(flops=0, bytes_accessed=8 * MIB, transcendentals=0),
    )(ids, slots, where, own, other)


def nt(a, b):
    return lax.dot_general(
        a, b, (((1,), (1,)), ((), ())), precision=HIGHEST, preferred_element_type=F32
    )


def nn(a, b):
    return lax.dot_general(
        a, b, (((1,), (0,)), ((), ())), precision=HIGHEST, preferred_element_type=F32
    )


NB = 64
WAYS = 8


def inverse_kernel(a_ref, out, w, f):
    n = PANEL // NB
    out[...] = jnp.zeros_like(out)
    row = lax.broadcasted_iota(I32, (NB, NB), 0)
    col = lax.broadcasted_iota(I32, (NB, NB), 1)
    eye = row == col
    lanes = lax.broadcasted_iota(I32, (1, 2 * NB), 1)
    sub = lax.broadcasted_iota(I32, (NB, 1), 0)

    def blk(i):
        return slice(i * NB, (i + 1) * NB)

    f[...] = a_ref[...]
    for k in range(n):
        w[:, :NB] = f[blk(k), blk(k)]
        w[:, NB:] = jnp.where(eye, 1.0, 0.0).astype(F32)

        def step(n4, _):
            j = n4 * WAYS
            lines = [w[pl.ds(j + a, 1), :] for a in range(WAYS)]
            square = w[:, :NB]
            columns = [
                jnp.sum(jnp.where(col == j + a, square, 0.0), axis=1, keepdims=True)
                for a in range(WAYS)
            ]
            small = [
                [
                    jnp.sum(jnp.where(lanes == j + b, lines[a], 0.0), axis=1, keepdims=True)
                    if b >= a
                    else None
                    for b in range(WAYS)
                ]
                for a in range(WAYS)
            ]
            factors = []
            for a in range(WAYS):
                inverse = 1.0 / small[a][a]
                for b in range(a + 1, WAYS):
                    times = small[a][b] * inverse
                    for d in range(b, WAYS):
                        small[b][d] = small[b][d] - times * small[a][d]
                    lines[b] = lines[b] - times * lines[a]
                    columns[b] = columns[b] - times * columns[a]
                factors.append(jnp.where(sub >= j + WAYS, columns[a] * inverse, 0.0))
            total = w[...]
            for a in range(WAYS):
                total = total - factors[a] * lines[a]
            w[...] = total
            for a in range(1, WAYS):
                w[pl.ds(j + a, 1), :] = lines[a]
            return 0

        lax.fori_loop(0, NB // WAYS, step, 0)
        d = jnp.sum(jnp.where(eye, w[:, :NB], 0.0), axis=1, keepdims=True)
        inv = w[:, NB:] * (1.0 / jnp.sqrt(d))
        out[blk(k), blk(k)] = inv
        rest = (k + 1) * NB
        if rest < PANEL:
            below = nt(f[rest:, blk(k)], inv)
            f[rest:, blk(k)] = below
            f[rest:, rest:] = f[rest:, rest:] - nt(below, below)
    for k in range(1, n):
        acc = nn(f[blk(k), : k * NB], out[: k * NB, : k * NB])
        out[blk(k), : k * NB] = -nn(out[blk(k), blk(k)], acc)


def inverse_factor(a):
    return pl.pallas_call(
        inverse_kernel,
        out_shape=jax.ShapeDtypeStruct((PANEL, PANEL), F32),
        scratch_shapes=[pltpu.VMEM((NB, 2 * NB), F32), pltpu.VMEM((PANEL, PANEL), F32)],
        compiler_params=pltpu.CompilerParams(vmem_limit_bytes=24 * MIB),
        cost_estimate=pl.CostEstimate(flops=1 << 34, bytes_accessed=2 * MIB, transcendentals=0),
    )(a)


def split(v):
    hi = v.astype(BF16)
    return hi, (v - hi.astype(F32)).astype(BF16)


def dot3(a, b):
    def one(x, y):
        return lax.dot_general(x, y, (((1,), (1,)), ((), ())), preferred_element_type=F32)

    return one(a[0], b[0]) + (one(a[0], b[1]) + one(a[1], b[0]))


def base_kernel(ids, where, recv, front, out, tiles, codes, tsem):
    t = pl.program_id(0)
    c, g = ids[2], ids[3]
    col = c * QT + t
    js = [where[ch, col] for ch in range(2)]
    there = [[where[ch, g * RT + p] >= 0 for p in range(RT)] for ch in range(2)]

    def each(act):
        for ch in range(2):
            src = js[ch] // CT

            @pl.when(js[ch] >= 0)
            def _():
                act(
                    pltpu.make_async_copy(
                        recv.at[src, pl.ds(2 * RT * TILE, CODE), :],
                        codes.at[ch],
                        tsem.at[2 * RT + ch],
                    )
                )

            for p in range(RT):
                m = ch * RT + p

                @pl.when(there[ch][p] & (js[ch] >= 0))
                def _():
                    act(
                        pltpu.make_async_copy(
                            recv.at[src, pl.ds(m * TILE, TILE), :], tiles.at[m], tsem.at[m]
                        )
                    )

    each(lambda copy: copy.start())

    out[...] = front[...]
    each(lambda copy: copy.wait())
    for p in range(RT):
        rows = slice(p * TILE, (p + 1) * TILE)
        for ch in range(2):
            m = ch * RT + p

            @pl.when(there[ch][p] & (js[ch] >= 0))
            def _():
                out[rows, :] += as_float(tiles[m]) * column_scale(codes[ch], m)


def base(ids, where, recv, front):
    line = pl.BlockSpec((RT * TILE, TILE), lambda i, *s: (0, i))
    return pl.pallas_call(
        base_kernel,
        grid_spec=pltpu.PrefetchScalarGridSpec(
            num_scalar_prefetch=2,
            grid=(QT,),
            in_specs=[pl.BlockSpec(memory_space=pl.ANY), line],
            out_specs=line,
            scratch_shapes=[
                pltpu.VMEM((2 * RT, TILE, TILE), I16),
                pltpu.VMEM((2, CODE, TILE), I16),
                pltpu.SemaphoreType.DMA((2 * RT + 2,)),
            ],
        ),
        out_shape=jax.ShapeDtypeStruct((RT * TILE, QT * TILE), F32),
        compiler_params=pltpu.CompilerParams(vmem_limit_bytes=24 * MIB),
        cost_estimate=pl.CostEstimate(flops=0, bytes_accessed=20 * MIB, transcendentals=0),
    )(ids, where, recv, front)


def final_kernel(
    ids, diag, inv, gx, goth, front, out,
    gbuf, rows_f, lh, ll, ih, il,
):
    t = pl.program_id(0)
    c, g, core = ids[2], ids[3], ids[4]
    col = c * QT + t
    @pl.when(t == 0)
    def _():
        hi, lo = split(inv[...])
        ih[...] = hi
        il[...] = lo
        for s in range(8):
            scale = column_scale(gx[s, 2 * RT * STRIP :, :], 0)
            v = as_float(gx[s, 0 : RT * STRIP, :]) * scale
            for p in range(RT):
                gbuf[p * TILE + s * STRIP : p * TILE + (s + 1) * STRIP, :] = v[
                    p * STRIP : (p + 1) * STRIP, :
                ]
        for p in range(RT):
            for a in range(2):

                @pl.when(g * RT + p == ids[8 + a])
                def _():
                    gbuf[p * TILE : (p + 1) * TILE, :] = diag[a * TILE : (a + 1) * TILE, :]

        v = dot3(split(gbuf[...]), (ih[...], il[...]))
        rows_f[...] = v
        hi, lo = split(v)
        lh[...] = hi
        ll[...] = lo

    side = pl.multiple_of((t % RT) * STRIP, STRIP)

    @pl.when(t // RT == core)
    def _():
        for s in range(8):
            gbuf[s * STRIP : (s + 1) * STRIP, :] = as_float(
                gx[s, pl.ds(RT * STRIP + side, STRIP), :]
            ) * column_scale(gx[s, 2 * RT * STRIP :, :], 1)

    @pl.when(t // RT != core)
    def _():
        for s in range(8):
            gbuf[s * STRIP : (s + 1) * STRIP, :] = as_float(
                goth[s, pl.ds(side, STRIP), :]
            ) * column_scale(goth[s, RT * STRIP :, :], 1)

    for a in range(2):

        @pl.when(col == ids[8 + a])
        def _():
            gbuf[0:TILE, :] = diag[a * TILE : (a + 1) * TILE, :]

    right = split(dot3(split(gbuf[0:TILE, :]), (ih[...], il[...])))
    out[...] = front[...] - dot3((lh[...], ll[...]), right)
    for a in range(2):

        @pl.when(col == ids[8 + a])
        def _():
            out[...] = rows_f[:, a * TILE : (a + 1) * TILE]


def final(ids, diag, inv, gx, goth, front):
    def whole(*shape):
        return pl.BlockSpec(shape, lambda i, *s: (0,) * len(shape))

    line = pl.BlockSpec((RT * TILE, TILE), lambda i, *s: (0, i))
    return pl.pallas_call(
        final_kernel,
        grid_spec=pltpu.PrefetchScalarGridSpec(
            num_scalar_prefetch=1,
            grid=(QT,),
            in_specs=[
                whole(PANEL, PANEL),
                whole(PANEL, PANEL),
                whole(8, GROWS, PANEL),
                whole(8, GROWS - RT * STRIP, PANEL),
                line,
            ],
            out_specs=line,
            scratch_shapes=[
                pltpu.VMEM((RT * TILE, PANEL), F32),
                pltpu.VMEM((RT * TILE, PANEL), F32),
                pltpu.VMEM((RT * TILE, PANEL), BF16),
                pltpu.VMEM((RT * TILE, PANEL), BF16),
                pltpu.VMEM((PANEL, PANEL), BF16),
                pltpu.VMEM((PANEL, PANEL), BF16),
            ],
        ),
        out_shape=jax.ShapeDtypeStruct((RT * TILE, QT * TILE), F32),
        compiler_params=pltpu.CompilerParams(vmem_limit_bytes=52 * MIB),
        cost_estimate=pl.CostEstimate(flops=1 << 33, bytes_accessed=20 * MIB, transcendentals=0),
    )(ids, diag, inv, gx, goth, front)


def pick(v, at):
    return lax.dynamic_index_in_dim(v, at, 0, keepdims=False)


def fetch_partner(panel, x, core, z, yh):
    halves = panel.reshape(2, 512, 1024)
    piece = pick(halves, ((z - x + 4) % 4) // 2)
    came = []
    for dx in (1, 2, 3):
        pairs = [
            (flat(c, xs, y, (xs + 2 * b) % 4, y), flat(c, (xs + dx) % 4, b, xs, y))
            for c in range(2)
            for xs in range(4)
            for y in range(2)
            for b in range(2)
        ]
        came.append(lax.ppermute(piece, AXES, pairs))
    pairs = [
        (flat(c, x, y, x, y), flat(c, x, 1 - y, x, y))
        for c in range(2)
        for x in range(4)
        for y in range(2)
    ]
    beside = lax.ppermute(pick(halves, 1 - core), AXES, pairs)
    way = (x - z + 4) % 4
    mine = jnp.where(way == 1, came[0], jnp.where(way == 2, came[1], came[2]))
    mine = jnp.where(way == 0, jnp.where(core == yh, pick(halves, core), beside), mine)
    return mine, shift(mine, dk=1)


def sum_first(v, core, z):
    v = v.reshape(2, 256, PANEL)
    v = pick(v, core) + shift(pick(v, 1 - core), dk=1)
    v = v.reshape(4, 64, PANEL)
    got = [shift(pick(v, (z + d) % 4), dz=d) for d in (1, 3, 2)]
    return pick(v, z) + got[0] + got[1] + got[2]


def gathered(v, at, **axis):
    (name,) = axis
    full = jnp.zeros((4,) + v.shape, v.dtype)
    full = lax.dynamic_update_index_in_dim(full, v, at, 0)
    for d in (1, 3, 2):
        full = lax.dynamic_update_index_in_dim(full, shift(v, **{name: d}), (at - d) % 4, 0)
    return full


def sum_x(v, x):
    v = v.reshape(4, 64, PANEL)
    got = [shift(pick(v, (x + d) % 4), dx=d) for d in (1, 3, 2)]
    return pick(v, x) + got[0] + got[1] + got[2]


def sum_y(v):
    return (v + shift(v, dc=1, dy=1)) + (shift(v, dc=1) + shift(v, dy=1))


def sum_third(v, x, core):
    v = gathered(v, x, dx=0).reshape(256, PANEL)
    other = shift(v, dk=1)
    return jnp.concatenate([jnp.where(core == 0, v, other), jnp.where(core == 0, other, v)])


def tables(child_maps, parent_place):
    hit = child_maps[:, :, None] == jnp.arange(48, dtype=I32)
    slots = jnp.sum(jnp.where(hit, parent_place, 0), axis=2)
    hit = slots[:, :, None] == jnp.arange(48, dtype=I32)
    where = jnp.max(jnp.where(hit, jnp.arange(32, dtype=I32)[None, :, None], -1), axis=1)
    return slots, where


def body(child_blocks, child_panels, child_patterns, child_maps, parent_place, parent_front):
    ch, x, core, z, yh = (lax.axis_index(n).astype(I32) for n in AXES)
    r, c = x * 2 + core, z * 2 + yh
    slots, where = tables(child_maps, parent_place)
    e = parent_place[0], parent_place[1]
    ids = jnp.stack([ch, r, c, ch * 8 + r, core, z, yh, ch * 4 + x, e[0], e[1], x])
    panel = child_panels[0]
    parent_front = pltpu.with_memory_space_constraint(parent_front, pltpu.HBM)
    block = pltpu.with_memory_space_constraint(child_blocks[0], pltpu.HBM)
    mine, theirs = fetch_partner(panel, x, core, z, yh)
    mine, theirs, ids, slots, where = lax.optimization_barrier((mine, theirs, ids, slots, where))
    send, diag, gcol = update(
        ids, slots, child_patterns, block, panel, mine, theirs, parent_front
    )
    own = lax.all_to_all(send, ("child", "x"), split_axis=0, concat_axis=0, tiled=True)

    diag = sum_first(diag, core, z)
    diag, gcol = lax.optimization_barrier((diag, gcol))
    parts = strips(ids, gcol, parent_front)
    parts = [parts[0]] + [shift(parts[d], dz=d) for d in range(1, 4)]
    diag = sum_x(gathered(diag, z, dz=0).reshape(256, PANEL), x)
    strip = choose_z(ids, where, parts)
    own, diag, strip = lax.optimization_barrier((own, diag, strip))

    other = shift(own, dk=1)
    send = route(ids, slots, where, own, other)
    kept, moved = pick(strip, yh), pick(strip, 1 - yh)
    moves = [shift(moved, dy=1), shift(kept, dc=1), shift(moved, dc=1, dy=1)]
    strip = choose_y(ids, where, [kept] + moves)
    diag = sum_y(diag)
    send, diag, strip = lax.optimization_barrier((send, diag, strip))
    recv = lax.all_to_all(send, ("z", "yh"), split_axis=0, concat_axis=0, tiled=True)

    diag = sum_third(diag, x, core)
    line = jnp.stack([strip] + [shift(strip, dx=d) for d in range(1, 4)])
    inv = inverse_factor(diag)
    gsend = compose(ids, where, line, shift(line, dk=1))
    recv, inv, gsend = lax.optimization_barrier((recv, inv, gsend))
    gx = lax.all_to_all(gsend, ("z", "yh"), split_axis=0, concat_axis=0, tiled=True)
    with_children = base(ids, where, recv, parent_front)
    gx, with_children = lax.optimization_barrier((gx, with_children))
    goth = shift(gx[:, RT * STRIP :], dk=1)
    return final(ids, diag, inv, gx, goth, with_children)


def solution(mesh):
    fine = Mesh(mesh.devices.reshape(SIZES), AXES)
    rows, cols = ("x", "core"), ("z", "yh")
    return jax.shard_map(
        body,
        mesh=fine,
        in_specs=(
            P("child", rows, cols),
            P("child", rows, None),
            P(),
            P(),
            P(),
            P(("child", "x", "core"), cols),
        ),
        out_specs=P(("child", "x", "core"), cols),
        check_vma=False,
    )
```

```python
import jax
import jax.numpy as jnp
from jax import lax
from jax.experimental import pallas as pl
from jax.experimental.pallas import tpu as pltpu
from jax.sharding import Mesh
from jax.sharding import PartitionSpec as P

TILE = 256
PANEL = 512
CODE = 16
CT = 4
RT = 3
QT = 6
STRIP = 32
GROWS = 2 * RT * STRIP + CODE
CROWS = 2 * RT * TILE + CODE
AXES = ("child", "x", "core", "z", "yh")
SIZES = (2, 4, 2, 4, 2)
MIB = 1 << 20
F32 = jnp.float32
I32 = jnp.int32
I16 = jnp.int16
BF16 = jnp.bfloat16
HIGHEST = lax.Precision.HIGHEST


def flat(c, x, k, z, y):
    return (((c * 4 + x) * 2 + k) * 4 + z) * 2 + y


def everyone():
    return [
        (c, x, k, z, y)
        for c in range(2)
        for x in range(4)
        for k in range(2)
        for z in range(4)
        for y in range(2)
    ]


def shift(v, dc=0, dx=0, dk=0, dz=0, dy=0):
    pairs = [
        (flat(c, x, k, z, y), flat(c ^ dc, (x + dx) % 4, k ^ dk, (z + dz) % 4, y ^ dy))
        for c, x, k, z, y in everyone()
    ]
    return lax.ppermute(v, AXES, pairs)


def encode(u):
    top = jnp.max(jnp.abs(u), axis=0, keepdims=True)
    code = jnp.ceil(jnp.log2(jnp.maximum(top, 1e-30)) * 128.0)
    scale = jnp.exp2(15.0 - code * (1.0 / 128.0)) * (32766.0 / 32768.0)
    return jnp.floor(u * scale + 0.5).astype(I32).astype(I16), code


def scale_rows(code):
    return jnp.broadcast_to(code, (CODE, code.shape[1])).astype(I32).astype(I16)


def as_float(q):
    return q.astype(I32).astype(F32)


def column_scale(codes, row=0):
    code = as_float(codes)[row : row + 1, :]
    return jnp.exp2(code * (1.0 / 128.0) - 15.0) * (32768.0 / 32766.0)


def update_kernel(
    ids, slots, pat, blk, pan, par, front, send, diag, gcol, tile, sem, lines, lsem
):
    n = pl.program_id(0)
    ch, r, c, g = ids[0], ids[1], ids[2], ids[3]
    e = (ids[8], ids[9])
    j = lax.rem(ids[4] * 2 + n, CT)
    turn = n % 2
    si = [slots[ch, r * CT + i] for i in range(CT)]
    sj = slots[ch, c * CT + j]

    def leave(turn, j, act):
        for i in range(CT):
            act(
                pltpu.make_async_copy(
                    lines.at[turn, i],
                    send.at[si[i] // QT, :, pl.ds(pl.multiple_of(j * TILE, TILE), TILE)],
                    lsem.at[turn, i],
                )
            )

    @pl.when(n == 0)
    def _():
        diag[...] = jnp.zeros_like(diag)
        for a in range(2):
            for b in range(2):

                @pl.when((e[a] // RT == g) & (e[b] // QT == c))
                def _():
                    rows = pl.multiple_of((e[a] % RT) * TILE, TILE)
                    cols = pl.multiple_of((e[b] % QT) * TILE, TILE)
                    copy = pltpu.make_async_copy(
                        front.at[pl.ds(rows, TILE), pl.ds(cols, TILE)], tile, sem
                    )
                    copy.start()
                    copy.wait()
                    diag[a * TILE : (a + 1) * TILE, b * TILE : (b + 1) * TILE] = tile[...]

    @pl.when(n >= 2)
    def _():
        leave(turn, lax.rem(ids[4] * 2 + n - 2, CT), lambda copy: copy.wait())

    prod = lax.dot_general(
        pan[...], par[0], (((1,), (1,)), ((), ())), preferred_element_type=F32
    )
    for i in range(CT):
        rows = slice(i * TILE, (i + 1) * TILE)
        u = (blk[rows, :] - prod[rows, :]) * pat[ch, r * CT + i, c * CT + j].astype(F32)
        q, code = encode(u)
        lines[turn, i, 0:TILE, :] = q
        lines[turn, i, TILE:, :] = scale_rows(code)
        for b in range(2):
            at = slice(b * TILE, (b + 1) * TILE)

            @pl.when(sj == e[b])
            def _():
                gcol[rows, at] = u
                for a in range(2):

                    @pl.when(si[i] == e[a])
                    def _():
                        diag[a * TILE : (a + 1) * TILE, at] += u

    leave(turn, j, lambda copy: copy.start())

    @pl.when(n == CT - 1)
    def _():
        leave(1 - turn, lax.rem(ids[4] * 2 + n - 1, CT), lambda copy: copy.wait())
        leave(turn, j, lambda copy: copy.wait())


def update(ids, slots, pat, blk, pan, par, front):
    def column(n, ids, slots, pat):
        return 0, lax.rem(ids[4] * 2 + n, CT)

    return pl.pallas_call(
        update_kernel,
        grid_spec=pltpu.PrefetchScalarGridSpec(
            num_scalar_prefetch=3,
            grid=(CT,),
            in_specs=[
                pl.BlockSpec((1024, TILE), column),
                pl.BlockSpec((1024, 1024), lambda n, *s: (0, 0)),
                pl.BlockSpec((1, TILE, 1024), lambda n, *s: (n, 0, 0)),
                pl.BlockSpec(memory_space=pl.ANY),
            ],
            out_specs=[
                pl.BlockSpec(memory_space=pl.ANY),
                pl.BlockSpec((PANEL, PANEL), lambda n, *s: (0, 0)),
                pl.BlockSpec((CT * TILE, PANEL), lambda n, *s: (0, 0)),
            ],
            scratch_shapes=[
                pltpu.VMEM((TILE, TILE), F32),
                pltpu.SemaphoreType.DMA,
                pltpu.VMEM((2, CT, TILE + CODE, TILE), I16),
                pltpu.SemaphoreType.DMA((2, CT)),
            ],
        ),
        out_shape=[
            pltpu.HBM((8, TILE + CODE, 1024), I16),
            pltpu.HBM((PANEL, PANEL), F32),
            pltpu.HBM((CT * TILE, PANEL), F32),
        ],
        compiler_params=pltpu.CompilerParams(vmem_limit_bytes=48 * MIB),
        cost_estimate=pl.CostEstimate(flops=1 << 31, bytes_accessed=14 * MIB, transcendentals=0),
    )(ids, slots, pat, blk, pan, par, front)


def strips_kernel(ids, gcol, front, *rest):
    outs, (wide, sem) = rest[:4], rest[4:]
    c, z = ids[2], ids[5]
    for a in range(2):
        e = ids[8 + a]

        @pl.when(e // QT == c)
        def _():
            at = pl.multiple_of((e % QT) * TILE, TILE)
            copy = pltpu.make_async_copy(
                front.at[:, pl.ds(at, TILE)], wide.at[:, pl.ds(a * TILE, TILE)], sem
            )
            copy.start()
            copy.wait()

    for d in range(4):
        for f in range(2):
            s = ((z + d) % 4) * 2 + f
            at = 0
            for ref, n in ((gcol, CT), (wide, RT)):
                parts = [
                    ref[pl.ds(pl.multiple_of(p * TILE + s * STRIP, STRIP), STRIP), :]
                    for p in range(n)
                ]
                q, code = encode(jnp.concatenate(parts, 0))
                outs[d][f, at : at + n * STRIP, :] = q
                outs[d][f, at + n * STRIP : at + n * STRIP + CODE, :] = scale_rows(code)
                at += n * STRIP + CODE


def strips(ids, gcol, front):
    return pl.pallas_call(
        strips_kernel,
        grid_spec=pltpu.PrefetchScalarGridSpec(
            num_scalar_prefetch=1,
            grid=(1,),
            in_specs=[
                pl.BlockSpec((CT * TILE, PANEL), lambda i, *s: (0, 0)),
                pl.BlockSpec(memory_space=pl.ANY),
            ],
            out_specs=[pl.BlockSpec((2, TILE, PANEL), lambda i, *s: (0, 0, 0))] * 4,
            scratch_shapes=[pltpu.VMEM((RT * TILE, PANEL), F32), pltpu.SemaphoreType.DMA],
        ),
        out_shape=[jax.ShapeDtypeStruct((2, TILE, PANEL), I16)] * 4,
        compiler_params=pltpu.CompilerParams(vmem_limit_bytes=24 * MIB),
        cost_estimate=pl.CostEstimate(flops=0, bytes_accessed=6 * MIB, transcendentals=0),
    )(ids, gcol, front)


CHILD_CODE = CT * STRIP
FRONT = CHILD_CODE + CODE
FRONT_CODE = FRONT + RT * STRIP


def regions(ids, where, child):
    for a in range(2):
        cols = slice(a * TILE, (a + 1) * TILE)
        yield slice(0, FRONT), cols, where[child, ids[8 + a]] // CT
        yield slice(FRONT, TILE), cols, ids[8 + a] // QT


def choose_z_kernel(ids, where, *refs):
    out, sems = refs[4], refs[5]

    def each(act):
        for n, (rows, cols, holder) in enumerate(regions(ids, where, ids[0])):
            for d in range(4):

                @pl.when(lax.rem(ids[5] - holder // 2 + 4, 4) == d)
                def _():
                    act(
                        pltpu.make_async_copy(
                            refs[d].at[:, rows, cols], out.at[:, rows, cols], sems.at[n]
                        )
                    )

    each(lambda copy: copy.start())
    each(lambda copy: copy.wait())


def choose_z(ids, where, parts):
    return pl.pallas_call(
        choose_z_kernel,
        grid_spec=pltpu.PrefetchScalarGridSpec(
            num_scalar_prefetch=2,
            grid=(1,),
            in_specs=[pl.BlockSpec(memory_space=pl.ANY)] * 4,
            out_specs=pl.BlockSpec((2, TILE, PANEL), lambda i, *s: (0, 0, 0)),
            scratch_shapes=[pltpu.SemaphoreType.DMA((4,))],
        ),
        out_shape=jax.ShapeDtypeStruct((2, TILE, PANEL), I16),
        cost_estimate=pl.CostEstimate(flops=0, bytes_accessed=MIB, transcendentals=0),
    )(ids, where, *parts)


def choose_y_kernel(ids, where, kept, beside, across, both, out, sems):
    def each(act):
        for n, (near, far) in enumerate(((kept, beside), (across, both))):
            child = lax.rem(ids[0] + n, 2)
            for m, (rows, cols, holder) in enumerate(regions(ids, where, child)):
                here = lax.rem(holder + 8, 2) == ids[6]
                for side, ref in ((True, near), (False, far)):

                    @pl.when(here == side)
                    def _():
                        act(
                            pltpu.make_async_copy(
                                ref.at[rows, cols], out.at[n, rows, cols], sems.at[n * 4 + m]
                            )
                        )

    each(lambda copy: copy.start())
    each(lambda copy: copy.wait())


def choose_y(ids, where, parts):
    return pl.pallas_call(
        choose_y_kernel,
        grid_spec=pltpu.PrefetchScalarGridSpec(
            num_scalar_prefetch=2,
            grid=(1,),
            in_specs=[pl.BlockSpec(memory_space=pl.ANY)] * 4,
            out_specs=pl.BlockSpec((2, TILE, PANEL), lambda i, *s: (0, 0, 0)),
            scratch_shapes=[pltpu.SemaphoreType.DMA((8,))],
        ),
        out_shape=jax.ShapeDtypeStruct((2, TILE, PANEL), I16),
        cost_estimate=pl.CostEstimate(flops=0, bytes_accessed=MIB, transcendentals=0),
    )(ids, where, *parts)


def compose_kernel(ids, where, own, other, out, acc, kept, kcode):
    q = pl.program_id(0)
    ch, core, k, x = ids[0], ids[4], ids[7], ids[10]
    half = lax.broadcasted_iota(I32, (STRIP, PANEL), 1) < TILE

    def group(q):
        first = q * QT + core * RT
        d, f = lax.rem(x - q % 4 + 4, 4), lax.rem(ch + q // 4, 2)
        acc[...] = as_float(own[d, f, FRONT:FRONT_CODE, :]) * column_scale(
            own[d, f, FRONT_CODE:, :]
        )
        for m in range(2):
            known = [(where[m, ids[8 + a]] >= 0).astype(I32) for a in range(2)]
            mask = jnp.where(half, known[0], known[1]) > 0
            for p in range(RT):
                i = where[m, first + p]
                for here, ref in ((True, own), (False, other)):

                    @pl.when((i >= 0) & (((i // CT) % 2 == core) == here))
                    def _():
                        dm, fm = lax.rem(x - i // 8 + 4, 4), lax.rem(ch + m, 2)
                        row = pl.multiple_of((i % CT) * STRIP, STRIP)
                        v = as_float(ref[dm, fm, pl.ds(row, STRIP), :]) * column_scale(
                            ref[dm, fm, CHILD_CODE:FRONT, :]
                        )
                        acc[p * STRIP : (p + 1) * STRIP, :] += jnp.where(mask, v, 0.0)

        return encode(acc[...])

    @pl.when(q == 0)
    def _():
        v, code = group(k)
        kept[...] = v
        kcode[...] = jnp.broadcast_to(code, kcode.shape)

    v, code = group(q)
    out[0, 0 : RT * STRIP, :] = kept[...]
    out[0, RT * STRIP : 2 * RT * STRIP, :] = v
    row = lax.broadcasted_iota(I32, (CODE, PANEL), 0)
    both = jnp.where(row == 0, kcode[0:1, :], code)
    out[0, 2 * RT * STRIP :, :] = both.astype(I32).astype(I16)


def compose(ids, where, own, other):
    whole = pl.BlockSpec((4, 2, TILE, PANEL), lambda i, *s: (0, 0, 0, 0))
    return pl.pallas_call(
        compose_kernel,
        grid_spec=pltpu.PrefetchScalarGridSpec(
            num_scalar_prefetch=2,
            grid=(8,),
            in_specs=[whole] * 2,
            out_specs=pl.BlockSpec((1, GROWS, PANEL), lambda i, *s: (i, 0, 0)),
            scratch_shapes=[
                pltpu.VMEM((RT * STRIP, PANEL), F32),
                pltpu.VMEM((RT * STRIP, PANEL), I16),
                pltpu.VMEM((8, PANEL), F32),
            ],
        ),
        out_shape=jax.ShapeDtypeStruct((8, GROWS, PANEL), I16),
        compiler_params=pltpu.CompilerParams(vmem_limit_bytes=24 * MIB),
        cost_estimate=pl.CostEstimate(flops=0, bytes_accessed=6 * MIB, transcendentals=0),
    )(ids, where, own, other)


def route_kernel(ids, slots, where, own, other, send, lines, codes, isem, osem, csem):
    c, g, core = ids[2], ids[3], ids[4]
    rows = [where[ch, g * RT + p] for ch in range(2) for p in range(RT)]
    to = [[slots[ch, c * CT + j] // QT for j in range(CT)] for ch in range(2)]

    def come(m, act):
        i = rows[m]
        src = (m // RT) * 4 + i // 8
        for here, buf in ((True, own), (False, other)):

            @pl.when((i >= 0) & (((i // CT) % 2 == core) == here))
            def _():
                act(pltpu.make_async_copy(buf.at[src], lines.at[m], isem.at[m]))

    def leave(m, act):
        @pl.when(rows[m] >= 0)
        def _():
            for j in range(CT):
                act(
                    pltpu.make_async_copy(
                        lines.at[m, pl.ds(0, TILE), pl.ds(j * TILE, TILE)],
                        send.at[to[m // RT][j], pl.ds(m * TILE, TILE), :],
                        osem.at[m * CT + j],
                    )
                )

    for m in range(2 * RT):
        come(m, lambda copy: copy.start())
    for m in range(2 * RT):
        come(m, lambda copy: copy.wait())
        leave(m, lambda copy: copy.start())
    line = lax.broadcasted_iota(I32, (CODE, TILE), 0)
    codes[...] = jnp.zeros_like(codes)
    for ch in range(2):
        for j in range(CT):
            q = to[ch][j]
            v = codes[q].astype(I32)
            for p in range(RT):
                m = ch * RT + p
                mine = lines[m, TILE:, j * TILE : (j + 1) * TILE].astype(I32)
                v = jnp.where(line == m, mine, v)
            codes[q] = v.astype(I16)
    tails = [
        pltpu.make_async_copy(codes.at[q], send.at[q, pl.ds(2 * RT * TILE, CODE), :], csem.at[q])
        for q in range(8)
    ]
    for copy in tails:
        copy.start()
    for m in range(2 * RT):
        leave(m, lambda copy: copy.wait())
    for copy in tails:
        copy.wait()


def route(ids, slots, where, own, other):
    return pl.pallas_call(
        route_kernel,
        grid_spec=pltpu.PrefetchScalarGridSpec(
            num_scalar_prefetch=3,
            grid=(1,),
            in_specs=[pl.BlockSpec(memory_space=pl.ANY)] * 2,
            out_specs=pl.BlockSpec(memory_space=pl.ANY),
            scratch_shapes=[
                pltpu.VMEM((2 * RT, TILE + CODE, 1024), I16),
                pltpu.VMEM((8, CODE, TILE), I16),
                pltpu.SemaphoreType.DMA((2 * RT,)),
                pltpu.SemaphoreType.DMA((2 * RT * CT,)),
                pltpu.SemaphoreType.DMA((8,)),
            ],
        ),
        out_shape=pltpu.HBM((8, CROWS, TILE), I16),
        compiler_params=pltpu.CompilerParams(vmem_limit_bytes=32 * MIB),
        cost_estimate=pl.CostEstimate(flops=0, bytes_accessed=8 * MIB, transcendentals=0),
    )(ids, slots, where, own, other)


def nt(a, b):
    return lax.dot_general(
        a, b, (((1,), (1,)), ((), ())), precision=HIGHEST, preferred_element_type=F32
    )


def nn(a, b):
    return lax.dot_general(
        a, b, (((1,), (0,)), ((), ())), precision=HIGHEST, preferred_element_type=F32
    )


NB = 64
WAYS = 8


def inverse_kernel(a_ref, out, w, f):
    n = PANEL // NB
    out[...] = jnp.zeros_like(out)
    row = lax.broadcasted_iota(I32, (NB, NB), 0)
    col = lax.broadcasted_iota(I32, (NB, NB), 1)
    eye = row == col
    lanes = lax.broadcasted_iota(I32, (1, 2 * NB), 1)
    sub = lax.broadcasted_iota(I32, (NB, 1), 0)

    def blk(i):
        return slice(i * NB, (i + 1) * NB)

    f[...] = a_ref[...]
    for k in range(n):
        w[:, :NB] = f[blk(k), blk(k)]
        w[:, NB:] = jnp.where(eye, 1.0, 0.0).astype(F32)

        def step(n4, _):
            j = n4 * WAYS
            lines = [w[pl.ds(j + a, 1), :] for a in range(WAYS)]
            square = w[:, :NB]
            columns = [
                jnp.sum(jnp.where(col == j + a, square, 0.0), axis=1, keepdims=True)
                for a in range(WAYS)
            ]
            small = [
                [
                    jnp.sum(jnp.where(lanes == j + b, lines[a], 0.0), axis=1, keepdims=True)
                    if b >= a
                    else None
                    for b in range(WAYS)
                ]
                for a in range(WAYS)
            ]
            factors = []
            for a in range(WAYS):
                inverse = 1.0 / small[a][a]
                for b in range(a + 1, WAYS):
                    times = small[a][b] * inverse
                    for d in range(b, WAYS):
                        small[b][d] = small[b][d] - times * small[a][d]
                    lines[b] = lines[b] - times * lines[a]
                    columns[b] = columns[b] - times * columns[a]
                factors.append(jnp.where(sub >= j + WAYS, columns[a] * inverse, 0.0))
            total = w[...]
            for a in range(WAYS):
                total = total - factors[a] * lines[a]
            w[...] = total
            for a in range(1, WAYS):
                w[pl.ds(j + a, 1), :] = lines[a]
            return 0

        lax.fori_loop(0, NB // WAYS, step, 0)
        d = jnp.sum(jnp.where(eye, w[:, :NB], 0.0), axis=1, keepdims=True)
        inv = w[:, NB:] * (1.0 / jnp.sqrt(d))
        out[blk(k), blk(k)] = inv
        rest = (k + 1) * NB
        if rest < PANEL:
            below = nt(f[rest:, blk(k)], inv)
            f[rest:, blk(k)] = below
            f[rest:, rest:] = f[rest:, rest:] - nt(below, below)
    for k in range(1, n):
        acc = nn(f[blk(k), : k * NB], out[: k * NB, : k * NB])
        out[blk(k), : k * NB] = -nn(out[blk(k), blk(k)], acc)


def inverse_factor(a):
    return pl.pallas_call(
        inverse_kernel,
        out_shape=jax.ShapeDtypeStruct((PANEL, PANEL), F32),
        scratch_shapes=[pltpu.VMEM((NB, 2 * NB), F32), pltpu.VMEM((PANEL, PANEL), F32)],
        compiler_params=pltpu.CompilerParams(vmem_limit_bytes=24 * MIB),
        cost_estimate=pl.CostEstimate(flops=1 << 34, bytes_accessed=2 * MIB, transcendentals=0),
    )(a)


def split(v):
    hi = v.astype(BF16)
    return hi, (v - hi.astype(F32)).astype(BF16)


def left3(v):
    hi, lo = split(v)
    return jnp.concatenate([hi, hi, lo], 1)


def right3(v):
    hi, lo = split(v)
    return jnp.concatenate([hi, lo, hi], 1)


def dot3(a, b):
    return lax.dot_general(a, b, (((1,), (1,)), ((), ())), preferred_element_type=F32)


def base_kernel(ids, where, recv, front, out, tiles, codes, tsem):
    t = pl.program_id(0)
    c, g = ids[2], ids[3]
    col = c * QT + t
    js = [where[ch, col] for ch in range(2)]
    there = [[where[ch, g * RT + p] >= 0 for p in range(RT)] for ch in range(2)]

    def each(act):
        for ch in range(2):
            src = js[ch] // CT

            @pl.when(js[ch] >= 0)
            def _():
                act(
                    pltpu.make_async_copy(
                        recv.at[src, pl.ds(2 * RT * TILE, CODE), :],
                        codes.at[ch],
                        tsem.at[2 * RT + ch],
                    )
                )

            for p in range(RT):
                m = ch * RT + p

                @pl.when(there[ch][p] & (js[ch] >= 0))
                def _():
                    act(
                        pltpu.make_async_copy(
                            recv.at[src, pl.ds(m * TILE, TILE), :], tiles.at[m], tsem.at[m]
                        )
                    )

    each(lambda copy: copy.start())

    out[...] = front[...]
    each(lambda copy: copy.wait())
    for p in range(RT):
        rows = slice(p * TILE, (p + 1) * TILE)
        for ch in range(2):
            m = ch * RT + p

            @pl.when(there[ch][p] & (js[ch] >= 0))
            def _():
                out[rows, :] += as_float(tiles[m]) * column_scale(codes[ch], m)


def base(ids, where, recv, front):
    line = pl.BlockSpec((RT * TILE, TILE), lambda i, *s: (0, i))
    return pl.pallas_call(
        base_kernel,
        grid_spec=pltpu.PrefetchScalarGridSpec(
            num_scalar_prefetch=2,
            grid=(QT,),
            in_specs=[pl.BlockSpec(memory_space=pl.ANY), line],
            out_specs=line,
            scratch_shapes=[
                pltpu.VMEM((2 * RT, TILE, TILE), I16),
                pltpu.VMEM((2, CODE, TILE), I16),
                pltpu.SemaphoreType.DMA((2 * RT + 2,)),
            ],
        ),
        out_shape=jax.ShapeDtypeStruct((RT * TILE, QT * TILE), F32),
        compiler_params=pltpu.CompilerParams(vmem_limit_bytes=24 * MIB),
        cost_estimate=pl.CostEstimate(flops=0, bytes_accessed=20 * MIB, transcendentals=0),
    )(ids, where, recv, front)


def final_kernel(
    ids, diag, inv, gx, goth, front, out,
    gbuf, rows_f, left, inverse,
):
    t = pl.program_id(0)
    c, g, core = ids[2], ids[3], ids[4]
    col = c * QT + t
    @pl.when(t == 0)
    def _():
        inverse[...] = right3(inv[...])
        for s in range(8):
            scale = column_scale(gx[s, 2 * RT * STRIP :, :], 0)
            v = as_float(gx[s, 0 : RT * STRIP, :]) * scale
            for p in range(RT):
                gbuf[p * TILE + s * STRIP : p * TILE + (s + 1) * STRIP, :] = v[
                    p * STRIP : (p + 1) * STRIP, :
                ]
        for p in range(RT):
            for a in range(2):

                @pl.when(g * RT + p == ids[8 + a])
                def _():
                    gbuf[p * TILE : (p + 1) * TILE, :] = diag[a * TILE : (a + 1) * TILE, :]

        v = dot3(left3(gbuf[...]), inverse[...])
        rows_f[...] = v
        left[...] = left3(v)

    side = pl.multiple_of((t % RT) * STRIP, STRIP)

    @pl.when(t // RT == core)
    def _():
        for s in range(8):
            gbuf[s * STRIP : (s + 1) * STRIP, :] = as_float(
                gx[s, pl.ds(RT * STRIP + side, STRIP), :]
            ) * column_scale(gx[s, 2 * RT * STRIP :, :], 1)

    @pl.when(t // RT != core)
    def _():
        for s in range(8):
            gbuf[s * STRIP : (s + 1) * STRIP, :] = as_float(
                goth[s, pl.ds(side, STRIP), :]
            ) * column_scale(goth[s, RT * STRIP :, :], 1)

    for a in range(2):

        @pl.when(col == ids[8 + a])
        def _():
            gbuf[0:TILE, :] = diag[a * TILE : (a + 1) * TILE, :]

    right = right3(dot3(left3(gbuf[0:TILE, :]), inverse[...]))
    out[...] = front[...] - dot3(left[...], right)
    for a in range(2):

        @pl.when(col == ids[8 + a])
        def _():
            out[...] = rows_f[:, a * TILE : (a + 1) * TILE]


def final(ids, diag, inv, gx, goth, front):
    def whole(*shape):
        return pl.BlockSpec(shape, lambda i, *s: (0,) * len(shape))

    line = pl.BlockSpec((RT * TILE, TILE), lambda i, *s: (0, i))
    return pl.pallas_call(
        final_kernel,
        grid_spec=pltpu.PrefetchScalarGridSpec(
            num_scalar_prefetch=1,
            grid=(QT,),
            in_specs=[
                whole(PANEL, PANEL),
                whole(PANEL, PANEL),
                whole(8, GROWS, PANEL),
                whole(8, GROWS - RT * STRIP, PANEL),
                line,
            ],
            out_specs=line,
            scratch_shapes=[
                pltpu.VMEM((RT * TILE, PANEL), F32),
                pltpu.VMEM((RT * TILE, PANEL), F32),
                pltpu.VMEM((RT * TILE, 3 * PANEL), BF16),
                pltpu.VMEM((PANEL, 3 * PANEL), BF16),
            ],
        ),
        out_shape=jax.ShapeDtypeStruct((RT * TILE, QT * TILE), F32),
        compiler_params=pltpu.CompilerParams(vmem_limit_bytes=52 * MIB),
        cost_estimate=pl.CostEstimate(flops=1 << 33, bytes_accessed=20 * MIB, transcendentals=0),
    )(ids, diag, inv, gx, goth, front)


def pick(v, at):
    return lax.dynamic_index_in_dim(v, at, 0, keepdims=False)


def fetch_partner(panel, x, core, z, yh):
    halves = panel.reshape(2, 512, 1024)
    piece = pick(halves, ((z - x + 4) % 4) // 2)
    came = []
    for dx in (1, 2, 3):
        pairs = [
            (flat(c, xs, y, (xs + 2 * b) % 4, y), flat(c, (xs + dx) % 4, b, xs, y))
            for c in range(2)
            for xs in range(4)
            for y in range(2)
            for b in range(2)
        ]
        came.append(lax.ppermute(piece, AXES, pairs))
    pairs = [
        (flat(c, x, y, x, y), flat(c, x, 1 - y, x, y))
        for c in range(2)
        for x in range(4)
        for y in range(2)
    ]
    beside = lax.ppermute(pick(halves, 1 - core), AXES, pairs)
    way = (x - z + 4) % 4
    mine = jnp.where(way == 1, came[0], jnp.where(way == 2, came[1], came[2]))
    mine = jnp.where(way == 0, jnp.where(core == yh, pick(halves, core), beside), mine)
    return mine, shift(mine, dk=1)


def sum_first(v, core, z):
    v = v.reshape(2, 256, PANEL)
    v = pick(v, core) + shift(pick(v, 1 - core), dk=1)
    v = v.reshape(4, 64, PANEL)
    got = [shift(pick(v, (z + d) % 4), dz=d) for d in (1, 3, 2)]
    return pick(v, z) + got[0] + got[1] + got[2]


def gathered(v, at, **axis):
    (name,) = axis
    full = jnp.zeros((4,) + v.shape, v.dtype)
    full = lax.dynamic_update_index_in_dim(full, v, at, 0)
    for d in (1, 3, 2):
        full = lax.dynamic_update_index_in_dim(full, shift(v, **{name: d}), (at - d) % 4, 0)
    return full


def sum_x(v, x):
    v = v.reshape(4, 64, PANEL)
    got = [shift(pick(v, (x + d) % 4), dx=d) for d in (1, 3, 2)]
    return pick(v, x) + got[0] + got[1] + got[2]


def sum_y(v):
    return (v + shift(v, dc=1, dy=1)) + (shift(v, dc=1) + shift(v, dy=1))


def sum_third(v, x, core):
    v = gathered(v, x, dx=0).reshape(256, PANEL)
    other = shift(v, dk=1)
    return jnp.concatenate([jnp.where(core == 0, v, other), jnp.where(core == 0, other, v)])


def tables(child_maps, parent_place):
    hit = child_maps[:, :, None] == jnp.arange(48, dtype=I32)
    slots = jnp.sum(jnp.where(hit, parent_place, 0), axis=2)
    hit = slots[:, :, None] == jnp.arange(48, dtype=I32)
    where = jnp.max(jnp.where(hit, jnp.arange(32, dtype=I32)[None, :, None], -1), axis=1)
    return slots, where


def body(child_blocks, child_panels, child_patterns, child_maps, parent_place, parent_front):
    ch, x, core, z, yh = (lax.axis_index(n).astype(I32) for n in AXES)
    r, c = x * 2 + core, z * 2 + yh
    slots, where = tables(child_maps, parent_place)
    e = parent_place[0], parent_place[1]
    ids = jnp.stack([ch, r, c, ch * 8 + r, core, z, yh, ch * 4 + x, e[0], e[1], x])
    panel = child_panels[0]
    parent_front = pltpu.with_memory_space_constraint(parent_front, pltpu.HBM)
    block = pltpu.with_memory_space_constraint(child_blocks[0], pltpu.HBM)
    mine, theirs = fetch_partner(panel, x, core, z, yh)
    mine, theirs, ids, slots, where = lax.optimization_barrier((mine, theirs, ids, slots, where))
    send, diag, gcol = update(
        ids, slots, child_patterns, block, panel, jnp.concatenate([mine, theirs]).reshape(CT, TILE, 1024), parent_front
    )
    own = lax.all_to_all(send, ("child", "x"), split_axis=0, concat_axis=0, tiled=True)

    diag = sum_first(diag, core, z)
    diag, gcol = lax.optimization_barrier((diag, gcol))
    parts = strips(ids, gcol, parent_front)
    parts = [parts[0]] + [shift(parts[d], dz=d) for d in range(1, 4)]
    diag = gathered(diag, z, dz=0).reshape(256, PANEL)
    strip = choose_z(ids, where, parts)
    own, diag, strip = lax.optimization_barrier((own, diag, strip))

    other = shift(own, dk=1)
    send = route(ids, slots, where, own, other)
    kept, moved = pick(strip, yh), pick(strip, 1 - yh)
    moves = [shift(moved, dy=1), shift(kept, dc=1), shift(moved, dc=1, dy=1)]
    diag, *moves = lax.optimization_barrier((sum_x(diag, x), *moves))
    strip = choose_y(ids, where, [kept] + moves)
    diag = sum_y(diag)
    send, diag, strip = lax.optimization_barrier((send, diag, strip))
    recv = lax.all_to_all(send, ("z", "yh"), split_axis=0, concat_axis=0, tiled=True)

    diag = sum_third(diag, x, core)
    line = jnp.stack([strip] + [shift(strip, dx=d) for d in range(1, 4)])
    inv = inverse_factor(diag)
    gsend = compose(ids, where, line, shift(line, dk=1))
    recv, inv, gsend = lax.optimization_barrier((recv, inv, gsend))
    gx = lax.all_to_all(gsend, ("z", "yh"), split_axis=0, concat_axis=0, tiled=True)
    with_children = base(ids, where, recv, parent_front)
    gx, with_children = lax.optimization_barrier((gx, with_children))
    goth = shift(gx[:, RT * STRIP :], dk=1)
    return final(ids, diag, inv, gx, goth, with_children)


def solution(mesh):
    fine = Mesh(mesh.devices.reshape(SIZES), AXES)
    rows, cols = ("x", "core"), ("z", "yh")
    return jax.shard_map(
        body,
        mesh=fine,
        in_specs=(
            P("child", rows, cols),
            P("child", rows, None),
            P(),
            P(),
            P(),
            P(("child", "x", "core"), cols),
        ),
        out_specs=P(("child", "x", "core"), cols),
        check_vma=False,
    )
```

```python
import jax
import jax.numpy as jnp
from jax import lax
from jax.experimental import pallas as pl
from jax.experimental.pallas import tpu as pltpu
from jax.sharding import Mesh
from jax.sharding import PartitionSpec as P

TILE = 256
PANEL = 512
CODE = 16
CT = 4
RT = 3
QT = 6
STRIP = 32
GROWS = 2 * RT * STRIP + CODE
CROWS = 2 * RT * TILE + CODE
AXES = ("child", "x", "core", "z", "yh")
SIZES = (2, 4, 2, 4, 2)
MIB = 1 << 20
F32 = jnp.float32
I32 = jnp.int32
I16 = jnp.int16
BF16 = jnp.bfloat16
HIGHEST = lax.Precision.HIGHEST


def flat(c, x, k, z, y):
    return (((c * 4 + x) * 2 + k) * 4 + z) * 2 + y


def everyone():
    return [
        (c, x, k, z, y)
        for c in range(2)
        for x in range(4)
        for k in range(2)
        for z in range(4)
        for y in range(2)
    ]


def shift(v, dc=0, dx=0, dk=0, dz=0, dy=0):
    pairs = [
        (flat(c, x, k, z, y), flat(c ^ dc, (x + dx) % 4, k ^ dk, (z + dz) % 4, y ^ dy))
        for c, x, k, z, y in everyone()
    ]
    return lax.ppermute(v, AXES, pairs)


def encode(u):
    top = jnp.max(jnp.abs(u), axis=0, keepdims=True)
    code = jnp.ceil(jnp.log2(jnp.maximum(top, 1e-30)) * 128.0)
    scale = jnp.exp2(15.0 - code * (1.0 / 128.0)) * (32766.0 / 32768.0)
    return jnp.floor(u * scale + 0.5).astype(I32).astype(I16), code


def scale_rows(code):
    return jnp.broadcast_to(code, (CODE, code.shape[1])).astype(I32).astype(I16)


def as_float(q):
    return q.astype(I32).astype(F32)


def column_scale(codes, row=0):
    code = as_float(codes)[row : row + 1, :]
    return jnp.exp2(code * (1.0 / 128.0) - 15.0) * (32768.0 / 32766.0)


def update_kernel(
    ids, slots, pat, blk, pan, mine, other, front, send, diag, gcol, tile, sem, lines, lsem
):
    n = pl.program_id(0)
    ch, r, c, g = ids[0], ids[1], ids[2], ids[3]
    e = (ids[8], ids[9])
    j = lax.rem(ids[4] * 2 + n, CT)
    turn = n % 2
    si = [slots[ch, r * CT + i] for i in range(CT)]
    sj = slots[ch, c * CT + j]

    def leave(turn, j, act):
        for i in range(CT):
            act(
                pltpu.make_async_copy(
                    lines.at[turn, i],
                    send.at[si[i] // QT, :, pl.ds(pl.multiple_of(j * TILE, TILE), TILE)],
                    lsem.at[turn, i],
                )
            )

    @pl.when(n == 0)
    def _():
        diag[...] = jnp.zeros_like(diag)
        for a in range(2):
            for b in range(2):

                @pl.when((e[a] // RT == g) & (e[b] // QT == c))
                def _():
                    rows = pl.multiple_of((e[a] % RT) * TILE, TILE)
                    cols = pl.multiple_of((e[b] % QT) * TILE, TILE)
                    copy = pltpu.make_async_copy(
                        front.at[pl.ds(rows, TILE), pl.ds(cols, TILE)], tile, sem
                    )
                    copy.start()
                    copy.wait()
                    diag[a * TILE : (a + 1) * TILE, b * TILE : (b + 1) * TILE] = tile[...]

    @pl.when(n >= 2)
    def _():
        leave(turn, lax.rem(ids[4] * 2 + n - 2, CT), lambda copy: copy.wait())

    par = jnp.where(n < 2, mine[...], other[...])
    prod = lax.dot_general(pan[...], par, (((1,), (1,)), ((), ())), preferred_element_type=F32)
    for i in range(CT):
        rows = slice(i * TILE, (i + 1) * TILE)
        u = (blk[rows, :] - prod[rows, :]) * pat[ch, r * CT + i, c * CT + j].astype(F32)
        q, code = encode(u)
        lines[turn, i, 0:TILE, :] = q
        lines[turn, i, TILE:, :] = scale_rows(code)
        for b in range(2):
            at = slice(b * TILE, (b + 1) * TILE)

            @pl.when(sj == e[b])
            def _():
                gcol[rows, at] = u
                for a in range(2):

                    @pl.when(si[i] == e[a])
                    def _():
                        diag[a * TILE : (a + 1) * TILE, at] += u

    leave(turn, j, lambda copy: copy.start())

    @pl.when(n == CT - 1)
    def _():
        leave(1 - turn, lax.rem(ids[4] * 2 + n - 1, CT), lambda copy: copy.wait())
        leave(turn, j, lambda copy: copy.wait())


def update(ids, slots, pat, blk, pan, mine, other, front):
    def column(n, ids, slots, pat):
        return 0, lax.rem(ids[4] * 2 + n, CT)

    return pl.pallas_call(
        update_kernel,
        grid_spec=pltpu.PrefetchScalarGridSpec(
            num_scalar_prefetch=3,
            grid=(CT,),
            in_specs=[
                pl.BlockSpec((1024, TILE), column),
                pl.BlockSpec((1024, 1024), lambda n, *s: (0, 0)),
                pl.BlockSpec((TILE, 1024), lambda n, *s: (jnp.minimum(n, 1), 0)),
                pl.BlockSpec((TILE, 1024), lambda n, *s: (jnp.maximum(n - 2, 0), 0)),
                pl.BlockSpec(memory_space=pl.ANY),
            ],
            out_specs=[
                pl.BlockSpec(memory_space=pl.ANY),
                pl.BlockSpec((PANEL, PANEL), lambda n, *s: (0, 0)),
                pl.BlockSpec((CT * TILE, PANEL), lambda n, *s: (0, 0)),
            ],
            scratch_shapes=[
                pltpu.VMEM((TILE, TILE), F32),
                pltpu.SemaphoreType.DMA,
                pltpu.VMEM((2, CT, TILE + CODE, TILE), I16),
                pltpu.SemaphoreType.DMA((2, CT)),
            ],
        ),
        out_shape=[
            pltpu.HBM((8, TILE + CODE, 1024), I16),
            pltpu.HBM((PANEL, PANEL), F32),
            pltpu.HBM((CT * TILE, PANEL), F32),
        ],
        compiler_params=pltpu.CompilerParams(vmem_limit_bytes=48 * MIB),
        cost_estimate=pl.CostEstimate(flops=1 << 31, bytes_accessed=14 * MIB, transcendentals=0),
    )(ids, slots, pat, blk, pan, mine, other, front)


def strips_kernel(ids, gcol, front, *rest):
    outs, (wide, sem) = rest[:4], rest[4:]
    c, z = ids[2], ids[5]
    for a in range(2):
        e = ids[8 + a]

        @pl.when(e // QT == c)
        def _():
            at = pl.multiple_of((e % QT) * TILE, TILE)
            copy = pltpu.make_async_copy(
                front.at[:, pl.ds(at, TILE)], wide.at[:, pl.ds(a * TILE, TILE)], sem
            )
            copy.start()
            copy.wait()

    for d in range(4):
        for f in range(2):
            s = ((z + d) % 4) * 2 + f
            at = 0
            for ref, n in ((gcol, CT), (wide, RT)):
                parts = [
                    ref[pl.ds(pl.multiple_of(p * TILE + s * STRIP, STRIP), STRIP), :]
                    for p in range(n)
                ]
                q, code = encode(jnp.concatenate(parts, 0))
                outs[d][f, at : at + n * STRIP, :] = q
                outs[d][f, at + n * STRIP : at + n * STRIP + CODE, :] = scale_rows(code)
                at += n * STRIP + CODE


def strips(ids, gcol, front):
    return pl.pallas_call(
        strips_kernel,
        grid_spec=pltpu.PrefetchScalarGridSpec(
            num_scalar_prefetch=1,
            grid=(1,),
            in_specs=[
                pl.BlockSpec((CT * TILE, PANEL), lambda i, *s: (0, 0)),
                pl.BlockSpec(memory_space=pl.ANY),
            ],
            out_specs=[pl.BlockSpec((2, TILE, PANEL), lambda i, *s: (0, 0, 0))] * 4,
            scratch_shapes=[pltpu.VMEM((RT * TILE, PANEL), F32), pltpu.SemaphoreType.DMA],
        ),
        out_shape=[jax.ShapeDtypeStruct((2, TILE, PANEL), I16)] * 4,
        compiler_params=pltpu.CompilerParams(vmem_limit_bytes=24 * MIB),
        cost_estimate=pl.CostEstimate(flops=0, bytes_accessed=6 * MIB, transcendentals=0),
    )(ids, gcol, front)


CHILD_CODE = CT * STRIP
FRONT = CHILD_CODE + CODE
FRONT_CODE = FRONT + RT * STRIP


def regions(ids, where, child):
    for a in range(2):
        cols = slice(a * TILE, (a + 1) * TILE)
        yield slice(0, FRONT), cols, where[child, ids[8 + a]] // CT
        yield slice(FRONT, TILE), cols, ids[8 + a] // QT


def choose_z_kernel(ids, where, *refs):
    out, sems = refs[4], refs[5]

    def each(act):
        for n, (rows, cols, holder) in enumerate(regions(ids, where, ids[0])):
            for d in range(4):

                @pl.when(lax.rem(ids[5] - holder // 2 + 4, 4) == d)
                def _():
                    act(
                        pltpu.make_async_copy(
                            refs[d].at[:, rows, cols], out.at[:, rows, cols], sems.at[n]
                        )
                    )

    each(lambda copy: copy.start())
    each(lambda copy: copy.wait())


def choose_z(ids, where, parts):
    return pl.pallas_call(
        choose_z_kernel,
        grid_spec=pltpu.PrefetchScalarGridSpec(
            num_scalar_prefetch=2,
            grid=(1,),
            in_specs=[pl.BlockSpec(memory_space=pl.ANY)] * 4,
            out_specs=pl.BlockSpec((2, TILE, PANEL), lambda i, *s: (0, 0, 0)),
            scratch_shapes=[pltpu.SemaphoreType.DMA((4,))],
        ),
        out_shape=jax.ShapeDtypeStruct((2, TILE, PANEL), I16),
        cost_estimate=pl.CostEstimate(flops=0, bytes_accessed=MIB, transcendentals=0),
    )(ids, where, *parts)


def choose_y_kernel(ids, where, kept, beside, across, both, out, sems):
    def each(act):
        for n, (near, far) in enumerate(((kept, beside), (across, both))):
            child = lax.rem(ids[0] + n, 2)
            for m, (rows, cols, holder) in enumerate(regions(ids, where, child)):
                here = lax.rem(holder + 8, 2) == ids[6]
                for side, ref in ((True, near), (False, far)):

                    @pl.when(here == side)
                    def _():
                        act(
                            pltpu.make_async_copy(
                                ref.at[rows, cols], out.at[n, rows, cols], sems.at[n * 4 + m]
                            )
                        )

    each(lambda copy: copy.start())
    each(lambda copy: copy.wait())


def choose_y(ids, where, parts):
    return pl.pallas_call(
        choose_y_kernel,
        grid_spec=pltpu.PrefetchScalarGridSpec(
            num_scalar_prefetch=2,
            grid=(1,),
            in_specs=[pl.BlockSpec(memory_space=pl.ANY)] * 4,
            out_specs=pl.BlockSpec((2, TILE, PANEL), lambda i, *s: (0, 0, 0)),
            scratch_shapes=[pltpu.SemaphoreType.DMA((8,))],
        ),
        out_shape=jax.ShapeDtypeStruct((2, TILE, PANEL), I16),
        cost_estimate=pl.CostEstimate(flops=0, bytes_accessed=MIB, transcendentals=0),
    )(ids, where, *parts)


def compose_kernel(ids, where, own, other, out, acc, kept, kcode):
    q = pl.program_id(0)
    ch, core, k, x = ids[0], ids[4], ids[7], ids[10]
    half = lax.broadcasted_iota(I32, (STRIP, PANEL), 1) < TILE

    def group(q):
        first = q * QT + core * RT
        d, f = lax.rem(x - q % 4 + 4, 4), lax.rem(ch + q // 4, 2)
        acc[...] = as_float(own[d, f, FRONT:FRONT_CODE, :]) * column_scale(
            own[d, f, FRONT_CODE:, :]
        )
        for m in range(2):
            known = [(where[m, ids[8 + a]] >= 0).astype(I32) for a in range(2)]
            mask = jnp.where(half, known[0], known[1]) > 0
            for p in range(RT):
                i = where[m, first + p]
                for here, ref in ((True, own), (False, other)):

                    @pl.when((i >= 0) & (((i // CT) % 2 == core) == here))
                    def _():
                        dm, fm = lax.rem(x - i // 8 + 4, 4), lax.rem(ch + m, 2)
                        row = pl.multiple_of((i % CT) * STRIP, STRIP)
                        v = as_float(ref[dm, fm, pl.ds(row, STRIP), :]) * column_scale(
                            ref[dm, fm, CHILD_CODE:FRONT, :]
                        )
                        acc[p * STRIP : (p + 1) * STRIP, :] += jnp.where(mask, v, 0.0)

        return encode(acc[...])

    @pl.when(q == 0)
    def _():
        v, code = group(k)
        kept[...] = v
        kcode[...] = jnp.broadcast_to(code, kcode.shape)

    v, code = group(q)
    out[0, 0 : RT * STRIP, :] = kept[...]
    out[0, RT * STRIP : 2 * RT * STRIP, :] = v
    row = lax.broadcasted_iota(I32, (CODE, PANEL), 0)
    both = jnp.where(row == 0, kcode[0:1, :], code)
    out[0, 2 * RT * STRIP :, :] = both.astype(I32).astype(I16)


def compose(ids, where, own, other):
    whole = pl.BlockSpec((4, 2, TILE, PANEL), lambda i, *s: (0, 0, 0, 0))
    return pl.pallas_call(
        compose_kernel,
        grid_spec=pltpu.PrefetchScalarGridSpec(
            num_scalar_prefetch=2,
            grid=(8,),
            in_specs=[whole] * 2,
            out_specs=pl.BlockSpec((1, GROWS, PANEL), lambda i, *s: (i, 0, 0)),
            scratch_shapes=[
                pltpu.VMEM((RT * STRIP, PANEL), F32),
                pltpu.VMEM((RT * STRIP, PANEL), I16),
                pltpu.VMEM((8, PANEL), F32),
            ],
        ),
        out_shape=jax.ShapeDtypeStruct((8, GROWS, PANEL), I16),
        compiler_params=pltpu.CompilerParams(vmem_limit_bytes=24 * MIB),
        cost_estimate=pl.CostEstimate(flops=0, bytes_accessed=6 * MIB, transcendentals=0),
    )(ids, where, own, other)


def route_kernel(ids, slots, where, own, other, send, lines, codes, isem, osem, csem):
    c, g, core = ids[2], ids[3], ids[4]
    rows = [where[ch, g * RT + p] for ch in range(2) for p in range(RT)]
    to = [[slots[ch, c * CT + j] // QT for j in range(CT)] for ch in range(2)]

    def come(m, act):
        i = rows[m]
        src = (m // RT) * 4 + i // 8
        for here, buf in ((True, own), (False, other)):

            @pl.when((i >= 0) & (((i // CT) % 2 == core) == here))
            def _():
                act(pltpu.make_async_copy(buf.at[src], lines.at[m], isem.at[m]))

    def leave(m, act):
        @pl.when(rows[m] >= 0)
        def _():
            for j in range(CT):
                act(
                    pltpu.make_async_copy(
                        lines.at[m, pl.ds(0, TILE), pl.ds(j * TILE, TILE)],
                        send.at[to[m // RT][j], pl.ds(m * TILE, TILE), :],
                        osem.at[m * CT + j],
                    )
                )

    for m in range(2 * RT):
        come(m, lambda copy: copy.start())
    for m in range(2 * RT):
        come(m, lambda copy: copy.wait())
        leave(m, lambda copy: copy.start())
    line = lax.broadcasted_iota(I32, (CODE, TILE), 0)
    codes[...] = jnp.zeros_like(codes)
    for ch in range(2):
        for j in range(CT):
            q = to[ch][j]
            v = codes[q].astype(I32)
            for p in range(RT):
                m = ch * RT + p
                mine = lines[m, TILE:, j * TILE : (j + 1) * TILE].astype(I32)
                v = jnp.where(line == m, mine, v)
            codes[q] = v.astype(I16)
    tails = [
        pltpu.make_async_copy(codes.at[q], send.at[q, pl.ds(2 * RT * TILE, CODE), :], csem.at[q])
        for q in range(8)
    ]
    for copy in tails:
        copy.start()
    for m in range(2 * RT):
        leave(m, lambda copy: copy.wait())
    for copy in tails:
        copy.wait()


def route(ids, slots, where, own, other):
    return pl.pallas_call(
        route_kernel,
        grid_spec=pltpu.PrefetchScalarGridSpec(
            num_scalar_prefetch=3,
            grid=(1,),
            in_specs=[pl.BlockSpec(memory_space=pl.ANY)] * 2,
            out_specs=pl.BlockSpec(memory_space=pl.ANY),
            scratch_shapes=[
                pltpu.VMEM((2 * RT, TILE + CODE, 1024), I16),
                pltpu.VMEM((8, CODE, TILE), I16),
                pltpu.SemaphoreType.DMA((2 * RT,)),
                pltpu.SemaphoreType.DMA((2 * RT * CT,)),
                pltpu.SemaphoreType.DMA((8,)),
            ],
        ),
        out_shape=pltpu.HBM((8, CROWS, TILE), I16),
        compiler_params=pltpu.CompilerParams(vmem_limit_bytes=32 * MIB),
        cost_estimate=pl.CostEstimate(flops=0, bytes_accessed=8 * MIB, transcendentals=0),
    )(ids, slots, where, own, other)


def nt(a, b):
    return lax.dot_general(
        a, b, (((1,), (1,)), ((), ())), precision=HIGHEST, preferred_element_type=F32
    )


def nn(a, b):
    return lax.dot_general(
        a, b, (((1,), (0,)), ((), ())), precision=HIGHEST, preferred_element_type=F32
    )


NB = 64
WAYS = 8


def inverse_kernel(a_ref, out, w, f):
    n = PANEL // NB
    out[...] = jnp.zeros_like(out)
    row = lax.broadcasted_iota(I32, (NB, NB), 0)
    col = lax.broadcasted_iota(I32, (NB, NB), 1)
    eye = row == col
    lanes = lax.broadcasted_iota(I32, (1, 2 * NB), 1)
    sub = lax.broadcasted_iota(I32, (NB, 1), 0)

    def blk(i):
        return slice(i * NB, (i + 1) * NB)

    f[...] = a_ref[...]
    for k in range(n):
        w[:, :NB] = f[blk(k), blk(k)]
        w[:, NB:] = jnp.where(eye, 1.0, 0.0).astype(F32)

        def step(n4, _):
            j = n4 * WAYS
            lines = [w[pl.ds(j + a, 1), :] for a in range(WAYS)]
            square = w[:, :NB]
            columns = [
                jnp.sum(jnp.where(col == j + a, square, 0.0), axis=1, keepdims=True)
                for a in range(WAYS)
            ]
            small = [
                [
                    jnp.sum(jnp.where(lanes == j + b, lines[a], 0.0), axis=1, keepdims=True)
                    if b >= a
                    else None
                    for b in range(WAYS)
                ]
                for a in range(WAYS)
            ]
            factors = []
            for a in range(WAYS):
                inverse = 1.0 / small[a][a]
                for b in range(a + 1, WAYS):
                    times = small[a][b] * inverse
                    for d in range(b, WAYS):
                        small[b][d] = small[b][d] - times * small[a][d]
                    lines[b] = lines[b] - times * lines[a]
                    columns[b] = columns[b] - times * columns[a]
                factors.append(jnp.where(sub >= j + WAYS, columns[a] * inverse, 0.0))
            total = w[...]
            for a in range(WAYS):
                total = total - factors[a] * lines[a]
            w[...] = total
            for a in range(1, WAYS):
                w[pl.ds(j + a, 1), :] = lines[a]
            return 0

        lax.fori_loop(0, NB // WAYS, step, 0)
        d = jnp.sum(jnp.where(eye, w[:, :NB], 0.0), axis=1, keepdims=True)
        inv = w[:, NB:] * (1.0 / jnp.sqrt(d))
        out[blk(k), blk(k)] = inv
        rest = (k + 1) * NB
        if rest < PANEL:
            below = nt(f[rest:, blk(k)], inv)
            f[rest:, blk(k)] = below
            f[rest:, rest:] = f[rest:, rest:] - nt(below, below)
    for k in range(1, n):
        acc = nn(f[blk(k), : k * NB], out[: k * NB, : k * NB])
        out[blk(k), : k * NB] = -nn(out[blk(k), blk(k)], acc)


def inverse_factor(a):
    return pl.pallas_call(
        inverse_kernel,
        out_shape=jax.ShapeDtypeStruct((PANEL, PANEL), F32),
        scratch_shapes=[pltpu.VMEM((NB, 2 * NB), F32), pltpu.VMEM((PANEL, PANEL), F32)],
        compiler_params=pltpu.CompilerParams(vmem_limit_bytes=24 * MIB),
        cost_estimate=pl.CostEstimate(flops=1 << 34, bytes_accessed=2 * MIB, transcendentals=0),
    )(a)


def split(v):
    hi = v.astype(BF16)
    return hi, (v - hi.astype(F32)).astype(BF16)


def left3(v):
    hi, lo = split(v)
    return jnp.concatenate([hi, hi, lo], 1)


def right3(v):
    hi, lo = split(v)
    return jnp.concatenate([hi, lo, hi], 1)


def dot3(a, b):
    return lax.dot_general(a, b, (((1,), (1,)), ((), ())), preferred_element_type=F32)


def base_kernel(ids, where, recv, front, out, tiles, codes, tsem):
    t = pl.program_id(0)
    c, g = ids[2], ids[3]
    col = c * QT + t
    js = [where[ch, col] for ch in range(2)]
    there = [[where[ch, g * RT + p] >= 0 for p in range(RT)] for ch in range(2)]

    def each(act):
        for ch in range(2):
            src = js[ch] // CT

            @pl.when(js[ch] >= 0)
            def _():
                act(
                    pltpu.make_async_copy(
                        recv.at[src, pl.ds(2 * RT * TILE, CODE), :],
                        codes.at[ch],
                        tsem.at[2 * RT + ch],
                    )
                )

            for p in range(RT):
                m = ch * RT + p

                @pl.when(there[ch][p] & (js[ch] >= 0))
                def _():
                    act(
                        pltpu.make_async_copy(
                            recv.at[src, pl.ds(m * TILE, TILE), :], tiles.at[m], tsem.at[m]
                        )
                    )

    each(lambda copy: copy.start())

    out[...] = front[...]
    each(lambda copy: copy.wait())
    for p in range(RT):
        rows = slice(p * TILE, (p + 1) * TILE)
        for ch in range(2):
            m = ch * RT + p

            @pl.when(there[ch][p] & (js[ch] >= 0))
            def _():
                out[rows, :] += as_float(tiles[m]) * column_scale(codes[ch], m)


def base(ids, where, recv, front):
    line = pl.BlockSpec((RT * TILE, TILE), lambda i, *s: (0, i))
    return pl.pallas_call(
        base_kernel,
        grid_spec=pltpu.PrefetchScalarGridSpec(
            num_scalar_prefetch=2,
            grid=(QT,),
            in_specs=[pl.BlockSpec(memory_space=pl.ANY), line],
            out_specs=line,
            scratch_shapes=[
                pltpu.VMEM((2 * RT, TILE, TILE), I16),
                pltpu.VMEM((2, CODE, TILE), I16),
                pltpu.SemaphoreType.DMA((2 * RT + 2,)),
            ],
        ),
        out_shape=jax.ShapeDtypeStruct((RT * TILE, QT * TILE), F32),
        compiler_params=pltpu.CompilerParams(vmem_limit_bytes=24 * MIB),
        cost_estimate=pl.CostEstimate(flops=0, bytes_accessed=20 * MIB, transcendentals=0),
    )(ids, where, recv, front)


def final_kernel(
    ids, diag, inv, gx, goth, front, out,
    gbuf, rows_f, left, inverse,
):
    t = pl.program_id(0)
    c, g, core = ids[2], ids[3], ids[4]
    col = c * QT + t
    @pl.when(t == 0)
    def _():
        inverse[...] = right3(inv[...])
        for s in range(8):
            scale = column_scale(gx[s, 2 * RT * STRIP :, :], 0)
            v = as_float(gx[s, 0 : RT * STRIP, :]) * scale
            for p in range(RT):
                gbuf[p * TILE + s * STRIP : p * TILE + (s + 1) * STRIP, :] = v[
                    p * STRIP : (p + 1) * STRIP, :
                ]
        for p in range(RT):
            for a in range(2):

                @pl.when(g * RT + p == ids[8 + a])
                def _():
                    gbuf[p * TILE : (p + 1) * TILE, :] = diag[a * TILE : (a + 1) * TILE, :]

        v = dot3(left3(gbuf[...]), inverse[...])
        rows_f[...] = v
        left[...] = left3(v)

    side = pl.multiple_of((t % RT) * STRIP, STRIP)

    @pl.when(t // RT == core)
    def _():
        for s in range(8):
            gbuf[s * STRIP : (s + 1) * STRIP, :] = as_float(
                gx[s, pl.ds(RT * STRIP + side, STRIP), :]
            ) * column_scale(gx[s, 2 * RT * STRIP :, :], 1)

    @pl.when(t // RT != core)
    def _():
        for s in range(8):
            gbuf[s * STRIP : (s + 1) * STRIP, :] = as_float(
                goth[s, pl.ds(side, STRIP), :]
            ) * column_scale(goth[s, RT * STRIP :, :], 1)

    for a in range(2):

        @pl.when(col == ids[8 + a])
        def _():
            gbuf[0:TILE, :] = diag[a * TILE : (a + 1) * TILE, :]

    right = right3(dot3(left3(gbuf[0:TILE, :]), inverse[...]))
    out[...] = front[...] - dot3(left[...], right)
    for a in range(2):

        @pl.when(col == ids[8 + a])
        def _():
            out[...] = rows_f[:, a * TILE : (a + 1) * TILE]


def final(ids, diag, inv, gx, goth, front):
    def whole(*shape):
        return pl.BlockSpec(shape, lambda i, *s: (0,) * len(shape))

    line = pl.BlockSpec((RT * TILE, TILE), lambda i, *s: (0, i))
    return pl.pallas_call(
        final_kernel,
        grid_spec=pltpu.PrefetchScalarGridSpec(
            num_scalar_prefetch=1,
            grid=(QT,),
            in_specs=[
                whole(PANEL, PANEL),
                whole(PANEL, PANEL),
                whole(8, GROWS, PANEL),
                whole(8, GROWS - RT * STRIP, PANEL),
                line,
            ],
            out_specs=line,
            scratch_shapes=[
                pltpu.VMEM((RT * TILE, PANEL), F32),
                pltpu.VMEM((RT * TILE, PANEL), F32),
                pltpu.VMEM((RT * TILE, 3 * PANEL), BF16),
                pltpu.VMEM((PANEL, 3 * PANEL), BF16),
            ],
        ),
        out_shape=jax.ShapeDtypeStruct((RT * TILE, QT * TILE), F32),
        compiler_params=pltpu.CompilerParams(vmem_limit_bytes=52 * MIB),
        cost_estimate=pl.CostEstimate(flops=1 << 33, bytes_accessed=20 * MIB, transcendentals=0),
    )(ids, diag, inv, gx, goth, front)


def pick(v, at):
    return lax.dynamic_index_in_dim(v, at, 0, keepdims=False)


def fetch_partner(panel, x, core, z, yh):
    halves = panel.reshape(2, 512, 1024)
    piece = pick(halves, ((z - x + 4) % 4) // 2)
    came = []
    for dx in (1, 2, 3):
        pairs = [
            (flat(c, xs, y, (xs + 2 * b) % 4, y), flat(c, (xs + dx) % 4, b, xs, y))
            for c in range(2)
            for xs in range(4)
            for y in range(2)
            for b in range(2)
        ]
        came.append(lax.ppermute(piece, AXES, pairs))
    pairs = [
        (flat(c, x, y, x, y), flat(c, x, 1 - y, x, y))
        for c in range(2)
        for x in range(4)
        for y in range(2)
    ]
    beside = lax.ppermute(pick(halves, 1 - core), AXES, pairs)
    way = (x - z + 4) % 4
    mine = jnp.where(way == 1, came[0], jnp.where(way == 2, came[1], came[2]))
    mine = jnp.where(way == 0, jnp.where(core == yh, pick(halves, core), beside), mine)
    return mine, shift(mine, dk=1)


def sum_first(v, core, z):
    v = v.reshape(2, 256, PANEL)
    v = pick(v, core) + shift(pick(v, 1 - core), dk=1)
    v = v.reshape(4, 64, PANEL)
    got = [shift(pick(v, (z + d) % 4), dz=d) for d in (1, 3, 2)]
    return pick(v, z) + got[0] + got[1] + got[2]


def gathered(v, at, **axis):
    (name,) = axis
    full = jnp.zeros((4,) + v.shape, v.dtype)
    full = lax.dynamic_update_index_in_dim(full, v, at, 0)
    for d in (1, 3, 2):
        full = lax.dynamic_update_index_in_dim(full, shift(v, **{name: d}), (at - d) % 4, 0)
    return full


def sum_x(v, x):
    v = v.reshape(4, 64, PANEL)
    got = [shift(pick(v, (x + d) % 4), dx=d) for d in (1, 3, 2)]
    return pick(v, x) + got[0] + got[1] + got[2]


def sum_y(v):
    v = v + shift(v, dc=1)
    return v + shift(v, dc=1, dy=1)


def sum_third(v, x, core):
    v = gathered(v, x, dx=0).reshape(256, PANEL)
    other = shift(v, dk=1)
    return jnp.concatenate([jnp.where(core == 0, v, other), jnp.where(core == 0, other, v)])


def tables(child_maps, parent_place):
    hit = child_maps[:, :, None] == jnp.arange(48, dtype=I32)
    slots = jnp.sum(jnp.where(hit, parent_place, 0), axis=2)
    hit = slots[:, :, None] == jnp.arange(48, dtype=I32)
    where = jnp.max(jnp.where(hit, jnp.arange(32, dtype=I32)[None, :, None], -1), axis=1)
    return slots, where


def body(child_blocks, child_panels, child_patterns, child_maps, parent_place, parent_front):
    ch, x, core, z, yh = (lax.axis_index(n).astype(I32) for n in AXES)
    r, c = x * 2 + core, z * 2 + yh
    slots, where = tables(child_maps, parent_place)
    e = parent_place[0], parent_place[1]
    ids = jnp.stack([ch, r, c, ch * 8 + r, core, z, yh, ch * 4 + x, e[0], e[1], x])
    panel = child_panels[0]
    parent_front = pltpu.with_memory_space_constraint(parent_front, pltpu.HBM)
    block = pltpu.with_memory_space_constraint(child_blocks[0], pltpu.HBM)
    mine, theirs = fetch_partner(panel, x, core, z, yh)
    mine, theirs, ids, slots, where = lax.optimization_barrier((mine, theirs, ids, slots, where))
    send, diag, gcol = update(
        ids, slots, child_patterns, block, panel, mine, theirs, parent_front
    )
    own = lax.all_to_all(send, ("child", "x"), split_axis=0, concat_axis=0, tiled=True)

    diag = sum_first(diag, core, z)
    diag, gcol = lax.optimization_barrier((diag, gcol))
    parts = strips(ids, gcol, parent_front)
    parts = [parts[0]] + [shift(parts[d], dz=d) for d in range(1, 4)]
    diag = gathered(diag, z, dz=0).reshape(256, PANEL)
    strip = choose_z(ids, where, parts)
    own, diag, strip = lax.optimization_barrier((own, diag, strip))

    other = shift(own, dk=1)
    send = route(ids, slots, where, own, other)
    kept, moved = pick(strip, yh), pick(strip, 1 - yh)
    moves = [shift(moved, dy=1), shift(kept, dc=1), shift(moved, dc=1, dy=1)]
    diag = sum_y(sum_x(diag, x))
    send, diag, kept, *moves = lax.optimization_barrier((send, diag, kept, *moves))
    recv = lax.all_to_all(send, ("z", "yh"), split_axis=0, concat_axis=0, tiled=True)

    strip = choose_y(ids, where, [kept] + moves)
    diag = sum_third(diag, x, core)
    line = jnp.stack([strip] + [shift(strip, dx=d) for d in range(1, 4)])
    inv = inverse_factor(diag)
    gsend = compose(ids, where, line, shift(line, dk=1))
    recv, inv, gsend = lax.optimization_barrier((recv, inv, gsend))
    gx = lax.all_to_all(gsend, ("z", "yh"), split_axis=0, concat_axis=0, tiled=True)
    with_children = base(ids, where, recv, parent_front)
    gx, with_children = lax.optimization_barrier((gx, with_children))
    goth = shift(gx[:, RT * STRIP :], dk=1)
    return final(ids, diag, inv, gx, goth, with_children)


def solution(mesh):
    fine = Mesh(mesh.devices.reshape(SIZES), AXES)
    rows, cols = ("x", "core"), ("z", "yh")
    return jax.shard_map(
        body,
        mesh=fine,
        in_specs=(
            P("child", rows, cols),
            P("child", rows, None),
            P(),
            P(),
            P(),
            P(("child", "x", "core"), cols),
        ),
        out_specs=P(("child", "x", "core"), cols),
        check_vma=False,
    )
```

```python
import jax
import jax.numpy as jnp
from jax import lax
from jax.experimental import pallas as pl
from jax.experimental.pallas import tpu as pltpu
from jax.sharding import Mesh
from jax.sharding import PartitionSpec as P

TILE = 256
PANEL = 512
CODE = 16
CT = 4
RT = 3
QT = 6
STRIP = 32
GROWS = 2 * RT * STRIP + CODE
CROWS = 2 * RT * TILE + CODE
AXES = ("child", "x", "core", "z", "yh")
SIZES = (2, 4, 2, 4, 2)
MIB = 1 << 20
F32 = jnp.float32
I32 = jnp.int32
I16 = jnp.int16
BF16 = jnp.bfloat16
HIGHEST = lax.Precision.HIGHEST


def flat(c, x, k, z, y):
    return (((c * 4 + x) * 2 + k) * 4 + z) * 2 + y


def everyone():
    return [
        (c, x, k, z, y)
        for c in range(2)
        for x in range(4)
        for k in range(2)
        for z in range(4)
        for y in range(2)
    ]


def shift(v, dc=0, dx=0, dk=0, dz=0, dy=0):
    pairs = [
        (flat(c, x, k, z, y), flat(c ^ dc, (x + dx) % 4, k ^ dk, (z + dz) % 4, y ^ dy))
        for c, x, k, z, y in everyone()
    ]
    return lax.ppermute(v, AXES, pairs)


def encode(u):
    top = jnp.max(jnp.abs(u), axis=0, keepdims=True)
    code = jnp.ceil(jnp.log2(jnp.maximum(top, 1e-30)) * 128.0)
    scale = jnp.exp2(15.0 - code * (1.0 / 128.0)) * (32766.0 / 32768.0)
    return jnp.floor(u * scale + 0.5).astype(I32).astype(I16), code


def scale_rows(code):
    return jnp.broadcast_to(code, (CODE, code.shape[1])).astype(I32).astype(I16)


def as_float(q):
    return q.astype(I32).astype(F32)


def column_scale(codes, row=0):
    code = as_float(codes)[row : row + 1, :]
    return jnp.exp2(code * (1.0 / 128.0) - 15.0) * (32768.0 / 32766.0)


def update_kernel(
    ids, slots, pat, blk, pan, mine, other, front, send, diag, gcol, tile, sem, lines, lsem
):
    n = pl.program_id(0)
    ch, r, c, g = ids[0], ids[1], ids[2], ids[3]
    e = (ids[8], ids[9])
    j = lax.rem(ids[4] * 2 + n, CT)
    turn = n % 2
    si = [slots[ch, r * CT + i] for i in range(CT)]
    sj = slots[ch, c * CT + j]

    def leave(turn, j, act):
        for i in range(CT):
            act(
                pltpu.make_async_copy(
                    lines.at[turn, i],
                    send.at[si[i] // QT, :, pl.ds(pl.multiple_of(j * TILE, TILE), TILE)],
                    lsem.at[turn, i],
                )
            )

    @pl.when(n == 0)
    def _():
        diag[...] = jnp.zeros_like(diag)
        for a in range(2):
            for b in range(2):

                @pl.when((e[a] // RT == g) & (e[b] // QT == c))
                def _():
                    rows = pl.multiple_of((e[a] % RT) * TILE, TILE)
                    cols = pl.multiple_of((e[b] % QT) * TILE, TILE)
                    copy = pltpu.make_async_copy(
                        front.at[pl.ds(rows, TILE), pl.ds(cols, TILE)], tile, sem
                    )
                    copy.start()
                    copy.wait()
                    diag[a * TILE : (a + 1) * TILE, b * TILE : (b + 1) * TILE] = tile[...]

    @pl.when(n >= 2)
    def _():
        leave(turn, lax.rem(ids[4] * 2 + n - 2, CT), lambda copy: copy.wait())

    par = jnp.where(n < 2, mine[...], other[...])
    prod = lax.dot_general(pan[...], par, (((1,), (1,)), ((), ())), preferred_element_type=F32)
    for i in range(CT):
        rows = slice(i * TILE, (i + 1) * TILE)
        u = (blk[rows, :] - prod[rows, :]) * pat[ch, r * CT + i, c * CT + j].astype(F32)
        q, code = encode(u)
        lines[turn, i, 0:TILE, :] = q
        lines[turn, i, TILE:, :] = scale_rows(code)
        for b in range(2):
            at = slice(b * TILE, (b + 1) * TILE)

            @pl.when(sj == e[b])
            def _():
                gcol[rows, at] = u
                for a in range(2):

                    @pl.when(si[i] == e[a])
                    def _():
                        diag[a * TILE : (a + 1) * TILE, at] += u

    leave(turn, j, lambda copy: copy.start())

    @pl.when(n == CT - 1)
    def _():
        leave(1 - turn, lax.rem(ids[4] * 2 + n - 1, CT), lambda copy: copy.wait())
        leave(turn, j, lambda copy: copy.wait())


def update(ids, slots, pat, blk, pan, mine, other, front):
    def column(n, ids, slots, pat):
        return 0, lax.rem(ids[4] * 2 + n, CT)

    return pl.pallas_call(
        update_kernel,
        grid_spec=pltpu.PrefetchScalarGridSpec(
            num_scalar_prefetch=3,
            grid=(CT,),
            in_specs=[
                pl.BlockSpec((1024, TILE), column),
                pl.BlockSpec((1024, 1024), lambda n, *s: (0, 0)),
                pl.BlockSpec((TILE, 1024), lambda n, *s: (jnp.minimum(n, 1), 0)),
                pl.BlockSpec((TILE, 1024), lambda n, *s: (jnp.maximum(n - 2, 0), 0)),
                pl.BlockSpec(memory_space=pl.ANY),
            ],
            out_specs=[
                pl.BlockSpec(memory_space=pl.ANY),
                pl.BlockSpec((PANEL, PANEL), lambda n, *s: (0, 0)),
                pl.BlockSpec((CT * TILE, PANEL), lambda n, *s: (0, 0)),
            ],
            scratch_shapes=[
                pltpu.VMEM((TILE, TILE), F32),
                pltpu.SemaphoreType.DMA,
                pltpu.VMEM((2, CT, TILE + CODE, TILE), I16),
                pltpu.SemaphoreType.DMA((2, CT)),
            ],
        ),
        out_shape=[
            pltpu.HBM((8, TILE + CODE, 1024), I16),
            pltpu.HBM((PANEL, PANEL), F32),
            pltpu.HBM((CT * TILE, PANEL), F32),
        ],
        compiler_params=pltpu.CompilerParams(vmem_limit_bytes=48 * MIB),
        cost_estimate=pl.CostEstimate(flops=1 << 31, bytes_accessed=14 * MIB, transcendentals=0),
    )(ids, slots, pat, blk, pan, mine, other, front)


def strips_kernel(ids, gcol, front, *rest):
    outs, (wide, sem) = rest[:4], rest[4:]
    c, z = ids[2], ids[5]
    for a in range(2):
        e = ids[8 + a]

        @pl.when(e // QT == c)
        def _():
            at = pl.multiple_of((e % QT) * TILE, TILE)
            copy = pltpu.make_async_copy(
                front.at[:, pl.ds(at, TILE)], wide.at[:, pl.ds(a * TILE, TILE)], sem
            )
            copy.start()
            copy.wait()

    for d in range(4):
        for f in range(2):
            s = ((z + d) % 4) * 2 + f
            at = 0
            for ref, n in ((gcol, CT), (wide, RT)):
                parts = [
                    ref[pl.ds(pl.multiple_of(p * TILE + s * STRIP, STRIP), STRIP), :]
                    for p in range(n)
                ]
                q, code = encode(jnp.concatenate(parts, 0))
                outs[d][f, at : at + n * STRIP, :] = q
                outs[d][f, at + n * STRIP : at + n * STRIP + CODE, :] = scale_rows(code)
                at += n * STRIP + CODE


def strips(ids, gcol, front):
    return pl.pallas_call(
        strips_kernel,
        grid_spec=pltpu.PrefetchScalarGridSpec(
            num_scalar_prefetch=1,
            grid=(1,),
            in_specs=[
                pl.BlockSpec((CT * TILE, PANEL), lambda i, *s: (0, 0)),
                pl.BlockSpec(memory_space=pl.ANY),
            ],
            out_specs=[pl.BlockSpec((2, TILE, PANEL), lambda i, *s: (0, 0, 0))] * 4,
            scratch_shapes=[pltpu.VMEM((RT * TILE, PANEL), F32), pltpu.SemaphoreType.DMA],
        ),
        out_shape=[jax.ShapeDtypeStruct((2, TILE, PANEL), I16)] * 4,
        compiler_params=pltpu.CompilerParams(vmem_limit_bytes=24 * MIB),
        cost_estimate=pl.CostEstimate(flops=0, bytes_accessed=6 * MIB, transcendentals=0),
    )(ids, gcol, front)


CHILD_CODE = CT * STRIP
FRONT = CHILD_CODE + CODE
FRONT_CODE = FRONT + RT * STRIP


def regions(ids, where, child):
    for a in range(2):
        cols = slice(a * TILE, (a + 1) * TILE)
        yield slice(0, FRONT), cols, where[child, ids[8 + a]] // CT
        yield slice(FRONT, TILE), cols, ids[8 + a] // QT


def choose_z_kernel(ids, where, *refs):
    out, sems = refs[4], refs[5]

    def each(act):
        for n, (rows, cols, holder) in enumerate(regions(ids, where, ids[0])):
            for d in range(4):

                @pl.when(lax.rem(ids[5] - holder // 2 + 4, 4) == d)
                def _():
                    act(
                        pltpu.make_async_copy(
                            refs[d].at[:, rows, cols], out.at[:, rows, cols], sems.at[n]
                        )
                    )

    each(lambda copy: copy.start())
    each(lambda copy: copy.wait())


def choose_z(ids, where, parts):
    return pl.pallas_call(
        choose_z_kernel,
        grid_spec=pltpu.PrefetchScalarGridSpec(
            num_scalar_prefetch=2,
            grid=(1,),
            in_specs=[pl.BlockSpec(memory_space=pl.ANY)] * 4,
            out_specs=pl.BlockSpec((2, TILE, PANEL), lambda i, *s: (0, 0, 0)),
            scratch_shapes=[pltpu.SemaphoreType.DMA((4,))],
        ),
        out_shape=jax.ShapeDtypeStruct((2, TILE, PANEL), I16),
        cost_estimate=pl.CostEstimate(flops=0, bytes_accessed=MIB, transcendentals=0),
    )(ids, where, *parts)


def choose_y_kernel(ids, where, kept, beside, across, both, out, sems):
    def each(act):
        for n, (near, far) in enumerate(((kept, beside), (across, both))):
            child = lax.rem(ids[0] + n, 2)
            for m, (rows, cols, holder) in enumerate(regions(ids, where, child)):
                here = lax.rem(holder + 8, 2) == ids[6]
                for side, ref in ((True, near), (False, far)):

                    @pl.when(here == side)
                    def _():
                        act(
                            pltpu.make_async_copy(
                                ref.at[rows, cols], out.at[n, rows, cols], sems.at[n * 4 + m]
                            )
                        )

    each(lambda copy: copy.start())
    each(lambda copy: copy.wait())


def choose_y(ids, where, parts):
    return pl.pallas_call(
        choose_y_kernel,
        grid_spec=pltpu.PrefetchScalarGridSpec(
            num_scalar_prefetch=2,
            grid=(1,),
            in_specs=[pl.BlockSpec(memory_space=pl.ANY)] * 4,
            out_specs=pl.BlockSpec((2, TILE, PANEL), lambda i, *s: (0, 0, 0)),
            scratch_shapes=[pltpu.SemaphoreType.DMA((8,))],
        ),
        out_shape=jax.ShapeDtypeStruct((2, TILE, PANEL), I16),
        cost_estimate=pl.CostEstimate(flops=0, bytes_accessed=MIB, transcendentals=0),
    )(ids, where, *parts)


def compose_kernel(ids, where, own, other, out, acc, kept, kcode):
    q = pl.program_id(0)
    ch, core, k, x = ids[0], ids[4], ids[7], ids[10]
    half = lax.broadcasted_iota(I32, (STRIP, PANEL), 1) < TILE

    def group(q):
        first = q * QT + core * RT
        d, f = lax.rem(x - q % 4 + 4, 4), lax.rem(ch + q // 4, 2)
        acc[...] = as_float(own[d, f, FRONT:FRONT_CODE, :]) * column_scale(
            own[d, f, FRONT_CODE:, :]
        )
        for m in range(2):
            known = [(where[m, ids[8 + a]] >= 0).astype(I32) for a in range(2)]
            mask = jnp.where(half, known[0], known[1]) > 0
            for p in range(RT):
                i = where[m, first + p]
                for here, ref in ((True, own), (False, other)):

                    @pl.when((i >= 0) & (((i // CT) % 2 == core) == here))
                    def _():
                        dm, fm = lax.rem(x - i // 8 + 4, 4), lax.rem(ch + m, 2)
                        row = pl.multiple_of((i % CT) * STRIP, STRIP)
                        v = as_float(ref[dm, fm, pl.ds(row, STRIP), :]) * column_scale(
                            ref[dm, fm, CHILD_CODE:FRONT, :]
                        )
                        acc[p * STRIP : (p + 1) * STRIP, :] += jnp.where(mask, v, 0.0)

        return encode(acc[...])

    @pl.when(q == 0)
    def _():
        v, code = group(k)
        kept[...] = v
        kcode[...] = jnp.broadcast_to(code, kcode.shape)

    v, code = group(q)
    out[0, 0 : RT * STRIP, :] = kept[...]
    out[0, RT * STRIP : 2 * RT * STRIP, :] = v
    row = lax.broadcasted_iota(I32, (CODE, PANEL), 0)
    both = jnp.where(row == 0, kcode[0:1, :], code)
    out[0, 2 * RT * STRIP :, :] = both.astype(I32).astype(I16)


def compose(ids, where, own, other):
    whole = pl.BlockSpec((4, 2, TILE, PANEL), lambda i, *s: (0, 0, 0, 0))
    return pl.pallas_call(
        compose_kernel,
        grid_spec=pltpu.PrefetchScalarGridSpec(
            num_scalar_prefetch=2,
            grid=(8,),
            in_specs=[whole] * 2,
            out_specs=pl.BlockSpec((1, GROWS, PANEL), lambda i, *s: (i, 0, 0)),
            scratch_shapes=[
                pltpu.VMEM((RT * STRIP, PANEL), F32),
                pltpu.VMEM((RT * STRIP, PANEL), I16),
                pltpu.VMEM((8, PANEL), F32),
            ],
        ),
        out_shape=jax.ShapeDtypeStruct((8, GROWS, PANEL), I16),
        compiler_params=pltpu.CompilerParams(vmem_limit_bytes=24 * MIB),
        cost_estimate=pl.CostEstimate(flops=0, bytes_accessed=6 * MIB, transcendentals=0),
    )(ids, where, own, other)


def route_kernel(ids, slots, where, own, other, send, lines, codes, isem, osem, csem):
    c, g, core = ids[2], ids[3], ids[4]
    rows = [where[ch, g * RT + p] for ch in range(2) for p in range(RT)]
    to = [[slots[ch, c * CT + j] // QT for j in range(CT)] for ch in range(2)]

    def come(m, act):
        i = rows[m]
        src = (m // RT) * 4 + i // 8
        for here, buf in ((True, own), (False, other)):

            @pl.when((i >= 0) & (((i // CT) % 2 == core) == here))
            def _():
                act(pltpu.make_async_copy(buf.at[src], lines.at[m], isem.at[m]))

    def leave(m, act):
        @pl.when(rows[m] >= 0)
        def _():
            for j in range(CT):
                act(
                    pltpu.make_async_copy(
                        lines.at[m, pl.ds(0, TILE), pl.ds(j * TILE, TILE)],
                        send.at[to[m // RT][j], pl.ds(m * TILE, TILE), :],
                        osem.at[m * CT + j],
                    )
                )

    for m in range(2 * RT):
        come(m, lambda copy: copy.start())
    for m in range(2 * RT):
        come(m, lambda copy: copy.wait())
        leave(m, lambda copy: copy.start())
    line = lax.broadcasted_iota(I32, (CODE, TILE), 0)
    codes[...] = jnp.zeros_like(codes)
    for ch in range(2):
        for j in range(CT):
            q = to[ch][j]
            v = codes[q].astype(I32)
            for p in range(RT):
                m = ch * RT + p
                mine = lines[m, TILE:, j * TILE : (j + 1) * TILE].astype(I32)
                v = jnp.where(line == m, mine, v)
            codes[q] = v.astype(I16)
    tails = [
        pltpu.make_async_copy(codes.at[q], send.at[q, pl.ds(2 * RT * TILE, CODE), :], csem.at[q])
        for q in range(8)
    ]
    for copy in tails:
        copy.start()
    for m in range(2 * RT):
        leave(m, lambda copy: copy.wait())
    for copy in tails:
        copy.wait()


def route(ids, slots, where, own, other):
    return pl.pallas_call(
        route_kernel,
        grid_spec=pltpu.PrefetchScalarGridSpec(
            num_scalar_prefetch=3,
            grid=(1,),
            in_specs=[pl.BlockSpec(memory_space=pl.ANY)] * 2,
            out_specs=pl.BlockSpec(memory_space=pl.ANY),
            scratch_shapes=[
                pltpu.VMEM((2 * RT, TILE + CODE, 1024), I16),
                pltpu.VMEM((8, CODE, TILE), I16),
                pltpu.SemaphoreType.DMA((2 * RT,)),
                pltpu.SemaphoreType.DMA((2 * RT * CT,)),
                pltpu.SemaphoreType.DMA((8,)),
            ],
        ),
        out_shape=pltpu.HBM((8, CROWS, TILE), I16),
        compiler_params=pltpu.CompilerParams(vmem_limit_bytes=32 * MIB),
        cost_estimate=pl.CostEstimate(flops=0, bytes_accessed=8 * MIB, transcendentals=0),
    )(ids, slots, where, own, other)


def nt(a, b):
    return lax.dot_general(
        a, b, (((1,), (1,)), ((), ())), precision=HIGHEST, preferred_element_type=F32
    )


def nn(a, b):
    return lax.dot_general(
        a, b, (((1,), (0,)), ((), ())), precision=HIGHEST, preferred_element_type=F32
    )


NB = 64
WAYS = 8


def inverse_kernel(a_ref, out, w, f):
    n = PANEL // NB
    out[...] = jnp.zeros_like(out)
    row = lax.broadcasted_iota(I32, (NB, NB), 0)
    col = lax.broadcasted_iota(I32, (NB, NB), 1)
    eye = row == col
    lanes = lax.broadcasted_iota(I32, (1, 2 * NB), 1)
    sub = lax.broadcasted_iota(I32, (NB, 1), 0)

    def blk(i):
        return slice(i * NB, (i + 1) * NB)

    f[...] = a_ref[...]
    for k in range(n):
        w[:, :NB] = f[blk(k), blk(k)]
        w[:, NB:] = jnp.where(eye, 1.0, 0.0).astype(F32)

        def step(n4, _):
            j = n4 * WAYS
            lines = [w[pl.ds(j + a, 1), :] for a in range(WAYS)]
            square = w[:, :NB]
            columns = [
                jnp.sum(jnp.where(col == j + a, square, 0.0), axis=1, keepdims=True)
                for a in range(WAYS)
            ]
            small = [
                [
                    jnp.sum(jnp.where(lanes == j + b, lines[a], 0.0), axis=1, keepdims=True)
                    if b >= a
                    else None
                    for b in range(WAYS)
                ]
                for a in range(WAYS)
            ]
            factors = []
            for a in range(WAYS):
                inverse = 1.0 / small[a][a]
                for b in range(a + 1, WAYS):
                    times = small[a][b] * inverse
                    for d in range(b, WAYS):
                        small[b][d] = small[b][d] - times * small[a][d]
                    lines[b] = lines[b] - times * lines[a]
                    columns[b] = columns[b] - times * columns[a]
                factors.append(jnp.where(sub >= j + WAYS, columns[a] * inverse, 0.0))
            total = w[...]
            for a in range(WAYS):
                total = total - factors[a] * lines[a]
            w[...] = total
            for a in range(1, WAYS):
                w[pl.ds(j + a, 1), :] = lines[a]
            return 0

        lax.fori_loop(0, NB // WAYS, step, 0)
        d = jnp.sum(jnp.where(eye, w[:, :NB], 0.0), axis=1, keepdims=True)
        inv = w[:, NB:] * (1.0 / jnp.sqrt(d))
        out[blk(k), blk(k)] = inv
        rest = (k + 1) * NB
        if rest < PANEL:
            below = nt(f[rest:, blk(k)], inv)
            f[rest:, blk(k)] = below
            f[rest:, rest:] = f[rest:, rest:] - nt(below, below)
    for k in range(1, n):
        acc = nn(f[blk(k), : k * NB], out[: k * NB, : k * NB])
        out[blk(k), : k * NB] = -nn(out[blk(k), blk(k)], acc)


def inverse_factor(a):
    return pl.pallas_call(
        inverse_kernel,
        out_shape=jax.ShapeDtypeStruct((PANEL, PANEL), F32),
        scratch_shapes=[pltpu.VMEM((NB, 2 * NB), F32), pltpu.VMEM((PANEL, PANEL), F32)],
        compiler_params=pltpu.CompilerParams(vmem_limit_bytes=24 * MIB),
        cost_estimate=pl.CostEstimate(flops=1 << 34, bytes_accessed=2 * MIB, transcendentals=0),
    )(a)


def split(v):
    hi = v.astype(BF16)
    return hi, (v - hi.astype(F32)).astype(BF16)


def left3(v):
    hi, lo = split(v)
    return jnp.concatenate([hi, hi, lo], 1)


def right3(v):
    hi, lo = split(v)
    return jnp.concatenate([hi, lo, hi], 1)


def dot3(a, b):
    return lax.dot_general(a, b, (((1,), (1,)), ((), ())), preferred_element_type=F32)


def base_kernel(ids, where, recv, front, out, tiles, codes, tsem):
    t = pl.program_id(0)
    c, g = ids[2], ids[3]
    col = c * QT + t
    js = [where[ch, col] for ch in range(2)]
    there = [[where[ch, g * RT + p] >= 0 for p in range(RT)] for ch in range(2)]

    def each(act):
        for ch in range(2):
            src = js[ch] // CT

            @pl.when(js[ch] >= 0)
            def _():
                act(
                    pltpu.make_async_copy(
                        recv.at[src, pl.ds(2 * RT * TILE, CODE), :],
                        codes.at[ch],
                        tsem.at[2 * RT + ch],
                    )
                )

            for p in range(RT):
                m = ch * RT + p

                @pl.when(there[ch][p] & (js[ch] >= 0))
                def _():
                    act(
                        pltpu.make_async_copy(
                            recv.at[src, pl.ds(m * TILE, TILE), :], tiles.at[m], tsem.at[m]
                        )
                    )

    each(lambda copy: copy.start())

    out[...] = front[...]
    each(lambda copy: copy.wait())
    for p in range(RT):
        rows = slice(p * TILE, (p + 1) * TILE)
        for ch in range(2):
            m = ch * RT + p

            @pl.when(there[ch][p] & (js[ch] >= 0))
            def _():
                out[rows, :] += as_float(tiles[m]) * column_scale(codes[ch], m)


def base(ids, where, recv, front):
    line = pl.BlockSpec((RT * TILE, TILE), lambda i, *s: (0, i))
    return pl.pallas_call(
        base_kernel,
        grid_spec=pltpu.PrefetchScalarGridSpec(
            num_scalar_prefetch=2,
            grid=(QT,),
            in_specs=[pl.BlockSpec(memory_space=pl.ANY), line],
            out_specs=line,
            scratch_shapes=[
                pltpu.VMEM((2 * RT, TILE, TILE), I16),
                pltpu.VMEM((2, CODE, TILE), I16),
                pltpu.SemaphoreType.DMA((2 * RT + 2,)),
            ],
        ),
        out_shape=jax.ShapeDtypeStruct((RT * TILE, QT * TILE), F32),
        compiler_params=pltpu.CompilerParams(vmem_limit_bytes=24 * MIB),
        cost_estimate=pl.CostEstimate(flops=0, bytes_accessed=20 * MIB, transcendentals=0),
    )(ids, where, recv, front)


def final_kernel(
    ids, diag, inv, gx, goth, front, out,
    gbuf, rows_f, left, inverse,
):
    t = pl.program_id(0)
    c, g, core = ids[2], ids[3], ids[4]
    col = c * QT + t
    @pl.when(t == 0)
    def _():
        inverse[...] = right3(inv[...])
        for s in range(8):
            scale = column_scale(gx[s, 2 * RT * STRIP :, :], 0)
            v = as_float(gx[s, 0 : RT * STRIP, :]) * scale
            for p in range(RT):
                gbuf[p * TILE + s * STRIP : p * TILE + (s + 1) * STRIP, :] = v[
                    p * STRIP : (p + 1) * STRIP, :
                ]
        for p in range(RT):
            for a in range(2):

                @pl.when(g * RT + p == ids[8 + a])
                def _():
                    gbuf[p * TILE : (p + 1) * TILE, :] = diag[a * TILE : (a + 1) * TILE, :]

        v = dot3(left3(gbuf[...]), inverse[...])
        rows_f[...] = v
        left[...] = left3(v)

    side = pl.multiple_of((t % RT) * STRIP, STRIP)

    @pl.when(t // RT == core)
    def _():
        for s in range(8):
            gbuf[s * STRIP : (s + 1) * STRIP, :] = as_float(
                gx[s, pl.ds(RT * STRIP + side, STRIP), :]
            ) * column_scale(gx[s, 2 * RT * STRIP :, :], 1)

    @pl.when(t // RT != core)
    def _():
        for s in range(8):
            gbuf[s * STRIP : (s + 1) * STRIP, :] = as_float(
                goth[s, pl.ds(side, STRIP), :]
            ) * column_scale(goth[s, RT * STRIP :, :], 1)

    for a in range(2):

        @pl.when(col == ids[8 + a])
        def _():
            gbuf[0:TILE, :] = diag[a * TILE : (a + 1) * TILE, :]

    right = right3(dot3(left3(gbuf[0:TILE, :]), inverse[...]))
    out[...] = front[...] - dot3(left[...], right)
    for a in range(2):

        @pl.when(col == ids[8 + a])
        def _():
            out[...] = rows_f[:, a * TILE : (a + 1) * TILE]


def final(ids, diag, inv, gx, goth, front):
    def whole(*shape):
        return pl.BlockSpec(shape, lambda i, *s: (0,) * len(shape))

    line = pl.BlockSpec((RT * TILE, TILE), lambda i, *s: (0, i))
    return pl.pallas_call(
        final_kernel,
        grid_spec=pltpu.PrefetchScalarGridSpec(
            num_scalar_prefetch=1,
            grid=(QT,),
            in_specs=[
                whole(PANEL, PANEL),
                whole(PANEL, PANEL),
                whole(8, GROWS, PANEL),
                whole(8, GROWS - RT * STRIP, PANEL),
                line,
            ],
            out_specs=line,
            scratch_shapes=[
                pltpu.VMEM((RT * TILE, PANEL), F32),
                pltpu.VMEM((RT * TILE, PANEL), F32),
                pltpu.VMEM((RT * TILE, 3 * PANEL), BF16),
                pltpu.VMEM((PANEL, 3 * PANEL), BF16),
            ],
        ),
        out_shape=jax.ShapeDtypeStruct((RT * TILE, QT * TILE), F32),
        compiler_params=pltpu.CompilerParams(vmem_limit_bytes=52 * MIB),
        cost_estimate=pl.CostEstimate(flops=1 << 33, bytes_accessed=20 * MIB, transcendentals=0),
    )(ids, diag, inv, gx, goth, front)


def pick(v, at):
    return lax.dynamic_index_in_dim(v, at, 0, keepdims=False)


def fetch_partner(panel, x, core, z, yh):
    halves = panel.reshape(2, 512, 1024)
    piece = pick(halves, ((z - x + 4) % 4) // 2)
    came = []
    for dx in (1, 2, 3):
        pairs = [
            (flat(c, xs, y, (xs + 2 * b) % 4, y), flat(c, (xs + dx) % 4, b, xs, y))
            for c in range(2)
            for xs in range(4)
            for y in range(2)
            for b in range(2)
        ]
        came.append(lax.ppermute(piece, AXES, pairs))
    pairs = [
        (flat(c, x, y, x, y), flat(c, x, 1 - y, x, y))
        for c in range(2)
        for x in range(4)
        for y in range(2)
    ]
    beside = lax.ppermute(pick(halves, 1 - core), AXES, pairs)
    way = (x - z + 4) % 4
    mine = jnp.where(way == 1, came[0], jnp.where(way == 2, came[1], came[2]))
    mine = jnp.where(way == 0, jnp.where(core == yh, pick(halves, core), beside), mine)
    return mine, shift(mine, dk=1)


def sum_first(v, core, z):
    v = v.reshape(2, 256, PANEL)
    v = pick(v, core) + shift(pick(v, 1 - core), dk=1)
    v = v.reshape(4, 64, PANEL)
    got = [shift(pick(v, (z + d) % 4), dz=d) for d in (1, 3, 2)]
    return pick(v, z) + got[0] + got[1] + got[2]


def gathered(v, at, **axis):
    (name,) = axis
    full = jnp.zeros((4,) + v.shape, v.dtype)
    full = lax.dynamic_update_index_in_dim(full, v, at, 0)
    for d in (1, 3, 2):
        full = lax.dynamic_update_index_in_dim(full, shift(v, **{name: d}), (at - d) % 4, 0)
    return full


def sum_x(v, x):
    v = v.reshape(4, 64, PANEL)
    got = [shift(pick(v, (x + d) % 4), dx=d) for d in (1, 3, 2)]
    return pick(v, x) + got[0] + got[1] + got[2]


def sum_y(v):
    return (v + shift(v, dc=1, dy=1)) + (shift(v, dc=1) + shift(v, dy=1))


def join_cores(v, core):
    other = shift(v, dk=1)
    return jnp.concatenate([jnp.where(core == 0, v, other), jnp.where(core == 0, other, v)])


def tables(child_maps, parent_place):
    hit = child_maps[:, :, None] == jnp.arange(48, dtype=I32)
    slots = jnp.sum(jnp.where(hit, parent_place, 0), axis=2)
    hit = slots[:, :, None] == jnp.arange(48, dtype=I32)
    where = jnp.max(jnp.where(hit, jnp.arange(32, dtype=I32)[None, :, None], -1), axis=1)
    return slots, where


def body(child_blocks, child_panels, child_patterns, child_maps, parent_place, parent_front):
    ch, x, core, z, yh = (lax.axis_index(n).astype(I32) for n in AXES)
    r, c = x * 2 + core, z * 2 + yh
    slots, where = tables(child_maps, parent_place)
    e = parent_place[0], parent_place[1]
    ids = jnp.stack([ch, r, c, ch * 8 + r, core, z, yh, ch * 4 + x, e[0], e[1], x])
    panel = child_panels[0]
    parent_front = pltpu.with_memory_space_constraint(parent_front, pltpu.HBM)
    block = pltpu.with_memory_space_constraint(child_blocks[0], pltpu.HBM)
    mine, theirs = fetch_partner(panel, x, core, z, yh)
    mine, theirs, ids, slots, where = lax.optimization_barrier((mine, theirs, ids, slots, where))
    send, diag, gcol = update(
        ids, slots, child_patterns, block, panel, mine, theirs, parent_front
    )
    own = lax.all_to_all(send, ("child", "x"), split_axis=0, concat_axis=0, tiled=True)

    diag = sum_first(diag, core, z)
    diag, gcol = lax.optimization_barrier((diag, gcol))
    parts = strips(ids, gcol, parent_front)
    parts = [parts[0]] + [shift(parts[d], dz=d) for d in range(1, 4)]
    diag = gathered(diag, z, dz=0).reshape(256, PANEL)
    strip = choose_z(ids, where, parts)
    own, diag, strip = lax.optimization_barrier((own, diag, strip))

    other = shift(own, dk=1)
    send = route(ids, slots, where, own, other)
    kept, moved = pick(strip, yh), pick(strip, 1 - yh)
    moves = [shift(moved, dy=1), shift(kept, dc=1), shift(moved, dc=1, dy=1)]
    diag, *moves = lax.optimization_barrier((sum_x(diag, x), *moves))
    diag = sum_y(diag)
    send, diag, kept, *moves = lax.optimization_barrier((send, diag, kept, *moves))
    recv = lax.all_to_all(send, ("z", "yh"), split_axis=0, concat_axis=0, tiled=True)

    diag = gathered(diag, x, dx=0).reshape(256, PANEL)
    diag, kept, *moves = lax.optimization_barrier((diag, kept, *moves))
    strip = choose_y(ids, where, [kept] + moves)
    diag = join_cores(diag, core)
    line = jnp.stack([strip] + [shift(strip, dx=d) for d in range(1, 4)])
    inv = inverse_factor(diag)
    gsend = compose(ids, where, line, shift(line, dk=1))
    recv, inv, gsend = lax.optimization_barrier((recv, inv, gsend))
    gx = lax.all_to_all(gsend, ("z", "yh"), split_axis=0, concat_axis=0, tiled=True)
    with_children = base(ids, where, recv, parent_front)
    gx, with_children = lax.optimization_barrier((gx, with_children))
    goth = shift(gx[:, RT * STRIP :], dk=1)
    return final(ids, diag, inv, gx, goth, with_children)


def solution(mesh):
    fine = Mesh(mesh.devices.reshape(SIZES), AXES)
    rows, cols = ("x", "core"), ("z", "yh")
    return jax.shard_map(
        body,
        mesh=fine,
        in_specs=(
            P("child", rows, cols),
            P("child", rows, None),
            P(),
            P(),
            P(),
            P(("child", "x", "core"), cols),
        ),
        out_specs=P(("child", "x", "core"), cols),
        check_vma=False,
    )
```

```python
import jax
import jax.numpy as jnp
from jax import lax
from jax.experimental import pallas as pl
from jax.experimental.pallas import tpu as pltpu
from jax.sharding import Mesh
from jax.sharding import PartitionSpec as P

TILE = 256
PANEL = 512
CODE = 16
CT = 4
RT = 3
QT = 6
STRIP = 32
GROWS = 2 * RT * STRIP + CODE
CROWS = 2 * RT * TILE + CODE
AXES = ("child", "x", "core", "z", "yh")
SIZES = (2, 4, 2, 4, 2)
MIB = 1 << 20
F32 = jnp.float32
I32 = jnp.int32
I16 = jnp.int16
BF16 = jnp.bfloat16
HIGHEST = lax.Precision.HIGHEST


def flat(c, x, k, z, y):
    return (((c * 4 + x) * 2 + k) * 4 + z) * 2 + y


def everyone():
    return [
        (c, x, k, z, y)
        for c in range(2)
        for x in range(4)
        for k in range(2)
        for z in range(4)
        for y in range(2)
    ]


def shift(v, dc=0, dx=0, dk=0, dz=0, dy=0):
    pairs = [
        (flat(c, x, k, z, y), flat(c ^ dc, (x + dx) % 4, k ^ dk, (z + dz) % 4, y ^ dy))
        for c, x, k, z, y in everyone()
    ]
    return lax.ppermute(v, AXES, pairs)


def encode(u):
    top = jnp.max(jnp.abs(u), axis=0, keepdims=True)
    code = jnp.ceil(jnp.log2(jnp.maximum(top, 1e-30)) * 128.0)
    scale = jnp.exp2(15.0 - code * (1.0 / 128.0)) * (32766.0 / 32768.0)
    return jnp.floor(u * scale + 0.5).astype(I32).astype(I16), code


def scale_rows(code):
    return jnp.broadcast_to(code, (CODE, code.shape[1])).astype(I32).astype(I16)


def as_float(q):
    return q.astype(I32).astype(F32)


def column_scale(codes, row=0):
    code = as_float(codes)[row : row + 1, :]
    return jnp.exp2(code * (1.0 / 128.0) - 15.0) * (32768.0 / 32766.0)


def update_kernel(
    ids, slots, pat, blk, pan, mine, other, front, send, diag, gcol, tile, sem, lines, lsem
):
    n = pl.program_id(0)
    ch, r, c, g = ids[0], ids[1], ids[2], ids[3]
    e = (ids[8], ids[9])
    j = lax.rem(ids[4] * 2 + n, CT)
    turn = n % 2
    si = [slots[ch, r * CT + i] for i in range(CT)]
    sj = slots[ch, c * CT + j]

    def leave(turn, j, act):
        for i in range(CT):
            act(
                pltpu.make_async_copy(
                    lines.at[turn, i],
                    send.at[si[i] // QT, :, pl.ds(pl.multiple_of(j * TILE, TILE), TILE)],
                    lsem.at[turn, i],
                )
            )

    @pl.when(n == 0)
    def _():
        diag[...] = jnp.zeros_like(diag)
        for a in range(2):
            for b in range(2):

                @pl.when((e[a] // RT == g) & (e[b] // QT == c))
                def _():
                    rows = pl.multiple_of((e[a] % RT) * TILE, TILE)
                    cols = pl.multiple_of((e[b] % QT) * TILE, TILE)
                    copy = pltpu.make_async_copy(
                        front.at[pl.ds(rows, TILE), pl.ds(cols, TILE)], tile, sem
                    )
                    copy.start()
                    copy.wait()
                    diag[a * TILE : (a + 1) * TILE, b * TILE : (b + 1) * TILE] = tile[...]

    @pl.when(n >= 2)
    def _():
        leave(turn, lax.rem(ids[4] * 2 + n - 2, CT), lambda copy: copy.wait())

    par = jnp.where(n < 2, mine[...], other[...])
    prod = lax.dot_general(pan[...], par, (((1,), (1,)), ((), ())), preferred_element_type=F32)
    for i in range(CT):
        rows = slice(i * TILE, (i + 1) * TILE)
        u = (blk[rows, :] - prod[rows, :]) * pat[ch, r * CT + i, c * CT + j].astype(F32)
        q, code = encode(u)
        lines[turn, i, 0:TILE, :] = q
        lines[turn, i, TILE:, :] = scale_rows(code)
        for b in range(2):
            at = slice(b * TILE, (b + 1) * TILE)

            @pl.when(sj == e[b])
            def _():
                gcol[rows, at] = u
                for a in range(2):

                    @pl.when(si[i] == e[a])
                    def _():
                        diag[a * TILE : (a + 1) * TILE, at] += u

    leave(turn, j, lambda copy: copy.start())

    @pl.when(n == CT - 1)
    def _():
        leave(1 - turn, lax.rem(ids[4] * 2 + n - 1, CT), lambda copy: copy.wait())
        leave(turn, j, lambda copy: copy.wait())


def update(ids, slots, pat, blk, pan, mine, other, front):
    def column(n, ids, slots, pat):
        return 0, lax.rem(ids[4] * 2 + n, CT)

    return pl.pallas_call(
        update_kernel,
        grid_spec=pltpu.PrefetchScalarGridSpec(
            num_scalar_prefetch=3,
            grid=(CT,),
            in_specs=[
                pl.BlockSpec((1024, TILE), column),
                pl.BlockSpec((1024, 1024), lambda n, *s: (0, 0)),
                pl.BlockSpec((TILE, 1024), lambda n, *s: (jnp.minimum(n, 1), 0)),
                pl.BlockSpec((TILE, 1024), lambda n, *s: (jnp.maximum(n - 2, 0), 0)),
                pl.BlockSpec(memory_space=pl.ANY),
            ],
            out_specs=[
                pl.BlockSpec(memory_space=pl.ANY),
                pl.BlockSpec((PANEL, PANEL), lambda n, *s: (0, 0)),
                pl.BlockSpec((CT * TILE, PANEL), lambda n, *s: (0, 0)),
            ],
            scratch_shapes=[
                pltpu.VMEM((TILE, TILE), F32),
                pltpu.SemaphoreType.DMA,
                pltpu.VMEM((2, CT, TILE + CODE, TILE), I16),
                pltpu.SemaphoreType.DMA((2, CT)),
            ],
        ),
        out_shape=[
            pltpu.HBM((8, TILE + CODE, 1024), I16),
            pltpu.HBM((PANEL, PANEL), F32),
            pltpu.HBM((CT * TILE, PANEL), F32),
        ],
        compiler_params=pltpu.CompilerParams(vmem_limit_bytes=48 * MIB),
        cost_estimate=pl.CostEstimate(flops=1 << 31, bytes_accessed=14 * MIB, transcendentals=0),
    )(ids, slots, pat, blk, pan, mine, other, front)


def strips_kernel(ids, gcol, front, *rest):
    outs, (wide, sem) = rest[:4], rest[4:]
    c, z = ids[2], ids[5]
    for a in range(2):
        e = ids[8 + a]

        @pl.when(e // QT == c)
        def _():
            at = pl.multiple_of((e % QT) * TILE, TILE)
            copy = pltpu.make_async_copy(
                front.at[:, pl.ds(at, TILE)], wide.at[:, pl.ds(a * TILE, TILE)], sem
            )
            copy.start()
            copy.wait()

    for d in range(4):
        for f in range(2):
            s = ((z + d) % 4) * 2 + f
            at = 0
            for ref, n in ((gcol, CT), (wide, RT)):
                parts = [
                    ref[pl.ds(pl.multiple_of(p * TILE + s * STRIP, STRIP), STRIP), :]
                    for p in range(n)
                ]
                q, code = encode(jnp.concatenate(parts, 0))
                outs[d][f, at : at + n * STRIP, :] = q
                outs[d][f, at + n * STRIP : at + n * STRIP + CODE, :] = scale_rows(code)
                at += n * STRIP + CODE


def strips(ids, gcol, front):
    return pl.pallas_call(
        strips_kernel,
        grid_spec=pltpu.PrefetchScalarGridSpec(
            num_scalar_prefetch=1,
            grid=(1,),
            in_specs=[
                pl.BlockSpec((CT * TILE, PANEL), lambda i, *s: (0, 0)),
                pl.BlockSpec(memory_space=pl.ANY),
            ],
            out_specs=[pl.BlockSpec((2, TILE, PANEL), lambda i, *s: (0, 0, 0))] * 4,
            scratch_shapes=[pltpu.VMEM((RT * TILE, PANEL), F32), pltpu.SemaphoreType.DMA],
        ),
        out_shape=[jax.ShapeDtypeStruct((2, TILE, PANEL), I16)] * 4,
        compiler_params=pltpu.CompilerParams(vmem_limit_bytes=24 * MIB),
        cost_estimate=pl.CostEstimate(flops=0, bytes_accessed=6 * MIB, transcendentals=0),
    )(ids, gcol, front)


CHILD_CODE = CT * STRIP
FRONT = CHILD_CODE + CODE
FRONT_CODE = FRONT + RT * STRIP


def regions(ids, where, child):
    for a in range(2):
        cols = slice(a * TILE, (a + 1) * TILE)
        yield slice(0, FRONT), cols, where[child, ids[8 + a]] // CT
        yield slice(FRONT, TILE), cols, ids[8 + a] // QT


def choose_z_kernel(ids, where, *refs):
    out, sems = refs[4], refs[5]

    def each(act):
        for n, (rows, cols, holder) in enumerate(regions(ids, where, ids[0])):
            for d in range(4):

                @pl.when(lax.rem(ids[5] - holder // 2 + 4, 4) == d)
                def _():
                    act(
                        pltpu.make_async_copy(
                            refs[d].at[:, rows, cols], out.at[:, rows, cols], sems.at[n]
                        )
                    )

    each(lambda copy: copy.start())
    each(lambda copy: copy.wait())


def choose_z(ids, where, parts):
    return pl.pallas_call(
        choose_z_kernel,
        grid_spec=pltpu.PrefetchScalarGridSpec(
            num_scalar_prefetch=2,
            grid=(1,),
            in_specs=[pl.BlockSpec(memory_space=pl.ANY)] * 4,
            out_specs=pl.BlockSpec((2, TILE, PANEL), lambda i, *s: (0, 0, 0)),
            scratch_shapes=[pltpu.SemaphoreType.DMA((4,))],
        ),
        out_shape=jax.ShapeDtypeStruct((2, TILE, PANEL), I16),
        cost_estimate=pl.CostEstimate(flops=0, bytes_accessed=MIB, transcendentals=0),
    )(ids, where, *parts)


def choose_y_kernel(ids, where, kept, beside, across, both, out, sems):
    def each(act):
        for n, (near, far) in enumerate(((kept, beside), (across, both))):
            child = lax.rem(ids[0] + n, 2)
            for m, (rows, cols, holder) in enumerate(regions(ids, where, child)):
                here = lax.rem(holder + 8, 2) == ids[6]
                for side, ref in ((True, near), (False, far)):

                    @pl.when(here == side)
                    def _():
                        act(
                            pltpu.make_async_copy(
                                ref.at[rows, cols], out.at[n, rows, cols], sems.at[n * 4 + m]
                            )
                        )

    each(lambda copy: copy.start())
    each(lambda copy: copy.wait())


def choose_y(ids, where, parts):
    return pl.pallas_call(
        choose_y_kernel,
        grid_spec=pltpu.PrefetchScalarGridSpec(
            num_scalar_prefetch=2,
            grid=(1,),
            in_specs=[pl.BlockSpec(memory_space=pl.ANY)] * 4,
            out_specs=pl.BlockSpec((2, TILE, PANEL), lambda i, *s: (0, 0, 0)),
            scratch_shapes=[pltpu.SemaphoreType.DMA((8,))],
        ),
        out_shape=jax.ShapeDtypeStruct((2, TILE, PANEL), I16),
        cost_estimate=pl.CostEstimate(flops=0, bytes_accessed=MIB, transcendentals=0),
    )(ids, where, *parts)


def compose_kernel(ids, where, own, other, out, acc, kept, kcode):
    q = pl.program_id(0)
    ch, core, k, x = ids[0], ids[4], ids[7], ids[10]
    half = lax.broadcasted_iota(I32, (STRIP, PANEL), 1) < TILE

    def group(q):
        first = q * QT + core * RT
        d, f = lax.rem(x - q % 4 + 4, 4), lax.rem(ch + q // 4, 2)
        acc[...] = as_float(own[d, f, FRONT:FRONT_CODE, :]) * column_scale(
            own[d, f, FRONT_CODE:, :]
        )
        for m in range(2):
            known = [(where[m, ids[8 + a]] >= 0).astype(I32) for a in range(2)]
            mask = jnp.where(half, known[0], known[1]) > 0
            for p in range(RT):
                i = where[m, first + p]
                for here, ref in ((True, own), (False, other)):

                    @pl.when((i >= 0) & (((i // CT) % 2 == core) == here))
                    def _():
                        dm, fm = lax.rem(x - i // 8 + 4, 4), lax.rem(ch + m, 2)
                        row = pl.multiple_of((i % CT) * STRIP, STRIP)
                        v = as_float(ref[dm, fm, pl.ds(row, STRIP), :]) * column_scale(
                            ref[dm, fm, CHILD_CODE:FRONT, :]
                        )
                        acc[p * STRIP : (p + 1) * STRIP, :] += jnp.where(mask, v, 0.0)

        return encode(acc[...])

    @pl.when(q == 0)
    def _():
        v, code = group(k)
        kept[...] = v
        kcode[...] = jnp.broadcast_to(code, kcode.shape)

    v, code = group(q)
    out[0, 0 : RT * STRIP, :] = kept[...]
    out[0, RT * STRIP : 2 * RT * STRIP, :] = v
    row = lax.broadcasted_iota(I32, (CODE, PANEL), 0)
    both = jnp.where(row == 0, kcode[0:1, :], code)
    out[0, 2 * RT * STRIP :, :] = both.astype(I32).astype(I16)


def compose(ids, where, own, other):
    whole = pl.BlockSpec((4, 2, TILE, PANEL), lambda i, *s: (0, 0, 0, 0))
    return pl.pallas_call(
        compose_kernel,
        grid_spec=pltpu.PrefetchScalarGridSpec(
            num_scalar_prefetch=2,
            grid=(8,),
            in_specs=[whole] * 2,
            out_specs=pl.BlockSpec((1, GROWS, PANEL), lambda i, *s: (i, 0, 0)),
            scratch_shapes=[
                pltpu.VMEM((RT * STRIP, PANEL), F32),
                pltpu.VMEM((RT * STRIP, PANEL), I16),
                pltpu.VMEM((8, PANEL), F32),
            ],
        ),
        out_shape=jax.ShapeDtypeStruct((8, GROWS, PANEL), I16),
        compiler_params=pltpu.CompilerParams(vmem_limit_bytes=24 * MIB),
        cost_estimate=pl.CostEstimate(flops=0, bytes_accessed=6 * MIB, transcendentals=0),
    )(ids, where, own, other)


def route_kernel(ids, slots, where, own, other, send, lines, codes, isem, osem, csem):
    c, g, core = ids[2], ids[3], ids[4]
    rows = [where[ch, g * RT + p] for ch in range(2) for p in range(RT)]
    to = [[slots[ch, c * CT + j] // QT for j in range(CT)] for ch in range(2)]

    def come(m, act):
        i = rows[m]
        src = (m // RT) * 4 + i // 8
        for here, buf in ((True, own), (False, other)):

            @pl.when((i >= 0) & (((i // CT) % 2 == core) == here))
            def _():
                act(pltpu.make_async_copy(buf.at[src], lines.at[m], isem.at[m]))

    def leave(m, act):
        @pl.when(rows[m] >= 0)
        def _():
            for j in range(CT):
                act(
                    pltpu.make_async_copy(
                        lines.at[m, pl.ds(0, TILE), pl.ds(j * TILE, TILE)],
                        send.at[to[m // RT][j], pl.ds(m * TILE, TILE), :],
                        osem.at[m * CT + j],
                    )
                )

    for m in range(2 * RT):
        come(m, lambda copy: copy.start())
    for m in range(2 * RT):
        come(m, lambda copy: copy.wait())
        leave(m, lambda copy: copy.start())
    line = lax.broadcasted_iota(I32, (CODE, TILE), 0)
    codes[...] = jnp.zeros_like(codes)
    for ch in range(2):
        for j in range(CT):
            q = to[ch][j]
            v = codes[q].astype(I32)
            for p in range(RT):
                m = ch * RT + p
                mine = lines[m, TILE:, j * TILE : (j + 1) * TILE].astype(I32)
                v = jnp.where(line == m, mine, v)
            codes[q] = v.astype(I16)
    tails = [
        pltpu.make_async_copy(codes.at[q], send.at[q, pl.ds(2 * RT * TILE, CODE), :], csem.at[q])
        for q in range(8)
    ]
    for copy in tails:
        copy.start()
    for m in range(2 * RT):
        leave(m, lambda copy: copy.wait())
    for copy in tails:
        copy.wait()


def route(ids, slots, where, own, other):
    return pl.pallas_call(
        route_kernel,
        grid_spec=pltpu.PrefetchScalarGridSpec(
            num_scalar_prefetch=3,
            grid=(1,),
            in_specs=[pl.BlockSpec(memory_space=pl.ANY)] * 2,
            out_specs=pl.BlockSpec(memory_space=pl.ANY),
            scratch_shapes=[
                pltpu.VMEM((2 * RT, TILE + CODE, 1024), I16),
                pltpu.VMEM((8, CODE, TILE), I16),
                pltpu.SemaphoreType.DMA((2 * RT,)),
                pltpu.SemaphoreType.DMA((2 * RT * CT,)),
                pltpu.SemaphoreType.DMA((8,)),
            ],
        ),
        out_shape=pltpu.HBM((8, CROWS, TILE), I16),
        compiler_params=pltpu.CompilerParams(vmem_limit_bytes=32 * MIB),
        cost_estimate=pl.CostEstimate(flops=0, bytes_accessed=8 * MIB, transcendentals=0),
    )(ids, slots, where, own, other)


def nt(a, b):
    return lax.dot_general(
        a, b, (((1,), (1,)), ((), ())), precision=HIGHEST, preferred_element_type=F32
    )


def nn(a, b):
    return lax.dot_general(
        a, b, (((1,), (0,)), ((), ())), precision=HIGHEST, preferred_element_type=F32
    )


NB = 64
WAYS = 8


def inverse_kernel(a_ref, out, w, f):
    n = PANEL // NB
    out[...] = jnp.zeros_like(out)
    row = lax.broadcasted_iota(I32, (NB, NB), 0)
    col = lax.broadcasted_iota(I32, (NB, NB), 1)
    eye = row == col
    lanes = lax.broadcasted_iota(I32, (1, 2 * NB), 1)
    sub = lax.broadcasted_iota(I32, (NB, 1), 0)

    def blk(i):
        return slice(i * NB, (i + 1) * NB)

    f[...] = a_ref[...]
    for k in range(n):
        w[:, :NB] = f[blk(k), blk(k)]
        w[:, NB:] = jnp.where(eye, 1.0, 0.0).astype(F32)

        def step(n4, _):
            j = n4 * WAYS
            lines = [w[pl.ds(j + a, 1), :] for a in range(WAYS)]
            square = w[:, :NB]
            columns = [
                jnp.sum(jnp.where(col == j + a, square, 0.0), axis=1, keepdims=True)
                for a in range(WAYS)
            ]
            small = [
                [
                    jnp.sum(jnp.where(lanes == j + b, lines[a], 0.0), axis=1, keepdims=True)
                    if b >= a
                    else None
                    for b in range(WAYS)
                ]
                for a in range(WAYS)
            ]
            factors = []
            for a in range(WAYS):
                inverse = 1.0 / small[a][a]
                for b in range(a + 1, WAYS):
                    times = small[a][b] * inverse
                    for d in range(b, WAYS):
                        small[b][d] = small[b][d] - times * small[a][d]
                    lines[b] = lines[b] - times * lines[a]
                    columns[b] = columns[b] - times * columns[a]
                factors.append(jnp.where(sub >= j + WAYS, columns[a] * inverse, 0.0))
            total = w[...]
            for a in range(WAYS):
                total = total - factors[a] * lines[a]
            w[...] = total
            for a in range(1, WAYS):
                w[pl.ds(j + a, 1), :] = lines[a]
            return 0

        lax.fori_loop(0, NB // WAYS, step, 0)
        d = jnp.sum(jnp.where(eye, w[:, :NB], 0.0), axis=1, keepdims=True)
        inv = w[:, NB:] * (1.0 / jnp.sqrt(d))
        out[blk(k), blk(k)] = inv
        rest = (k + 1) * NB
        if rest < PANEL:
            below = nt(f[rest:, blk(k)], inv)
            f[rest:, blk(k)] = below
            f[rest:, rest:] = f[rest:, rest:] - nt(below, below)
    for k in range(1, n):
        acc = nn(f[blk(k), : k * NB], out[: k * NB, : k * NB])
        out[blk(k), : k * NB] = -nn(out[blk(k), blk(k)], acc)


def inverse_factor(a):
    return pl.pallas_call(
        inverse_kernel,
        out_shape=jax.ShapeDtypeStruct((PANEL, PANEL), F32),
        scratch_shapes=[pltpu.VMEM((NB, 2 * NB), F32), pltpu.VMEM((PANEL, PANEL), F32)],
        compiler_params=pltpu.CompilerParams(vmem_limit_bytes=24 * MIB),
        cost_estimate=pl.CostEstimate(flops=1 << 34, bytes_accessed=2 * MIB, transcendentals=0),
    )(a)


def split(v):
    hi = v.astype(BF16)
    return hi, (v - hi.astype(F32)).astype(BF16)


def left3(v):
    hi, lo = split(v)
    return jnp.concatenate([hi, hi, lo], 1)


def right3(v):
    hi, lo = split(v)
    return jnp.concatenate([hi, lo, hi], 1)


def dot3(a, b):
    return lax.dot_general(a, b, (((1,), (1,)), ((), ())), preferred_element_type=F32)


def base_kernel(ids, where, recv, front, out, tiles, codes, tsem):
    t = pl.program_id(0)
    c, g = ids[2], ids[3]
    col = c * QT + t
    js = [where[ch, col] for ch in range(2)]
    there = [[where[ch, g * RT + p] >= 0 for p in range(RT)] for ch in range(2)]

    def each(act):
        for ch in range(2):
            src = js[ch] // CT

            @pl.when(js[ch] >= 0)
            def _():
                act(
                    pltpu.make_async_copy(
                        recv.at[src, pl.ds(2 * RT * TILE, CODE), :],
                        codes.at[ch],
                        tsem.at[2 * RT + ch],
                    )
                )

            for p in range(RT):
                m = ch * RT + p

                @pl.when(there[ch][p] & (js[ch] >= 0))
                def _():
                    act(
                        pltpu.make_async_copy(
                            recv.at[src, pl.ds(m * TILE, TILE), :], tiles.at[m], tsem.at[m]
                        )
                    )

    each(lambda copy: copy.start())

    out[...] = front[...]
    each(lambda copy: copy.wait())
    for p in range(RT):
        rows = slice(p * TILE, (p + 1) * TILE)
        for ch in range(2):
            m = ch * RT + p

            @pl.when(there[ch][p] & (js[ch] >= 0))
            def _():
                out[rows, :] += as_float(tiles[m]) * column_scale(codes[ch], m)


def base(ids, where, recv, front):
    line = pl.BlockSpec((RT * TILE, TILE), lambda i, *s: (0, i))
    return pl.pallas_call(
        base_kernel,
        grid_spec=pltpu.PrefetchScalarGridSpec(
            num_scalar_prefetch=2,
            grid=(QT,),
            in_specs=[pl.BlockSpec(memory_space=pl.ANY), line],
            out_specs=line,
            scratch_shapes=[
                pltpu.VMEM((2 * RT, TILE, TILE), I16),
                pltpu.VMEM((2, CODE, TILE), I16),
                pltpu.SemaphoreType.DMA((2 * RT + 2,)),
            ],
        ),
        out_shape=jax.ShapeDtypeStruct((RT * TILE, QT * TILE), F32),
        compiler_params=pltpu.CompilerParams(vmem_limit_bytes=24 * MIB),
        cost_estimate=pl.CostEstimate(flops=0, bytes_accessed=20 * MIB, transcendentals=0),
    )(ids, where, recv, front)


def final_kernel(
    ids, diag, inv, gx, goth, front, out,
    gbuf, rows_f, left, inverse,
):
    t = pl.program_id(0)
    c, g, core = ids[2], ids[3], ids[4]
    col = c * QT + t
    @pl.when(t == 0)
    def _():
        inverse[...] = right3(inv[...])
        for s in range(8):
            scale = column_scale(gx[s, 2 * RT * STRIP :, :], 0)
            v = as_float(gx[s, 0 : RT * STRIP, :]) * scale
            for p in range(RT):
                gbuf[p * TILE + s * STRIP : p * TILE + (s + 1) * STRIP, :] = v[
                    p * STRIP : (p + 1) * STRIP, :
                ]
        for p in range(RT):
            for a in range(2):

                @pl.when(g * RT + p == ids[8 + a])
                def _():
                    gbuf[p * TILE : (p + 1) * TILE, :] = diag[a * TILE : (a + 1) * TILE, :]

        v = dot3(left3(gbuf[...]), inverse[...])
        rows_f[...] = v
        left[...] = left3(v)

    side = pl.multiple_of((t % RT) * STRIP, STRIP)

    @pl.when(t // RT == core)
    def _():
        for s in range(8):
            gbuf[s * STRIP : (s + 1) * STRIP, :] = as_float(
                gx[s, pl.ds(RT * STRIP + side, STRIP), :]
            ) * column_scale(gx[s, 2 * RT * STRIP :, :], 1)

    @pl.when(t // RT != core)
    def _():
        for s in range(8):
            gbuf[s * STRIP : (s + 1) * STRIP, :] = as_float(
                goth[s, pl.ds(side, STRIP), :]
            ) * column_scale(goth[s, RT * STRIP :, :], 1)

    for a in range(2):

        @pl.when(col == ids[8 + a])
        def _():
            gbuf[0:TILE, :] = diag[a * TILE : (a + 1) * TILE, :]

    right = right3(dot3(left3(gbuf[0:TILE, :]), inverse[...]))
    out[...] = front[...] - dot3(left[...], right)
    for a in range(2):

        @pl.when(col == ids[8 + a])
        def _():
            out[...] = rows_f[:, a * TILE : (a + 1) * TILE]


def final(ids, diag, inv, gx, goth, front):
    def whole(*shape):
        return pl.BlockSpec(shape, lambda i, *s: (0,) * len(shape))

    line = pl.BlockSpec((RT * TILE, TILE), lambda i, *s: (0, i))
    return pl.pallas_call(
        final_kernel,
        grid_spec=pltpu.PrefetchScalarGridSpec(
            num_scalar_prefetch=1,
            grid=(QT,),
            in_specs=[
                whole(PANEL, PANEL),
                whole(PANEL, PANEL),
                whole(8, GROWS, PANEL),
                whole(8, GROWS - RT * STRIP, PANEL),
                line,
            ],
            out_specs=line,
            scratch_shapes=[
                pltpu.VMEM((RT * TILE, PANEL), F32),
                pltpu.VMEM((RT * TILE, PANEL), F32),
                pltpu.VMEM((RT * TILE, 3 * PANEL), BF16),
                pltpu.VMEM((PANEL, 3 * PANEL), BF16),
            ],
        ),
        out_shape=jax.ShapeDtypeStruct((RT * TILE, QT * TILE), F32),
        compiler_params=pltpu.CompilerParams(vmem_limit_bytes=52 * MIB),
        cost_estimate=pl.CostEstimate(flops=1 << 33, bytes_accessed=20 * MIB, transcendentals=0),
    )(ids, diag, inv, gx, goth, front)


def pick(v, at):
    return lax.dynamic_index_in_dim(v, at, 0, keepdims=False)


def fetch_partner(panel, x, core, z, yh):
    halves = panel.reshape(2, 512, 1024)
    piece = pick(halves, ((z - x + 4) % 4) // 2)
    came = []
    for dx in (1, 2, 3):
        pairs = [
            (flat(c, xs, y, (xs + 2 * b) % 4, y), flat(c, (xs + dx) % 4, b, xs, y))
            for c in range(2)
            for xs in range(4)
            for y in range(2)
            for b in range(2)
        ]
        came.append(lax.ppermute(piece, AXES, pairs))
    pairs = [
        (flat(c, x, y, x, y), flat(c, x, 1 - y, x, y))
        for c in range(2)
        for x in range(4)
        for y in range(2)
    ]
    beside = lax.ppermute(pick(halves, 1 - core), AXES, pairs)
    way = (x - z + 4) % 4
    mine = jnp.where(way == 1, came[0], jnp.where(way == 2, came[1], came[2]))
    mine = jnp.where(way == 0, jnp.where(core == yh, pick(halves, core), beside), mine)
    return mine, shift(mine, dk=1)


def sum_first(v, core, z):
    v = v.reshape(2, 256, PANEL)
    v = pick(v, core) + shift(pick(v, 1 - core), dk=1)
    v = v.reshape(4, 64, PANEL)
    got = [shift(pick(v, (z + d) % 4), dz=d) for d in (1, 3, 2)]
    return pick(v, z) + got[0] + got[1] + got[2]


def gathered(v, at, **axis):
    (name,) = axis
    full = jnp.zeros((4,) + v.shape, v.dtype)
    full = lax.dynamic_update_index_in_dim(full, v, at, 0)
    for d in (1, 3, 2):
        full = lax.dynamic_update_index_in_dim(full, shift(v, **{name: d}), (at - d) % 4, 0)
    return full


def sum_x(v, x):
    v = v.reshape(4, 64, PANEL)
    got = [shift(pick(v, (x + d) % 4), dx=d) for d in (1, 3, 2)]
    return pick(v, x) + got[0] + got[1] + got[2]


def sum_y(v):
    return (v + shift(v, dc=1, dy=1)) + (shift(v, dc=1) + shift(v, dy=1))


def join_cores(v, core):
    other = shift(v, dk=1)
    return jnp.concatenate([jnp.where(core == 0, v, other), jnp.where(core == 0, other, v)])


def tables(child_maps, parent_place):
    hit = child_maps[:, :, None] == jnp.arange(48, dtype=I32)
    slots = jnp.sum(jnp.where(hit, parent_place, 0), axis=2)
    hit = slots[:, :, None] == jnp.arange(48, dtype=I32)
    where = jnp.max(jnp.where(hit, jnp.arange(32, dtype=I32)[None, :, None], -1), axis=1)
    return slots, where


def body(child_blocks, child_panels, child_patterns, child_maps, parent_place, parent_front):
    ch, x, core, z, yh = (lax.axis_index(n).astype(I32) for n in AXES)
    r, c = x * 2 + core, z * 2 + yh
    slots, where = tables(child_maps, parent_place)
    e = parent_place[0], parent_place[1]
    ids = jnp.stack([ch, r, c, ch * 8 + r, core, z, yh, ch * 4 + x, e[0], e[1], x])
    panel = child_panels[0]
    parent_front = pltpu.with_memory_space_constraint(parent_front, pltpu.HBM)
    block = pltpu.with_memory_space_constraint(child_blocks[0], pltpu.HBM)
    mine, theirs = fetch_partner(panel, x, core, z, yh)
    mine, theirs, ids, slots, where = lax.optimization_barrier((mine, theirs, ids, slots, where))
    send, diag, gcol = update(
        ids, slots, child_patterns, block, panel, mine, theirs, parent_front
    )
    own = lax.all_to_all(send, ("child", "x"), split_axis=0, concat_axis=0, tiled=True)

    diag = sum_first(diag, core, z)
    diag, gcol = lax.optimization_barrier((diag, gcol))
    parts = strips(ids, gcol, parent_front)
    parts = [parts[0]] + [shift(parts[d], dz=d) for d in range(1, 4)]
    diag = gathered(diag, z, dz=0).reshape(256, PANEL)
    strip = choose_z(ids, where, parts)
    own, diag, strip = lax.optimization_barrier((own, diag, strip))

    other = shift(own, dk=1)
    send = route(ids, slots, where, own, other)
    kept, moved = pick(strip, yh), pick(strip, 1 - yh)
    moves = [shift(moved, dy=1), shift(kept, dc=1), shift(moved, dc=1, dy=1)]
    diag, *moves = lax.optimization_barrier((sum_x(diag, x), *moves))
    diag = sum_y(diag)
    send, diag, kept, *moves = lax.optimization_barrier((send, diag, kept, *moves))
    recv = lax.all_to_all(send, ("z", "yh"), split_axis=0, concat_axis=0, tiled=True)

    diag = gathered(diag, x, dx=0).reshape(256, PANEL)
    diag, kept, *moves = lax.optimization_barrier((diag, kept, *moves))
    strip = choose_y(ids, where, [kept] + moves)
    diag = join_cores(diag, core)
    inv = inverse_factor(diag)
    line = [strip] + [shift(strip, dx=d) for d in range(1, 4)]
    inv, *line = lax.optimization_barrier((inv, *line))
    line = jnp.stack(line)
    gsend = compose(ids, where, line, shift(line, dk=1))
    recv, inv, gsend = lax.optimization_barrier((recv, inv, gsend))
    gx = lax.all_to_all(gsend, ("z", "yh"), split_axis=0, concat_axis=0, tiled=True)
    with_children = base(ids, where, recv, parent_front)
    gx, with_children = lax.optimization_barrier((gx, with_children))
    goth = shift(gx[:, RT * STRIP :], dk=1)
    return final(ids, diag, inv, gx, goth, with_children)


def solution(mesh):
    fine = Mesh(mesh.devices.reshape(SIZES), AXES)
    rows, cols = ("x", "core"), ("z", "yh")
    return jax.shard_map(
        body,
        mesh=fine,
        in_specs=(
            P("child", rows, cols),
            P("child", rows, None),
            P(),
            P(),
            P(),
            P(("child", "x", "core"), cols),
        ),
        out_specs=P(("child", "x", "core"), cols),
        check_vma=False,
    )
```

```python
import jax
import jax.numpy as jnp
from jax import lax
from jax.experimental import pallas as pl
from jax.experimental.pallas import tpu as pltpu
from jax.sharding import Mesh
from jax.sharding import PartitionSpec as P

TILE = 256
PANEL = 512
CODE = 16
CT = 4
RT = 3
QT = 6
STRIP = 32
GROWS = 2 * RT * STRIP + CODE
CROWS = 2 * RT * TILE + CODE
AXES = ("child", "x", "core", "z", "yh")
SIZES = (2, 4, 2, 4, 2)
MIB = 1 << 20
F32 = jnp.float32
I32 = jnp.int32
I16 = jnp.int16
BF16 = jnp.bfloat16
HIGHEST = lax.Precision.HIGHEST


def flat(c, x, k, z, y):
    return (((c * 4 + x) * 2 + k) * 4 + z) * 2 + y


def everyone():
    return [
        (c, x, k, z, y)
        for c in range(2)
        for x in range(4)
        for k in range(2)
        for z in range(4)
        for y in range(2)
    ]


def shift(v, dc=0, dx=0, dk=0, dz=0, dy=0):
    pairs = [
        (flat(c, x, k, z, y), flat(c ^ dc, (x + dx) % 4, k ^ dk, (z + dz) % 4, y ^ dy))
        for c, x, k, z, y in everyone()
    ]
    return lax.ppermute(v, AXES, pairs)


def encode(u):
    top = jnp.max(jnp.abs(u), axis=0, keepdims=True)
    code = jnp.ceil(jnp.log2(jnp.maximum(top, 1e-30)) * 128.0)
    scale = jnp.exp2(15.0 - code * (1.0 / 128.0)) * (32766.0 / 32768.0)
    return jnp.floor(u * scale + 0.5).astype(I32).astype(I16), code


def scale_rows(code):
    return jnp.broadcast_to(code, (CODE, code.shape[1])).astype(I32).astype(I16)


def as_float(q):
    return q.astype(I32).astype(F32)


def column_scale(codes, row=0):
    code = as_float(codes)[row : row + 1, :]
    return jnp.exp2(code * (1.0 / 128.0) - 15.0) * (32768.0 / 32766.0)


def update_kernel(
    ids, slots, pat, blk, pan, mine, other, front, send, diag, gcol, tile, sem, lines, lsem
):
    n = pl.program_id(0)
    ch, r, c, g = ids[0], ids[1], ids[2], ids[3]
    e = (ids[8], ids[9])
    j = lax.rem(ids[4] * 2 + n, CT)
    turn = n % 2
    si = [slots[ch, r * CT + i] for i in range(CT)]
    sj = slots[ch, c * CT + j]

    def leave(turn, j, act):
        for i in range(CT):
            act(
                pltpu.make_async_copy(
                    lines.at[turn, i],
                    send.at[si[i] // QT, :, pl.ds(pl.multiple_of(j * TILE, TILE), TILE)],
                    lsem.at[turn, i],
                )
            )

    @pl.when(n == 0)
    def _():
        diag[...] = jnp.zeros_like(diag)
        for a in range(2):
            for b in range(2):

                @pl.when((e[a] // RT == g) & (e[b] // QT == c))
                def _():
                    rows = pl.multiple_of((e[a] % RT) * TILE, TILE)
                    cols = pl.multiple_of((e[b] % QT) * TILE, TILE)
                    copy = pltpu.make_async_copy(
                        front.at[pl.ds(rows, TILE), pl.ds(cols, TILE)], tile, sem
                    )
                    copy.start()
                    copy.wait()
                    diag[a * TILE : (a + 1) * TILE, b * TILE : (b + 1) * TILE] = tile[...]

    @pl.when(n >= 2)
    def _():
        leave(turn, lax.rem(ids[4] * 2 + n - 2, CT), lambda copy: copy.wait())

    par = jnp.where(n < 2, mine[...], other[...])
    prod = lax.dot_general(pan[...], par, (((1,), (1,)), ((), ())), preferred_element_type=F32)
    for i in range(CT):
        rows = slice(i * TILE, (i + 1) * TILE)
        u = (blk[rows, :] - prod[rows, :]) * pat[ch, r * CT + i, c * CT + j].astype(F32)
        q, code = encode(u)
        lines[turn, i, 0:TILE, :] = q
        lines[turn, i, TILE:, :] = scale_rows(code)
        for b in range(2):
            at = slice(b * TILE, (b + 1) * TILE)

            @pl.when(sj == e[b])
            def _():
                gcol[rows, at] = u
                for a in range(2):

                    @pl.when(si[i] == e[a])
                    def _():
                        diag[a * TILE : (a + 1) * TILE, at] += u

    leave(turn, j, lambda copy: copy.start())

    @pl.when(n == CT - 1)
    def _():
        leave(1 - turn, lax.rem(ids[4] * 2 + n - 1, CT), lambda copy: copy.wait())
        leave(turn, j, lambda copy: copy.wait())


def update(ids, slots, pat, blk, pan, mine, other, front):
    def column(n, ids, slots, pat):
        return 0, lax.rem(ids[4] * 2 + n, CT)

    return pl.pallas_call(
        update_kernel,
        grid_spec=pltpu.PrefetchScalarGridSpec(
            num_scalar_prefetch=3,
            grid=(CT,),
            in_specs=[
                pl.BlockSpec((1024, TILE), column),
                pl.BlockSpec((1024, 1024), lambda n, *s: (0, 0)),
                pl.BlockSpec((TILE, 1024), lambda n, *s: (jnp.minimum(n, 1), 0)),
                pl.BlockSpec((TILE, 1024), lambda n, *s: (jnp.maximum(n - 2, 0), 0)),
                pl.BlockSpec(memory_space=pl.ANY),
            ],
            out_specs=[
                pl.BlockSpec(memory_space=pl.ANY),
                pl.BlockSpec((PANEL, PANEL), lambda n, *s: (0, 0)),
                pl.BlockSpec((CT * TILE, PANEL), lambda n, *s: (0, 0)),
            ],
            scratch_shapes=[
                pltpu.VMEM((TILE, TILE), F32),
                pltpu.SemaphoreType.DMA,
                pltpu.VMEM((2, CT, TILE + CODE, TILE), I16),
                pltpu.SemaphoreType.DMA((2, CT)),
            ],
        ),
        out_shape=[
            pltpu.HBM((8, TILE + CODE, 1024), I16),
            pltpu.HBM((PANEL, PANEL), F32),
            pltpu.HBM((CT * TILE, PANEL), F32),
        ],
        compiler_params=pltpu.CompilerParams(vmem_limit_bytes=48 * MIB),
        cost_estimate=pl.CostEstimate(flops=1 << 31, bytes_accessed=14 * MIB, transcendentals=0),
    )(ids, slots, pat, blk, pan, mine, other, front)


def strips_kernel(ids, gcol, front, *rest):
    outs, (wide, sem) = rest[:4], rest[4:]
    c, z = ids[2], ids[5]
    for a in range(2):
        e = ids[8 + a]

        @pl.when(e // QT == c)
        def _():
            at = pl.multiple_of((e % QT) * TILE, TILE)
            copy = pltpu.make_async_copy(
                front.at[:, pl.ds(at, TILE)], wide.at[:, pl.ds(a * TILE, TILE)], sem
            )
            copy.start()
            copy.wait()

    for d in range(4):
        for f in range(2):
            s = ((z + d) % 4) * 2 + f
            at = 0
            for ref, n in ((gcol, CT), (wide, RT)):
                parts = [
                    ref[pl.ds(pl.multiple_of(p * TILE + s * STRIP, STRIP), STRIP), :]
                    for p in range(n)
                ]
                q, code = encode(jnp.concatenate(parts, 0))
                outs[d][f, at : at + n * STRIP, :] = q
                outs[d][f, at + n * STRIP : at + n * STRIP + CODE, :] = scale_rows(code)
                at += n * STRIP + CODE


def strips(ids, gcol, front):
    return pl.pallas_call(
        strips_kernel,
        grid_spec=pltpu.PrefetchScalarGridSpec(
            num_scalar_prefetch=1,
            grid=(1,),
            in_specs=[
                pl.BlockSpec((CT * TILE, PANEL), lambda i, *s: (0, 0)),
                pl.BlockSpec(memory_space=pl.ANY),
            ],
            out_specs=[pl.BlockSpec((2, TILE, PANEL), lambda i, *s: (0, 0, 0))] * 4,
            scratch_shapes=[pltpu.VMEM((RT * TILE, PANEL), F32), pltpu.SemaphoreType.DMA],
        ),
        out_shape=[jax.ShapeDtypeStruct((2, TILE, PANEL), I16)] * 4,
        compiler_params=pltpu.CompilerParams(vmem_limit_bytes=24 * MIB),
        cost_estimate=pl.CostEstimate(flops=0, bytes_accessed=6 * MIB, transcendentals=0),
    )(ids, gcol, front)


CHILD_CODE = CT * STRIP
FRONT = CHILD_CODE + CODE
FRONT_CODE = FRONT + RT * STRIP


def regions(ids, where, child):
    for a in range(2):
        cols = slice(a * TILE, (a + 1) * TILE)
        yield slice(0, FRONT), cols, where[child, ids[8 + a]] // CT
        yield slice(FRONT, TILE), cols, ids[8 + a] // QT


def choose_z_kernel(ids, where, *refs):
    out, sems = refs[4], refs[5]

    def each(act):
        for n, (rows, cols, holder) in enumerate(regions(ids, where, ids[0])):
            for d in range(4):

                @pl.when(lax.rem(ids[5] - holder // 2 + 4, 4) == d)
                def _():
                    act(
                        pltpu.make_async_copy(
                            refs[d].at[:, rows, cols], out.at[:, rows, cols], sems.at[n]
                        )
                    )

    each(lambda copy: copy.start())
    each(lambda copy: copy.wait())


def choose_z(ids, where, parts):
    return pl.pallas_call(
        choose_z_kernel,
        grid_spec=pltpu.PrefetchScalarGridSpec(
            num_scalar_prefetch=2,
            grid=(1,),
            in_specs=[pl.BlockSpec(memory_space=pl.ANY)] * 4,
            out_specs=pl.BlockSpec((2, TILE, PANEL), lambda i, *s: (0, 0, 0)),
            scratch_shapes=[pltpu.SemaphoreType.DMA((4,))],
        ),
        out_shape=jax.ShapeDtypeStruct((2, TILE, PANEL), I16),
        cost_estimate=pl.CostEstimate(flops=0, bytes_accessed=MIB, transcendentals=0),
    )(ids, where, *parts)


def choose_y_kernel(ids, where, kept, beside, across, both, out, sems):
    def each(act):
        for n, (near, far) in enumerate(((kept, beside), (across, both))):
            child = lax.rem(ids[0] + n, 2)
            for m, (rows, cols, holder) in enumerate(regions(ids, where, child)):
                here = lax.rem(holder + 8, 2) == ids[6]
                for side, ref in ((True, near), (False, far)):

                    @pl.when(here == side)
                    def _():
                        act(
                            pltpu.make_async_copy(
                                ref.at[rows, cols], out.at[n, rows, cols], sems.at[n * 4 + m]
                            )
                        )

    each(lambda copy: copy.start())
    each(lambda copy: copy.wait())


def choose_y(ids, where, parts):
    return pl.pallas_call(
        choose_y_kernel,
        grid_spec=pltpu.PrefetchScalarGridSpec(
            num_scalar_prefetch=2,
            grid=(1,),
            in_specs=[pl.BlockSpec(memory_space=pl.ANY)] * 4,
            out_specs=pl.BlockSpec((2, TILE, PANEL), lambda i, *s: (0, 0, 0)),
            scratch_shapes=[pltpu.SemaphoreType.DMA((8,))],
        ),
        out_shape=jax.ShapeDtypeStruct((2, TILE, PANEL), I16),
        cost_estimate=pl.CostEstimate(flops=0, bytes_accessed=MIB, transcendentals=0),
    )(ids, where, *parts)


def compose_kernel(ids, where, own, other, out, acc, kept, kcode):
    q = pl.program_id(0)
    ch, core, k, x = ids[0], ids[4], ids[7], ids[10]
    half = lax.broadcasted_iota(I32, (STRIP, PANEL), 1) < TILE

    def group(q):
        first = q * QT + core * RT
        d, f = lax.rem(x - q % 4 + 4, 4), lax.rem(ch + q // 4, 2)
        acc[...] = as_float(own[d, f, FRONT:FRONT_CODE, :]) * column_scale(
            own[d, f, FRONT_CODE:, :]
        )
        for m in range(2):
            known = [(where[m, ids[8 + a]] >= 0).astype(I32) for a in range(2)]
            mask = jnp.where(half, known[0], known[1]) > 0
            for p in range(RT):
                i = where[m, first + p]
                for here, ref in ((True, own), (False, other)):

                    @pl.when((i >= 0) & (((i // CT) % 2 == core) == here))
                    def _():
                        dm, fm = lax.rem(x - i // 8 + 4, 4), lax.rem(ch + m, 2)
                        row = pl.multiple_of((i % CT) * STRIP, STRIP)
                        v = as_float(ref[dm, fm, pl.ds(row, STRIP), :]) * column_scale(
                            ref[dm, fm, CHILD_CODE:FRONT, :]
                        )
                        acc[p * STRIP : (p + 1) * STRIP, :] += jnp.where(mask, v, 0.0)

        return encode(acc[...])

    @pl.when(q == 0)
    def _():
        v, code = group(k)
        kept[...] = v
        kcode[...] = jnp.broadcast_to(code, kcode.shape)

    v, code = group(q)
    out[0, 0 : RT * STRIP, :] = kept[...]
    out[0, RT * STRIP : 2 * RT * STRIP, :] = v
    row = lax.broadcasted_iota(I32, (CODE, PANEL), 0)
    both = jnp.where(row == 0, kcode[0:1, :], code)
    out[0, 2 * RT * STRIP :, :] = both.astype(I32).astype(I16)


def compose(ids, where, own, other):
    whole = pl.BlockSpec((4, 2, TILE, PANEL), lambda i, *s: (0, 0, 0, 0))
    return pl.pallas_call(
        compose_kernel,
        grid_spec=pltpu.PrefetchScalarGridSpec(
            num_scalar_prefetch=2,
            grid=(8,),
            in_specs=[whole] * 2,
            out_specs=pl.BlockSpec((1, GROWS, PANEL), lambda i, *s: (i, 0, 0)),
            scratch_shapes=[
                pltpu.VMEM((RT * STRIP, PANEL), F32),
                pltpu.VMEM((RT * STRIP, PANEL), I16),
                pltpu.VMEM((8, PANEL), F32),
            ],
        ),
        out_shape=jax.ShapeDtypeStruct((8, GROWS, PANEL), I16),
        compiler_params=pltpu.CompilerParams(vmem_limit_bytes=24 * MIB),
        cost_estimate=pl.CostEstimate(flops=0, bytes_accessed=6 * MIB, transcendentals=0),
    )(ids, where, own, other)


def route_kernel(ids, slots, where, own, other, send, lines, codes, isem, osem, csem):
    c, g, core = ids[2], ids[3], ids[4]
    rows = [where[ch, g * RT + p] for ch in range(2) for p in range(RT)]
    to = [[slots[ch, c * CT + j] // QT for j in range(CT)] for ch in range(2)]

    def come(m, act):
        i = rows[m]
        src = (m // RT) * 4 + i // 8
        for here, buf in ((True, own), (False, other)):

            @pl.when((i >= 0) & (((i // CT) % 2 == core) == here))
            def _():
                act(pltpu.make_async_copy(buf.at[src], lines.at[m], isem.at[m]))

    def leave(m, act):
        @pl.when(rows[m] >= 0)
        def _():
            for j in range(CT):
                act(
                    pltpu.make_async_copy(
                        lines.at[m, pl.ds(0, TILE), pl.ds(j * TILE, TILE)],
                        send.at[to[m // RT][j], pl.ds(m * TILE, TILE), :],
                        osem.at[m * CT + j],
                    )
                )

    for m in range(2 * RT):
        come(m, lambda copy: copy.start())
    for m in range(2 * RT):
        come(m, lambda copy: copy.wait())
        leave(m, lambda copy: copy.start())
    line = lax.broadcasted_iota(I32, (CODE, TILE), 0)
    codes[...] = jnp.zeros_like(codes)
    for ch in range(2):
        for j in range(CT):
            q = to[ch][j]
            v = codes[q].astype(I32)
            for p in range(RT):
                m = ch * RT + p
                mine = lines[m, TILE:, j * TILE : (j + 1) * TILE].astype(I32)
                v = jnp.where(line == m, mine, v)
            codes[q] = v.astype(I16)
    tails = [
        pltpu.make_async_copy(codes.at[q], send.at[q, pl.ds(2 * RT * TILE, CODE), :], csem.at[q])
        for q in range(8)
    ]
    for copy in tails:
        copy.start()
    for m in range(2 * RT):
        leave(m, lambda copy: copy.wait())
    for copy in tails:
        copy.wait()


def route(ids, slots, where, own, other):
    return pl.pallas_call(
        route_kernel,
        grid_spec=pltpu.PrefetchScalarGridSpec(
            num_scalar_prefetch=3,
            grid=(1,),
            in_specs=[pl.BlockSpec(memory_space=pl.ANY)] * 2,
            out_specs=pl.BlockSpec(memory_space=pl.ANY),
            scratch_shapes=[
                pltpu.VMEM((2 * RT, TILE + CODE, 1024), I16),
                pltpu.VMEM((8, CODE, TILE), I16),
                pltpu.SemaphoreType.DMA((2 * RT,)),
                pltpu.SemaphoreType.DMA((2 * RT * CT,)),
                pltpu.SemaphoreType.DMA((8,)),
            ],
        ),
        out_shape=pltpu.HBM((8, CROWS, TILE), I16),
        compiler_params=pltpu.CompilerParams(vmem_limit_bytes=32 * MIB),
        cost_estimate=pl.CostEstimate(flops=0, bytes_accessed=8 * MIB, transcendentals=0),
    )(ids, slots, where, own, other)


def nt(a, b):
    return lax.dot_general(
        a, b, (((1,), (1,)), ((), ())), precision=HIGHEST, preferred_element_type=F32
    )


def nn(a, b):
    return lax.dot_general(
        a, b, (((1,), (0,)), ((), ())), precision=HIGHEST, preferred_element_type=F32
    )


NB = 64
WAYS = 8


def inverse_kernel(a_ref, out, w, f):
    n = PANEL // NB
    out[...] = jnp.zeros_like(out)
    row = lax.broadcasted_iota(I32, (NB, NB), 0)
    col = lax.broadcasted_iota(I32, (NB, NB), 1)
    eye = row == col
    lanes = lax.broadcasted_iota(I32, (1, 2 * NB), 1)
    sub = lax.broadcasted_iota(I32, (NB, 1), 0)

    def blk(i):
        return slice(i * NB, (i + 1) * NB)

    f[...] = a_ref[...]
    for k in range(n):
        w[:, :NB] = f[blk(k), blk(k)]
        w[:, NB:] = jnp.where(eye, 1.0, 0.0).astype(F32)

        def step(n4, _):
            j = n4 * WAYS
            lines = [w[pl.ds(j + a, 1), :] for a in range(WAYS)]
            square = w[:, :NB]
            columns = [
                jnp.sum(jnp.where(col == j + a, square, 0.0), axis=1, keepdims=True)
                for a in range(WAYS)
            ]
            small = [
                [
                    jnp.sum(jnp.where(lanes == j + b, lines[a], 0.0), axis=1, keepdims=True)
                    if b >= a
                    else None
                    for b in range(WAYS)
                ]
                for a in range(WAYS)
            ]
            factors = []
            for a in range(WAYS):
                inverse = 1.0 / small[a][a]
                for b in range(a + 1, WAYS):
                    times = small[a][b] * inverse
                    for d in range(b, WAYS):
                        small[b][d] = small[b][d] - times * small[a][d]
                    lines[b] = lines[b] - times * lines[a]
                    columns[b] = columns[b] - times * columns[a]
                factors.append(jnp.where(sub >= j + WAYS, columns[a] * inverse, 0.0))
            total = w[...]
            for a in range(WAYS):
                total = total - factors[a] * lines[a]
            w[...] = total
            for a in range(1, WAYS):
                w[pl.ds(j + a, 1), :] = lines[a]
            return 0

        lax.fori_loop(0, NB // WAYS, step, 0)
        d = jnp.sum(jnp.where(eye, w[:, :NB], 0.0), axis=1, keepdims=True)
        inv = w[:, NB:] * (1.0 / jnp.sqrt(d))
        out[blk(k), blk(k)] = inv
        rest = (k + 1) * NB
        if rest < PANEL:
            below = nt(f[rest:, blk(k)], inv)
            f[rest:, blk(k)] = below
            f[rest:, rest:] = f[rest:, rest:] - nt(below, below)
    for k in range(1, n):
        acc = nn(f[blk(k), : k * NB], out[: k * NB, : k * NB])
        out[blk(k), : k * NB] = -nn(out[blk(k), blk(k)], acc)


def inverse_factor(a):
    return pl.pallas_call(
        inverse_kernel,
        out_shape=jax.ShapeDtypeStruct((PANEL, PANEL), F32),
        scratch_shapes=[pltpu.VMEM((NB, 2 * NB), F32), pltpu.VMEM((PANEL, PANEL), F32)],
        compiler_params=pltpu.CompilerParams(vmem_limit_bytes=24 * MIB),
        cost_estimate=pl.CostEstimate(flops=1 << 34, bytes_accessed=2 * MIB, transcendentals=0),
    )(a)


def split(v):
    hi = v.astype(BF16)
    return hi, (v - hi.astype(F32)).astype(BF16)


def left3(v):
    hi, lo = split(v)
    return jnp.concatenate([hi, hi, lo], 1)


def right3(v):
    hi, lo = split(v)
    return jnp.concatenate([hi, lo, hi], 1)


def dot3(a, b):
    return lax.dot_general(a, b, (((1,), (1,)), ((), ())), preferred_element_type=F32)


def base_kernel(ids, where, recv, front, out, tiles, codes, tsem):
    t = pl.program_id(0)
    c, g = ids[2], ids[3]
    col = c * QT + t
    js = [where[ch, col] for ch in range(2)]
    there = [[where[ch, g * RT + p] >= 0 for p in range(RT)] for ch in range(2)]

    def each(act):
        for ch in range(2):
            src = js[ch] // CT

            @pl.when(js[ch] >= 0)
            def _():
                act(
                    pltpu.make_async_copy(
                        recv.at[src, pl.ds(2 * RT * TILE, CODE), :],
                        codes.at[ch],
                        tsem.at[2 * RT + ch],
                    )
                )

            for p in range(RT):
                m = ch * RT + p

                @pl.when(there[ch][p] & (js[ch] >= 0))
                def _():
                    act(
                        pltpu.make_async_copy(
                            recv.at[src, pl.ds(m * TILE, TILE), :], tiles.at[m], tsem.at[m]
                        )
                    )

    each(lambda copy: copy.start())

    out[...] = front[...]
    each(lambda copy: copy.wait())
    for p in range(RT):
        rows = slice(p * TILE, (p + 1) * TILE)
        for ch in range(2):
            m = ch * RT + p

            @pl.when(there[ch][p] & (js[ch] >= 0))
            def _():
                out[rows, :] += as_float(tiles[m]) * column_scale(codes[ch], m)


def base(ids, where, recv, front):
    line = pl.BlockSpec((RT * TILE, TILE), lambda i, *s: (0, i))
    return pl.pallas_call(
        base_kernel,
        grid_spec=pltpu.PrefetchScalarGridSpec(
            num_scalar_prefetch=2,
            grid=(QT,),
            in_specs=[pl.BlockSpec(memory_space=pl.ANY), line],
            out_specs=line,
            scratch_shapes=[
                pltpu.VMEM((2 * RT, TILE, TILE), I16),
                pltpu.VMEM((2, CODE, TILE), I16),
                pltpu.SemaphoreType.DMA((2 * RT + 2,)),
            ],
        ),
        out_shape=jax.ShapeDtypeStruct((RT * TILE, QT * TILE), F32),
        compiler_params=pltpu.CompilerParams(vmem_limit_bytes=24 * MIB),
        cost_estimate=pl.CostEstimate(flops=0, bytes_accessed=20 * MIB, transcendentals=0),
    )(ids, where, recv, front)


def final_kernel(
    ids, diag, inv, gx, goth, front, out,
    gbuf, rows_f, left, inverse,
):
    t = pl.program_id(0)
    c, g, core = ids[2], ids[3], ids[4]
    col = c * QT + t
    @pl.when(t == 0)
    def _():
        inverse[...] = right3(inv[...])
        for s in range(8):
            scale = column_scale(gx[s, 2 * RT * STRIP :, :], 0)
            v = as_float(gx[s, 0 : RT * STRIP, :]) * scale
            for p in range(RT):
                gbuf[p * TILE + s * STRIP : p * TILE + (s + 1) * STRIP, :] = v[
                    p * STRIP : (p + 1) * STRIP, :
                ]
        for p in range(RT):
            for a in range(2):

                @pl.when(g * RT + p == ids[8 + a])
                def _():
                    gbuf[p * TILE : (p + 1) * TILE, :] = diag[a * TILE : (a + 1) * TILE, :]

        v = dot3(left3(gbuf[...]), inverse[...])
        rows_f[...] = v
        left[...] = left3(v)

    side = pl.multiple_of((t % RT) * STRIP, STRIP)

    @pl.when(t // RT == core)
    def _():
        for s in range(8):
            gbuf[s * STRIP : (s + 1) * STRIP, :] = as_float(
                gx[s, pl.ds(RT * STRIP + side, STRIP), :]
            ) * column_scale(gx[s, 2 * RT * STRIP :, :], 1)

    @pl.when(t // RT != core)
    def _():
        for s in range(8):
            gbuf[s * STRIP : (s + 1) * STRIP, :] = as_float(
                goth[s, pl.ds(side, STRIP), :]
            ) * column_scale(goth[s, RT * STRIP :, :], 1)

    for a in range(2):

        @pl.when(col == ids[8 + a])
        def _():
            gbuf[0:TILE, :] = diag[a * TILE : (a + 1) * TILE, :]

    right = right3(dot3(left3(gbuf[0:TILE, :]), inverse[...]))
    out[...] = front[...] - dot3(left[...], right)
    for a in range(2):

        @pl.when(col == ids[8 + a])
        def _():
            out[...] = rows_f[:, a * TILE : (a + 1) * TILE]


def final(ids, diag, inv, gx, goth, front):
    def whole(*shape):
        return pl.BlockSpec(shape, lambda i, *s: (0,) * len(shape))

    line = pl.BlockSpec((RT * TILE, TILE), lambda i, *s: (0, i))
    return pl.pallas_call(
        final_kernel,
        grid_spec=pltpu.PrefetchScalarGridSpec(
            num_scalar_prefetch=1,
            grid=(QT,),
            in_specs=[
                whole(PANEL, PANEL),
                whole(PANEL, PANEL),
                whole(8, GROWS, PANEL),
                whole(8, GROWS - RT * STRIP, PANEL),
                line,
            ],
            out_specs=line,
            scratch_shapes=[
                pltpu.VMEM((RT * TILE, PANEL), F32),
                pltpu.VMEM((RT * TILE, PANEL), F32),
                pltpu.VMEM((RT * TILE, 3 * PANEL), BF16),
                pltpu.VMEM((PANEL, 3 * PANEL), BF16),
            ],
        ),
        out_shape=jax.ShapeDtypeStruct((RT * TILE, QT * TILE), F32),
        compiler_params=pltpu.CompilerParams(vmem_limit_bytes=52 * MIB),
        cost_estimate=pl.CostEstimate(flops=1 << 33, bytes_accessed=20 * MIB, transcendentals=0),
    )(ids, diag, inv, gx, goth, front)


def pick(v, at):
    return lax.dynamic_index_in_dim(v, at, 0, keepdims=False)


def fetch_partner(panel, x, core, z, yh):
    halves = panel.reshape(2, 512, 1024)
    piece = pick(halves, ((z - x + 4) % 4) // 2)
    came = []
    for dx in (1, 2, 3):
        pairs = [
            (flat(c, xs, y, (xs + 2 * b) % 4, y), flat(c, (xs + dx) % 4, b, xs, y))
            for c in range(2)
            for xs in range(4)
            for y in range(2)
            for b in range(2)
        ]
        came.append(lax.ppermute(piece, AXES, pairs))
    pairs = [
        (flat(c, x, y, x, y), flat(c, x, 1 - y, x, y))
        for c in range(2)
        for x in range(4)
        for y in range(2)
    ]
    beside = lax.ppermute(pick(halves, 1 - core), AXES, pairs)
    way = (x - z + 4) % 4
    mine = jnp.where(way == 1, came[0], jnp.where(way == 2, came[1], came[2]))
    mine = jnp.where(way == 0, jnp.where(core == yh, pick(halves, core), beside), mine)
    return mine, shift(mine, dk=1)


def sum_first(v, core, z):
    v = v.reshape(2, 256, PANEL)
    v = pick(v, core) + shift(pick(v, 1 - core), dk=1)
    v = v.reshape(4, 64, PANEL)
    got = [shift(pick(v, (z + d) % 4), dz=d) for d in (1, 3, 2)]
    return pick(v, z) + got[0] + got[1] + got[2]


def gathered(v, at, **axis):
    (name,) = axis
    full = jnp.zeros((4,) + v.shape, v.dtype)
    full = lax.dynamic_update_index_in_dim(full, v, at, 0)
    for d in (1, 3, 2):
        full = lax.dynamic_update_index_in_dim(full, shift(v, **{name: d}), (at - d) % 4, 0)
    return full


def sum_x(v, x):
    v = v.reshape(4, 64, PANEL)
    got = [shift(pick(v, (x + d) % 4), dx=d) for d in (1, 3, 2)]
    return pick(v, x) + got[0] + got[1] + got[2]


def sum_y(v):
    return (v + shift(v, dc=1, dy=1)) + (shift(v, dc=1) + shift(v, dy=1))


def sum_third(v, x, core):
    v = gathered(v, x, dx=0).reshape(256, PANEL)
    other = shift(v, dk=1)
    return jnp.concatenate([jnp.where(core == 0, v, other), jnp.where(core == 0, other, v)])


def tables(child_maps, parent_place):
    hit = child_maps[:, :, None] == jnp.arange(48, dtype=I32)
    slots = jnp.sum(jnp.where(hit, parent_place, 0), axis=2)
    hit = slots[:, :, None] == jnp.arange(48, dtype=I32)
    where = jnp.max(jnp.where(hit, jnp.arange(32, dtype=I32)[None, :, None], -1), axis=1)
    return slots, where


def body(child_blocks, child_panels, child_patterns, child_maps, parent_place, parent_front):
    ch, x, core, z, yh = (lax.axis_index(n).astype(I32) for n in AXES)
    r, c = x * 2 + core, z * 2 + yh
    slots, where = tables(child_maps, parent_place)
    e = parent_place[0], parent_place[1]
    ids = jnp.stack([ch, r, c, ch * 8 + r, core, z, yh, ch * 4 + x, e[0], e[1], x])
    panel = child_panels[0]
    parent_front = pltpu.with_memory_space_constraint(parent_front, pltpu.HBM)
    block = pltpu.with_memory_space_constraint(child_blocks[0], pltpu.HBM)
    mine, theirs = fetch_partner(panel, x, core, z, yh)
    mine, theirs, ids, slots, where = lax.optimization_barrier((mine, theirs, ids, slots, where))
    send, diag, gcol = update(
        ids, slots, child_patterns, block, panel, mine, theirs, parent_front
    )
    own = lax.all_to_all(send, ("child", "x"), split_axis=0, concat_axis=0, tiled=True)

    diag = sum_first(diag, core, z)
    diag, gcol = lax.optimization_barrier((diag, gcol))
    parts = strips(ids, gcol, parent_front)
    parts = [parts[0]] + [shift(parts[d], dz=d) for d in range(1, 4)]
    diag = gathered(diag, z, dz=0).reshape(256, PANEL)
    strip = choose_z(ids, where, parts)
    own, diag, strip = lax.optimization_barrier((own, diag, strip))

    other = shift(own, dk=1)
    send = route(ids, slots, where, own, other)
    kept, moved = pick(strip, yh), pick(strip, 1 - yh)
    moves = [shift(moved, dy=1), shift(kept, dc=1), shift(moved, dc=1, dy=1)]
    diag, *moves = lax.optimization_barrier((sum_x(diag, x), *moves))
    strip = choose_y(ids, where, [kept] + moves)
    diag = sum_y(diag)
    send, diag, strip = lax.optimization_barrier((send, diag, strip))
    recv = lax.all_to_all(send, ("z", "yh"), split_axis=0, concat_axis=0, tiled=True)

    diag = sum_third(diag, x, core)
    line = jnp.stack([strip] + [shift(strip, dx=d) for d in range(1, 4)])
    inv = inverse_factor(diag)
    gsend = compose(ids, where, line, shift(line, dk=1))
    recv, inv, gsend = lax.optimization_barrier((recv, inv, gsend))
    gx = lax.all_to_all(gsend, ("z", "yh"), split_axis=0, concat_axis=0, tiled=True)
    with_children = base(ids, where, recv, parent_front)
    gx, with_children = lax.optimization_barrier((gx, with_children))
    goth = shift(gx[:, RT * STRIP :], dk=1)
    return final(ids, diag, inv, gx, goth, with_children)


def solution(mesh):
    fine = Mesh(mesh.devices.reshape(SIZES), AXES)
    rows, cols = ("x", "core"), ("z", "yh")
    return jax.shard_map(
        body,
        mesh=fine,
        in_specs=(
            P("child", rows, cols),
            P("child", rows, None),
            P(),
            P(),
            P(),
            P(("child", "x", "core"), cols),
        ),
        out_specs=P(("child", "x", "core"), cols),
        check_vma=False,
    )
```
